32 devices in a mesh: frame: 8 (over z, x), batch: 4 (over y, core).
Axes of the slice: x: 2, y: 2, z: 4, core: 2. Of those that a mesh axis runs over, the one named last changes fastest.
Arguments:
- tokens: bfloat16 [4, 3136, 768], P('batch', 'frame'), may hold values from -6 to 6
- cotangent: bfloat16 [4, 128, 768], P('batch', 'frame'), may hold values from -6 to 6
- clip_lengths: int32 [4, 8], P('batch'), may hold values from 1 to 8, 16 in all within a row
- clip_order: int32 [4, 8], P('batch'), may hold values from 0 to 7, each once within a row
- block_owner: int32 [448], replicated, may hold values from 0 to 447, as said below
- master: float32 [448, 128, 128], P(('frame', 'batch'))
- moment1: float32 [448, 128, 128], P(('frame', 'batch'))
- moment2: float32 [448, 128, 128], P(('frame', 'batch')), as said below
- stat_left: float32 [448, 128, 128], P(('frame', 'batch')), as said below
- stat_right: float32 [448, 128, 128], P(('frame', 'batch')), as said below
- basis_left: float32 [448, 128, 128], P(('frame', 'batch')), as said below
- basis_right: float32 [448, 128, 128], P(('frame', 'batch')), as said below
- small_params: float32 [67808], replicated
- small_moment1: float32 [67808], replicated
- small_moment2: float32 [67808], replicated, as said below
Outputs:
- learned: float32 [4, 128, 768], P('batch', 'frame')
- grad_input: float32 [4, 3136, 768], P('batch', 'frame')
- new_master: float32 [448, 128, 128], P(('frame', 'batch'))
- new_moment1: float32 [448, 128, 128], P(('frame', 'batch'))
- new_moment2: float32 [448, 128, 128], P(('frame', 'batch'))
- new_left: float32 [448, 128, 128], P(('frame', 'batch'))
- new_right: float32 [448, 128, 128], P(('frame', 'batch'))
- new_basis_left: float32 [448, 128, 128], P(('frame', 'batch'))
- new_basis_right: float32 [448, 128, 128], P(('frame', 'batch'))
- small_first: float32 [67808], replicated
- small_second: float32 [67808], replicated
- small_new: float32 [67808], replicated
- grad_norm: float32 [], replicated
The draws below stay inside these ranges and needn't reach their ends.
Inputs may be any that keep to these rules, and one draw needn't show every extreme that they name: `clip_lengths`: in each group the lengths sum to 16; the longest is exactly 8. `clip_order`: each row is a permutation of the clip numbers. `block_owner`: a permutation of the slot numbers; values of 432 or more mark empty slots. `basis_left`: each block is orthogonal. `basis_right`: each block is orthogonal. `stat_left`: each block is symmetric positive definite. `stat_right`: each block is symmetric positive definite. `moment2`: positive. `small_moment2`: positive.
All inputs are finite; a program needn't handle non-finite values.
Results may differ from the reference program's by a relative error of at most 0.012.
Values may be sent and summed in bfloat16 or wider, within the bound.
No kernel may reach another device: no remote copies, remote signals or barrier semaphores. Data moves between devices by JAX's collectives and lax.ppermute only.
A program may use at most 256 MiB of HBM per device.

```python
import math
import jax
import jax.numpy as jnp
import numpy as np
from jax import lax

D = 768
HEADS = 12
HD = 64
FF = 3072
GRID = 14
NT = 8
BLOCK_SIDE = 128
STEP = 10
FR_DEV = 2
TOK_DEV = 392
GF = 16
LONGEST = 8
TOK_GROUP = 3136
NCLIP = 8
GROUPS = 4
MATRIX_BLOCKS = 432
SLOT_COUNT = 448
P_SMALL = 67808
N_FRAME = 8


def layout_drawn():
    return [('gain_one', (D,)), ('shift_one', (D,)), ('gain_two', (D,)), ('shift_two', (D,)), ('gain_three', (D,)), ('shift_three', (D,)), ('bias_query', (D,)), ('bias_value', (D,)), ('bias_out', (D,)), ('bias_up', (FF,)), ('bias_down', (D,)), ('conv_first', (D, 9, NT)), ('conv_second', (9, NT, NT)), ('conv_third', (9, NT, NT)), ('conv_fourth', (9, NT, NT)), ('conv_bias', (4, NT))]


def element_size():
    return 1.0 / math.sqrt(MATRIX_BLOCKS * BLOCK_SIDE * BLOCK_SIDE + P_SMALL)


def owner_table(key):
    return jax.random.permutation(jax.random.fold_in(key, 101), SLOT_COUNT).astype(jnp.int32)


def logarithm_uniform(key, shape_out, lower, upper):
    return jnp.exp(jax.random.uniform(key, shape_out, jnp.float32, math.log(lower), math.log(upper)))


def statistics(key):
    diagonal_key, wide_matrix_key = jax.random.split(key)
    starting_size = BLOCK_SIDE * element_size() ** 2
    diagonal_entries = logarithm_uniform(diagonal_key, (SLOT_COUNT, BLOCK_SIDE), starting_size, 4.0 * starting_size)
    factor_list = jax.random.truncated_normal(wide_matrix_key, -4.0, 4.0, (SLOT_COUNT, BLOCK_SIDE, BLOCK_SIDE), jnp.float32)
    gram_part = jnp.einsum('sij,skj->sik', factor_list, factor_list, precision=jax.lax.Precision.HIGHEST) * (starting_size / BLOCK_SIDE)
    return gram_part + diagonal_entries[:, :, None] * jnp.eye(BLOCK_SIDE, dtype=jnp.float32)


def orthogonal(key):
    rotation_key, sign_flip_key = jax.random.split(key)
    rotation_angles = jax.random.uniform(rotation_key, (SLOT_COUNT, BLOCK_SIDE // 2, 1), jnp.float32, -math.pi, math.pi)
    sign_flips = jnp.where(jax.random.bernoulli(sign_flip_key, 0.5, (SLOT_COUNT, BLOCK_SIDE)), 1.0, -1.0)
    house = jnp.eye(BLOCK_SIDE, dtype=jnp.float32)[None] - 2.0 / BLOCK_SIDE * sign_flips[:, :, None] * sign_flips[:, None, :]
    even_rows = house[:, 0::2, :]
    odd_rows = house[:, 1::2, :]
    upper_rows = jnp.cos(rotation_angles) * even_rows - jnp.sin(rotation_angles) * odd_rows
    lower_rows = jnp.sin(rotation_angles) * even_rows + jnp.cos(rotation_angles) * odd_rows
    return jnp.stack([upper_rows, lower_rows], axis=2).reshape(SLOT_COUNT, BLOCK_SIDE, BLOCK_SIDE)


def draw_block_owner(key, part):
    return owner_table(key)


def draw_master(key, part):
    owner_ids = owner_table(key)
    key = jax.random.fold_in(key, 2)
    tile_side = D // BLOCK_SIDE
    count_qkv = tile_side * 3 * tile_side
    count_out = tile_side * tile_side
    count_up = tile_side * (FF // BLOCK_SIDE)
    block_scale = jnp.where(owner_ids < count_qkv, D ** (-0.5), jnp.where(owner_ids < count_qkv + count_out, 8.0 / math.sqrt(D), jnp.where(owner_ids < count_qkv + count_out + count_up, D ** (-0.5), FF ** (-0.5))))
    gaussian_draw = jax.random.truncated_normal(key, -4.0, 4.0, (SLOT_COUNT, BLOCK_SIDE, BLOCK_SIDE), jnp.float32)
    return gaussian_draw * block_scale[:, None, None]


def draw_moment1(key, part):
    key = jax.random.fold_in(key, 3)
    return 0.11 * element_size() * jax.random.truncated_normal(key, -4.0, 4.0, (SLOT_COUNT, BLOCK_SIDE, BLOCK_SIDE), jnp.float32)


def draw_moment2(key, part):
    key = jax.random.fold_in(key, 4)
    square_matrix = 0.0526 * element_size() ** 2
    return logarithm_uniform(key, (SLOT_COUNT, BLOCK_SIDE, BLOCK_SIDE), square_matrix, 4.0 * square_matrix)


def draw_stat_left(key, part):
    key = jax.random.fold_in(key, 5)
    return statistics(key)


def draw_stat_right(key, part):
    key = jax.random.fold_in(key, 6)
    return statistics(key)


def draw_basis_left(key, part):
    key = jax.random.fold_in(key, 7)
    return orthogonal(key)


def draw_basis_right(key, part):
    key = jax.random.fold_in(key, 8)
    return orthogonal(key)


def draw_small_params(key, part):
    key = jax.random.fold_in(key, 9)
    gain_names = ('gain_one', 'gain_two', 'gain_three')
    kernel_names = ('conv_second', 'conv_third', 'conv_fourth')
    pieces = []
    for position, (part_name, part_shape) in enumerate(layout_drawn()):
        sub_key = jax.random.fold_in(key, position)
        entries = math.prod(part_shape)
        gaussian_draw = jax.random.normal(sub_key, (entries,), jnp.float32)
        if part_name in gain_names:
            segment_values = jax.random.uniform(sub_key, (entries,), jnp.float32, 0.6, 1.4)
        elif part_name == 'conv_first':
            segment_values = 1.5 / math.sqrt(9 * D) * gaussian_draw
        elif part_name == 'conv_bias':
            segment_values = 0.3 * gaussian_draw
        elif part_name in kernel_names:
            segment_values = 1.5 / math.sqrt(9 * NT) * gaussian_draw
        else:
            segment_values = 0.3 * gaussian_draw
        pieces.append(segment_values)
    return jnp.concatenate(pieces)


def draw_small_moment1(key, part):
    key = jax.random.fold_in(key, 10)
    return 0.44 * element_size() * jax.random.truncated_normal(key, -4.0, 4.0, (P_SMALL,), jnp.float32)


def draw_small_moment2(key, part):
    key = jax.random.fold_in(key, 11)
    square_matrix = 0.0526 * (4.0 * element_size()) ** 2
    return logarithm_uniform(key, (P_SMALL,), square_matrix, 4.0 * square_matrix)


def levels(rng, dims, cuts, low, high):
    level = 1.0
    for axis_at, shards_of in cuts:
        heights = jax.random.uniform(jax.random.fold_in(jax.random.fold_in(rng, 6), axis_at), (shards_of,), jnp.float32, low / len(cuts), high / len(cuts))
        level = level * jnp.repeat(jnp.exp(heights), dims[axis_at] // shards_of).reshape((-1,) + (1,) * (len(dims) - 1 - axis_at))
    return level


def split_up(amount, total, most, slope):
    weights = [(1 << 20) // math.isqrt(grade ** slope) + 1 for grade in range(2, amount + 1)]
    spare, given = total - most - (amount - 1), [1] * (amount - 1)
    while spare > 0:
        movable = [i for i in range(amount - 1) if given[i] < most]
        pool, budget = sum([weights[i] for i in movable]), spare
        for i in movable:
            more = min(most - given[i], max(1, budget * weights[i] // pool), spare)
            given[i] = given[i] + more
            spare = spare - more
    return np.array([most] + given)


def ragged(key, amount, total, reach, lean):
    if amount == 2:
        one = jax.random.randint(key, (), max(1, total - reach), min(reach, total - 1) + 1)
        return jnp.stack([one, total - one])
    sizes = jnp.asarray(split_up(amount, total, reach, lean), jnp.int32)
    twos = (amount - 1) // 2
    giver, receiver = sizes[1:1 + 2 * twos:2], sizes[2:2 + 2 * twos:2]
    room = jnp.minimum(giver - 1, reach - receiver)
    moved = jax.random.randint(jax.random.fold_in(key, 1), (twos,), 0, 1 << 20) % (room + 1)
    sizes = sizes.at[1:1 + 2 * twos:2].set(giver - moved).at[2:2 + 2 * twos:2].set(receiver + moved)
    return sizes[jax.random.permutation(jax.random.fold_in(key, 2), amount)]


def normal_values(own_key, dims, width, limit, shards=(), held_as=jnp.bfloat16):
    loudness = levels(own_key, dims, shards, -0.22, 0.18) if shards else 1.0
    array = jax.random.normal(own_key, dims, jnp.float32) * width * loudness
    return jnp.minimum(jnp.maximum(array, -limit), limit).astype(held_as)


def setup_inputs(seed: int = 0) -> dict:
    streams_of = jax.random.split(jax.random.key(seed), 16)
    return {
        "tokens": normal_values(streams_of[0], (GROUPS, TOK_GROUP, D), 1.0, 6.0, ((0, 4), (1, 8))),
        "cotangent": normal_values(streams_of[1], (GROUPS, GF * NT, D), 1.0, 6.0, ((0, 4), (1, 8))),
        "clip_lengths": jax.vmap(lambda own: ragged(own, NCLIP, GF, LONGEST, 2))(jax.random.split(streams_of[2], GROUPS)).reshape((GROUPS, NCLIP)).astype(jnp.int32),
        "clip_order": jax.vmap(lambda own: jax.random.permutation(own, NCLIP))(jax.random.split(streams_of[3], GROUPS)).reshape((GROUPS, NCLIP)).astype(jnp.int32),
        "block_owner": draw_block_owner(jax.random.fold_in(streams_of[15], 71), 0),
        "master": draw_master(jax.random.fold_in(streams_of[15], 71), 0),
        "moment1": draw_moment1(jax.random.fold_in(streams_of[15], 71), 0),
        "moment2": draw_moment2(jax.random.fold_in(streams_of[15], 71), 0),
        "stat_left": draw_stat_left(jax.random.fold_in(streams_of[15], 71), 0),
        "stat_right": draw_stat_right(jax.random.fold_in(streams_of[15], 71), 0),
        "basis_left": draw_basis_left(jax.random.fold_in(streams_of[15], 71), 0),
        "basis_right": draw_basis_right(jax.random.fold_in(streams_of[15], 71), 0),
        "small_params": draw_small_params(jax.random.fold_in(streams_of[15], 71), 0),
        "small_moment1": draw_small_moment1(jax.random.fold_in(streams_of[15], 71), 0),
        "small_moment2": draw_small_moment2(jax.random.fold_in(streams_of[15], 71), 0),
    }


FULL_PRECISION = lax.Precision.HIGHEST
NORM_EPSILON = 1e-06
BETA_ONE = 0.9
BETA_TWO = 0.95
STAT_DECAY = 0.95
LEARN_RATE = 0.1
WEIGHT_DECAY = 0.01
ADAM_EPSILON = 1e-08
CLIP_NORM = 1.0
MASK_FLOOR = -1e+30

@jax.custom_vjp
def low(v):
    return lax.optimization_barrier(v.astype(jnp.bfloat16)).astype(jnp.float32)

@jax.custom_vjp
def low_back(v):
    return v

def low_keep(v):
    return (low(v), None)

def low_pass(kept, grad):
    return (grad,)

def back_keep(v):
    return (v, None)

def back_low(kept, grad):
    return (low(grad),)
low.defvjp(low_keep, low_pass)
low_back.defvjp(back_keep, back_low)

def layout():
    return [('gain_one', (D,)), ('shift_one', (D,)), ('gain_two', (D,)), ('shift_two', (D,)), ('gain_three', (D,)), ('shift_three', (D,)), ('bias_query', (D,)), ('bias_value', (D,)), ('bias_out', (D,)), ('bias_up', (FF,)), ('bias_down', (D,)), ('conv_first', (D, 9, NT)), ('conv_second', (9, NT, NT)), ('conv_third', (9, NT, NT)), ('conv_fourth', (9, NT, NT)), ('conv_bias', (4, NT))]

def unpack(vector):
    params_split = {}
    offset = 0
    for part_name, part_shape in layout():
        entries = math.prod(part_shape)
        params_split[part_name] = vector[offset:offset + entries].reshape(part_shape)
        offset = offset + entries
    return params_split

def matrix_shapes():
    return [(D, 3 * D), (D, D), (D, FF), (FF, D)]

def to_blocks(matrix):
    row_count, col_count = matrix.shape
    tiled = matrix.reshape(row_count // BLOCK_SIDE, BLOCK_SIDE, col_count // BLOCK_SIDE, BLOCK_SIDE)
    return tiled.transpose(0, 2, 1, 3).reshape(-1, BLOCK_SIDE, BLOCK_SIDE)

def from_blocks(blocks):
    matrices = []
    offset = 0
    for row_count, col_count in matrix_shapes():
        tiles = row_count // BLOCK_SIDE * (col_count // BLOCK_SIDE)
        piece_tiles = blocks[offset:offset + tiles].reshape(row_count // BLOCK_SIDE, col_count // BLOCK_SIDE, BLOCK_SIDE, BLOCK_SIDE)
        matrices.append(piece_tiles.transpose(0, 2, 1, 3).reshape(row_count, col_count))
        offset = offset + tiles
    return matrices

def layer_norm(values, gain_vec, shift_vec):
    centre = lax.optimization_barrier(jnp.mean(values, -1, keepdims=True))
    centered = values - centre
    spread = lax.optimization_barrier(jnp.mean(centered * centered, -1, keepdims=True))
    return centered * lax.rsqrt(spread + NORM_EPSILON) * gain_vec + shift_vec

def gelu_exact(values):
    return jax.nn.gelu(values, approximate=False)

def taps_sum(taps):
    padded = jnp.pad(taps, ((0, 0), (1, 1), (1, 1), (0, 0), (0, 0)))
    summed = jnp.zeros(taps.shape[:3] + taps.shape[4:], taps.dtype)
    for tap_index in range(9):
        row_off = tap_index // 3 - 1
        col_off = tap_index % 3 - 1
        summed = summed + padded[:, 1 + row_off:1 + row_off + GRID, 1 + col_off:1 + col_off + GRID, tap_index]
    return summed

def conv_small(values, weight):
    taps = jnp.einsum('fyxc,tco->fyxto', values, weight, precision=FULL_PRECISION)
    return taps_sum(taps)

def learner_tail(first_pre, values, second_w, third_w, fourth_w, tail_bias):
    frames = first_pre.shape[0]
    act_one = gelu_exact(first_pre)
    act_two = gelu_exact(conv_small(act_one, second_w) + tail_bias[0])
    act_three = gelu_exact(conv_small(act_two, third_w) + tail_bias[1])
    maps = jax.nn.sigmoid(conv_small(act_three, fourth_w) + tail_bias[2])
    grid_values = values.reshape(frames, GRID, GRID, values.shape[-1])
    pooled = jnp.einsum('fyxk,fyxd->fkd', maps, grid_values, precision=FULL_PRECISION)
    return pooled.reshape(frames * NT, values.shape[-1])

def clip_segments(lengths, order_row):
    clip_ids = jnp.arange(lengths.shape[0], dtype=jnp.int32)
    ordered_len = lax.optimization_barrier(jnp.sum(jnp.where(order_row[:, None] == clip_ids[None, :], lengths[None, :], 0), 1))
    ends = jnp.cumsum(ordered_len)
    slots = jnp.arange(GF, dtype=jnp.int32)
    places = slots % FR_DEV * N_FRAME + slots // FR_DEV
    return lax.optimization_barrier(jnp.sum((ends[None, :] <= places[:, None]).astype(jnp.int32), 1))

def cholesky_basis(product):
    gram_matrix = jnp.einsum('sji,sjk->sik', product, product, precision=FULL_PRECISION)
    lower_factor = jnp.linalg.cholesky(gram_matrix)
    solved = jax.scipy.linalg.solve_triangular(lower_factor, jnp.swapaxes(product, 1, 2), lower=True)
    return jnp.swapaxes(solved, 1, 2)

def soap_update(clipped, master, moment1, moment2, stat_left, stat_right, basis_left, basis_right):
    rotated = jnp.einsum('sji,sjk->sik', basis_left, clipped, precision=FULL_PRECISION)
    rotated = jnp.einsum('sik,skl->sil', rotated, basis_right, precision=FULL_PRECISION)
    first_new = BETA_ONE * moment1 + (1.0 - BETA_ONE) * rotated
    second_new = BETA_TWO * moment2 + (1.0 - BETA_TWO) * rotated * rotated
    direction = first_new / (1.0 - BETA_ONE ** STEP) / (jnp.sqrt(second_new / (1.0 - BETA_TWO ** STEP)) + ADAM_EPSILON)
    returned = jnp.einsum('sij,sjk->sik', basis_left, direction, precision=FULL_PRECISION)
    returned = jnp.einsum('sik,slk->sil', returned, basis_right, precision=FULL_PRECISION)
    new_master = master - LEARN_RATE * (returned + WEIGHT_DECAY * master)
    new_left = STAT_DECAY * stat_left + (1.0 - STAT_DECAY) * jnp.einsum('sij,skj->sik', clipped, clipped, precision=FULL_PRECISION)
    new_right = STAT_DECAY * stat_right + (1.0 - STAT_DECAY) * jnp.einsum('sji,sjk->sik', clipped, clipped, precision=FULL_PRECISION)
    new_basis_left = cholesky_basis(jnp.einsum('sij,sjk->sik', new_left, basis_left, precision=FULL_PRECISION))
    new_basis_right = cholesky_basis(jnp.einsum('sij,sjk->sik', new_right, basis_right, precision=FULL_PRECISION))
    turn_left = jnp.einsum('sji,sjk->sik', new_basis_left, basis_left, precision=FULL_PRECISION)
    turn_right = jnp.einsum('sji,sjk->sik', basis_right, new_basis_right, precision=FULL_PRECISION)
    moved = jnp.einsum('sij,sjk->sik', turn_left, first_new, precision=FULL_PRECISION)
    moved = jnp.einsum('sij,sjk->sik', moved, turn_right, precision=FULL_PRECISION)
    return (new_master, moved, second_new, new_left, new_right, new_basis_left, new_basis_right)

def adam_update(clipped, params_old, first_old, second_old):
    first_new = BETA_ONE * first_old + (1.0 - BETA_ONE) * clipped
    second_new = BETA_TWO * second_old + (1.0 - BETA_TWO) * clipped * clipped
    stepped = first_new / (1.0 - BETA_ONE ** STEP) / (jnp.sqrt(second_new / (1.0 - BETA_TWO ** STEP)) + ADAM_EPSILON)
    return (first_new, second_new, params_old - LEARN_RATE * stepped)

def attention(query_rows, key_heads, value_heads, seg_tokens):
    rows_block = TOK_DEV
    score_scale = 1.0 / math.sqrt(HD)

    def one_block(block_id):
        first_row = block_id * rows_block
        query_block = lax.dynamic_slice_in_dim(query_rows, first_row, rows_block)
        seg_query = lax.dynamic_slice_in_dim(seg_tokens, first_row, rows_block)
        scores = jnp.einsum('qhd,khd->hqk', query_block, key_heads, precision=FULL_PRECISION) * score_scale
        allowed = (seg_query[:, None] == seg_tokens[None, :])[None]
        scores = low_back(jnp.where(allowed, scores, MASK_FLOOR))
        softmax_weights = jax.nn.softmax(scores, axis=-1)
        return jnp.einsum('hqk,khd->qhd', low(softmax_weights), value_heads, precision=FULL_PRECISION)
    blocks_out = lax.map(jax.checkpoint(one_block), jnp.arange(TOK_GROUP // rows_block, dtype=jnp.int32))
    return blocks_out.reshape(TOK_GROUP, D)

def group_forward(group_tokens, segment_slots, lowered, params_split, conv_low):
    w_qkv, w_out, w_up, w_down = lowered
    normed_one = layer_norm(group_tokens, params_split['gain_one'], params_split['shift_one'])
    qkv_bias = jnp.concatenate([params_split['bias_query'], jnp.zeros_like(params_split['bias_query']), params_split['bias_value']])
    projected = low_back(low(jnp.dot(low(normed_one), w_qkv, precision=FULL_PRECISION) + qkv_bias))
    query_rows = projected[:, :D].reshape(TOK_GROUP, HEADS, HD)
    key_heads = projected[:, D:2 * D].reshape(TOK_GROUP, HEADS, HD)
    value_heads = projected[:, 2 * D:].reshape(TOK_GROUP, HEADS, HD)
    seg_tokens = jnp.repeat(segment_slots, GRID * GRID)
    attended = low_back(low(attention(query_rows, key_heads, value_heads, seg_tokens)))
    mixed_sum = group_tokens + low_back(jnp.dot(attended, w_out, precision=FULL_PRECISION) + params_split['bias_out'])
    normed_two = layer_norm(mixed_sum, params_split['gain_two'], params_split['shift_two'])
    hidden = low_back(jnp.dot(low(normed_two), w_up, precision=FULL_PRECISION) + params_split['bias_up'])
    activated = low(gelu_exact(hidden))
    output_two = mixed_sum + low_back(jnp.dot(activated, w_down, precision=FULL_PRECISION) + params_split['bias_down'])
    normed_three = layer_norm(output_two, params_split['gain_three'], params_split['shift_three'])
    taps = jnp.dot(low(normed_three), conv_low.reshape(D, 9 * NT), precision=FULL_PRECISION).reshape(GF, GRID, GRID, 9, NT)
    first_pre = low_back(taps_sum(taps) + params_split['conv_bias'][0])
    return learner_tail(first_pre, output_two, params_split['conv_second'], params_split['conv_third'], params_split['conv_fourth'], params_split['conv_bias'][1:])

def reference(tokens, cotangent, clip_lengths, clip_order, block_owner, master, moment1, moment2, stat_left, stat_right, basis_left, basis_right, small_params, small_moment1, small_moment2):
    ordered = jnp.zeros_like(master).at[block_owner].set(master)
    matrices = tuple(from_blocks(ordered))
    segments = jax.vmap(clip_segments)(clip_lengths, clip_order)
    inputs = tokens.astype(jnp.float32)

    def forward(group_inputs, weight_set, small_vector):
        lowered = [low(matrix) for matrix in weight_set]
        params_split = unpack(small_vector)
        conv_low = low(params_split['conv_first'])

        def one_group(paired):
            return group_forward(paired[0], paired[1], lowered, params_split, conv_low)
        return lax.map(jax.checkpoint(one_group), (group_inputs, segments))
    learned, pullback = jax.vjp(forward, inputs, matrices, small_params)
    grad_input, gradient_matrices, grad_small = pullback(cotangent.astype(jnp.float32))
    padding_amount = jnp.zeros((SLOT_COUNT - MATRIX_BLOCKS, BLOCK_SIDE, BLOCK_SIDE), gradient_matrices[0].dtype)
    grad_blocks = jnp.concatenate([to_blocks(matrix) for matrix in gradient_matrices] + [padding_amount])[block_owner]
    grad_norm = jnp.sqrt(jnp.sum(grad_blocks * grad_blocks) + jnp.sum(grad_small * grad_small))
    factor = 1.0 / jnp.maximum(grad_norm, CLIP_NORM)
    soap_out = soap_update(grad_blocks * factor, master, moment1, moment2, stat_left, stat_right, basis_left, basis_right)
    small_first, small_second, small_new = adam_update(grad_small * factor, small_params, small_moment1, small_moment2)
    return (learned, grad_input, soap_out[0], soap_out[1], soap_out[2], soap_out[3], soap_out[4], soap_out[5], soap_out[6], small_first, small_second, small_new, grad_norm)
```

```python
import math

import jax
import jax.numpy as jnp
from jax import lax
from jax.experimental import pallas as pl
from jax.experimental.pallas import tpu as pltpu
from jax.sharding import Mesh
from jax.sharding import PartitionSpec as P

D = 768
HEADS = 12
HD = 64
FF = 3072
GRID = 14
NT = 8
BLOCK_SIDE = 128
STEP = 10
MATRIX_BLOCKS = 432


FULL_PRECISION = lax.Precision.HIGHEST
NORM_EPSILON = 1e-06
BETA_ONE = 0.9
BETA_TWO = 0.95
STAT_DECAY = 0.95
LEARN_RATE = 0.1
WEIGHT_DECAY = 0.01
ADAM_EPSILON = 1e-08
CLIP_NORM = 1.0
MASK_FLOOR = -1e30


def layout():
    return [
        ("gain_one", (D,)),
        ("shift_one", (D,)),
        ("gain_two", (D,)),
        ("shift_two", (D,)),
        ("gain_three", (D,)),
        ("shift_three", (D,)),
        ("bias_query", (D,)),
        ("bias_value", (D,)),
        ("bias_out", (D,)),
        ("bias_up", (FF,)),
        ("bias_down", (D,)),
        ("conv_first", (D, 9, NT)),
        ("conv_second", (9, NT, NT)),
        ("conv_third", (9, NT, NT)),
        ("conv_fourth", (9, NT, NT)),
        ("conv_bias", (4, NT)),
    ]


def unpack(vector):
    params_split = {}
    offset = 0
    for part_name, part_shape in layout():
        entries = math.prod(part_shape)
        params_split[part_name] = vector[offset : offset + entries].reshape(part_shape)
        offset = offset + entries
    return params_split


def matrix_shapes():
    return [(D, 3 * D), (D, D), (D, FF), (FF, D)]


def to_blocks(matrix):
    row_count, col_count = matrix.shape
    tiled = matrix.reshape(row_count // BLOCK_SIDE, BLOCK_SIDE, col_count // BLOCK_SIDE, BLOCK_SIDE)
    return tiled.transpose(0, 2, 1, 3).reshape(-1, BLOCK_SIDE, BLOCK_SIDE)


def from_blocks(blocks):
    matrices = []
    offset = 0
    for row_count, col_count in matrix_shapes():
        tiles = row_count // BLOCK_SIDE * (col_count // BLOCK_SIDE)
        piece_tiles = blocks[offset : offset + tiles].reshape(
            row_count // BLOCK_SIDE, col_count // BLOCK_SIDE, BLOCK_SIDE, BLOCK_SIDE
        )
        matrices.append(piece_tiles.transpose(0, 2, 1, 3).reshape(row_count, col_count))
        offset = offset + tiles
    return matrices


def layer_norm(values, gain_vec, shift_vec):
    centre = jnp.mean(values, -1, keepdims=True)
    centered = values - centre
    spread = jnp.mean(centered * centered, -1, keepdims=True)
    return centered * lax.rsqrt(spread + NORM_EPSILON) * gain_vec + shift_vec


def gelu_exact(values):
    return jax.nn.gelu(values, approximate=False)


def taps_sum(taps):
    padded = jnp.pad(taps, ((0, 0), (1, 1), (1, 1), (0, 0), (0, 0)))
    summed = jnp.zeros(taps.shape[:3] + taps.shape[4:], taps.dtype)
    for tap_index in range(9):
        row_off = tap_index // 3 - 1
        col_off = tap_index % 3 - 1
        summed = (
            summed
            + padded[
                :, 1 + row_off : 1 + row_off + GRID, 1 + col_off : 1 + col_off + GRID, tap_index
            ]
        )
    return summed


def taps_back(grads):
    padded = jnp.pad(grads, ((0, 0), (1, 1), (1, 1), (0, 0)))
    shifted = []
    for tap_index in range(9):
        row_off = tap_index // 3 - 1
        col_off = tap_index % 3 - 1
        shifted.append(
            padded[:, 1 - row_off : 1 - row_off + GRID, 1 - col_off : 1 - col_off + GRID]
        )
    return jnp.stack(shifted, axis=3)


def conv_small(values, weight):
    taps = jnp.einsum("fyxc,tco->fyxto", values, weight, precision=FULL_PRECISION)
    return taps_sum(taps)


def learner_tail(first_pre, values, second_w, third_w, fourth_w, tail_bias):
    frames = first_pre.shape[0]
    act_one = gelu_exact(first_pre)
    act_two = gelu_exact(conv_small(act_one, second_w) + tail_bias[0])
    act_three = gelu_exact(conv_small(act_two, third_w) + tail_bias[1])
    maps = jax.nn.sigmoid(conv_small(act_three, fourth_w) + tail_bias[2])
    grid_values = values.reshape(frames, GRID, GRID, values.shape[-1])
    pooled = jnp.einsum("fyxk,fyxd->fkd", maps, grid_values, precision=FULL_PRECISION)
    return pooled.reshape(frames * NT, values.shape[-1])


def clip_segments(lengths, order_row, group_frames, frames_dev, frame_count):
    clip_ids = jnp.arange(lengths.shape[0], dtype=jnp.int32)
    ordered_len = jnp.sum(
        jnp.where(order_row[:, None] == clip_ids[None, :], lengths[None, :], 0), 1
    )
    ends = jnp.cumsum(ordered_len)
    slots = jnp.arange(group_frames, dtype=jnp.int32)
    places = slots % frames_dev * frame_count + slots // frames_dev
    return jnp.sum((ends[None, :] <= places[:, None]).astype(jnp.int32), 1)


F32=jnp.float32; BF=jnp.bfloat16
NN=(((1,),(0,)),((),()))
NT_=(((1,),(1,)),((),()))
TN=(((0,),(0,)),((),()))

def halves(a):
    high = a.astype(BF)
    return high, (a - high.astype(F32)).astype(BF)

def dot_low(a, b, dims):
    return lax.dot_general(a, b, dims, preferred_element_type=F32)

def dot_parts(a, b, dims):
    ah, al = a
    bh, bl = b
    return dot_low(ah, bh, dims) + (dot_low(ah, bl, dims) + dot_low(al, bh, dims))

def dot_wide(a, b, dims):
    return dot_parts(halves(a), halves(b), dims)

def stat_kernel(sl, sr, bl, br, ol, orr):
    ol[0] = STAT_DECAY * dot_wide(bl[0], sl[0], TN)
    orr[0] = STAT_DECAY * dot_wide(br[0], sr[0], TN)

def slot_spec():
    return pl.BlockSpec((1, BLOCK_SIDE, BLOCK_SIDE), lambda i: (i, 0, 0))

def stat_products(sl, sr, bl, br):
    n = sl.shape[0]
    shape = jax.ShapeDtypeStruct(sl.shape, F32)
    return pl.pallas_call(stat_kernel, grid=(n,), in_specs=[slot_spec()]*4, out_specs=[slot_spec()]*2, out_shape=[shape]*2)(sl, sr, bl, br)

def raw_kernel(g, bl, br, rot, gl, gr, ql, qr):
    gp = halves(g[0]); blp = halves(bl[0]); brp = halves(br[0])
    u = halves(dot_parts(blp, gp, TN))
    v = halves(dot_parts(gp, brp, NN))
    rot[0] = dot_parts(u, brp, NN)
    gl[0] = dot_parts(gp, gp, NT_)
    gr[0] = dot_parts(gp, gp, TN)
    ql[0] = dot_parts(u, gp, NT_)
    qr[0] = dot_parts(v, gp, TN)

def raw_products(g, bl, br):
    n = g.shape[0]
    shape = jax.ShapeDtypeStruct(g.shape, F32)
    return pl.pallas_call(raw_kernel, grid=(n,), in_specs=[slot_spec()]*3, out_specs=[slot_spec()]*5, out_shape=[shape]*5)(g, bl, br)

NB=32
def finish_kernel(factor, rot, gl, gr, ql, qr, pl_, pr_, sl, sr, bl, br, master, m1, m2,
                  o_master, o_m1, o_m2, o_left, o_right, o_bl, o_br, work, elim, mom):
    n = rot.shape[0]
    f = factor[0]
    f2 = (1.0 - STAT_DECAY) * f * f
    for s in range(n):
        r = f * rot[s]
        m = BETA_ONE * m1[s] + (1.0 - BETA_ONE) * r
        v = BETA_TWO * m2[s] + (1.0 - BETA_TWO) * r * r
        mom[s] = m
        o_m2[s] = v
        o_left[s] = STAT_DECAY * sl[s] + f2 * gl[s]
        o_right[s] = STAT_DECAY * sr[s] + f2 * gr[s]
        for side, (p_, q_) in enumerate(((pl_, ql), (pr_, qr))):
            at = p_[s] + f2 * q_[s]
            work[2*s+side, :, 128:] = at
            atp = halves(at)
            work[2*s+side, :, :128] = dot_parts(atp, atp, NT_)
    rows = lax.broadcasted_iota(jnp.int32, (1, 8, 2*NB), 1)
    lanes = lax.broadcasted_iota(jnp.int32, (1, 8, 2*NB), 2)
    count = 2*n

    def panel(p, carry):
        for q in range(128 // NB):
            @pl.when(p == q)
            def _(q=q):
                for t in range(NB // 8):
                    block = work[:, NB*q+8*t:NB*q+8*t+8, NB*q:NB*q+NB]
                    eye = jnp.where(lanes - NB == rows + 8*t, 1.0, 0.0).astype(F32)
                    eye = jnp.broadcast_to(eye, (count, 8, 2*NB))
                    elim[:, 8*t:8*t+8, :] = jnp.concatenate([block, eye[:, :, NB:]], axis=2)
        tiles = [elim[:, 8*t:8*t+8, :] for t in range(NB // 8)]
        for k in range(NB):
            t0, j = divmod(k, 8)
            pivot = tiles[t0][:, j:j+1, k:k+1]
            scale = lax.rsqrt(pivot)
            row = tiles[t0][:, j:j+1, :] * scale
            for t in range(t0, NB // 8):
                col = tiles[t][:, :, k:k+1] * scale
                new = tiles[t] - col * row
                if t == t0:
                    new = jnp.where(rows > j, new, jnp.where(rows == j, row, tiles[t]))
                tiles[t] = new
        for t in range(NB // 8):
            elim[:, 8*t:8*t+8, :] = tiles[t]
        for q in range(128 // NB):
            @pl.when(p == q)
            def _(q=q):
                lo, hi = NB*q, NB*q+NB
                for m in range(count):
                    inv = halves(elim[m, :, NB:])
                    y = dot_parts(inv, halves(work[m, lo:hi, :]), NN)
                    if m % 2 == 0:
                        o_bl[m // 2, lo:hi, :] = y[:, 128:]
                    else:
                        o_br[m // 2, lo:hi, :] = y[:, 128:]
                    if hi < 128:
                        yp = halves(y)
                        up = (yp[0][:, hi:128], yp[1][:, hi:128])
                        work[m, hi:, :] = work[m, hi:, :] - dot_parts(up, yp, TN)
        return carry
    lax.fori_loop(0, 128 // NB, panel, 0)

    for s in range(n):
        m = mom[s]
        v = o_m2[s]
        direction = m / (1.0 - BETA_ONE**STEP) / (jnp.sqrt(v / (1.0 - BETA_TWO**STEP)) + ADAM_EPSILON)
        blp, brp = halves(bl[s]), halves(br[s])
        back = halves(dot_parts(blp, halves(direction), NN))
        returned = dot_parts(back, brp, NT_)
        o_master[s] = master[s] - LEARN_RATE * (returned + WEIGHT_DECAY * master[s])
        qlt, qrt = o_bl[s], o_br[s]
        qltp, qrtp = halves(qlt), halves(qrt)
        turn_l = halves(dot_parts(qltp, blp, NN))
        turn_r = halves(dot_parts(qrtp, brp, NN))
        half = halves(dot_parts(turn_l, halves(m), NN))
        o_m1[s] = dot_parts(half, turn_r, NT_)
        o_bl[s] = qlt.T
        o_br[s] = qrt.T

def finish(factor, rot, gl, gr, ql, qr, pl_, pr_, sl, sr, bl, br, master, m1, m2):
    n = rot.shape[0]
    shape = jax.ShapeDtypeStruct(rot.shape, F32)
    vm = pl.BlockSpec(memory_space=pltpu.VMEM)
    return pl.pallas_call(finish_kernel,
        in_specs=[pl.BlockSpec(memory_space=pltpu.SMEM)] + [vm]*14, out_specs=[vm]*7, out_shape=[shape]*7,
        scratch_shapes=[pltpu.VMEM((2*n,128,256),F32), pltpu.VMEM((2*n,NB,2*NB),F32), pltpu.VMEM((n,128,128),F32)],
        compiler_params=pltpu.CompilerParams(vmem_limit_bytes=56*1024*1024),
    )(factor, rot, gl, gr, ql, qr, pl_, pr_, sl, sr, bl, br, master, m1, m2)

def soap(g, factor, master, m1, m2, sl, sr, bl, br):
    p_l, p_r = stat_products(sl, sr, bl, br)
    rot, gl, gr, ql, qr = raw_products(g, bl, br)
    return finish(factor.reshape(1), rot, gl, gr, ql, qr, p_l, p_r, sl, sr, bl, br, master, m1, m2)


def adam_update(clipped, params_old, first_old, second_old):
    first_new = BETA_ONE * first_old + (1.0 - BETA_ONE) * clipped
    second_new = BETA_TWO * second_old + (1.0 - BETA_TWO) * clipped * clipped
    stepped = (
        first_new
        / (1.0 - BETA_ONE**STEP)
        / (jnp.sqrt(second_new / (1.0 - BETA_TWO**STEP)) + ADAM_EPSILON)
    )
    return (first_new, second_new, params_old - LEARN_RATE * stepped)


FRAME_ROWS = GRID * GRID
PAD_ROWS = 208
PAIRS = HEADS // 2
PAIR = 2 * HD
ALL_AXES = ("fz", "fx", "by", "core")
FRAME_AXES = ("fz", "fx")


def matrix_places():
    places = []
    first = 0
    for row_count, col_count in matrix_shapes():
        cols = col_count // BLOCK_SIDE
        count = row_count // BLOCK_SIDE * cols
        places.append((first, count, cols))
        first = first + count
    return places


def tile_at(ref, tile, cols):
    row = pl.multiple_of(lax.div(tile, cols) * BLOCK_SIDE, BLOCK_SIDE)
    col = pl.multiple_of(lax.rem(tile, cols) * BLOCK_SIDE, BLOCK_SIDE)
    return ref.at[pl.ds(row, BLOCK_SIDE), pl.ds(col, BLOCK_SIDE)]


def place_kernel(owner, gathered, w_qkv, w_out, w_up, w_down, sems):
    outs = (w_qkv, w_out, w_up, w_down)

    def one_slot(slot, carry):
        block = owner[slot]
        for which, (first, count, cols) in enumerate(matrix_places()):
            @pl.when((block >= first) & (block < first + count))
            def _():
                pltpu.make_async_copy(
                    gathered.at[slot], tile_at(outs[which], block - first, cols), sems.at[which]
                ).start()
        return carry

    lax.fori_loop(0, gathered.shape[0], one_slot, 0)
    for which in range(4):
        pltpu.make_async_copy(outs[which], outs[which], sems.at[which]).wait()


def place_blocks(owner, gathered):
    anywhere = pl.BlockSpec(memory_space=pl.ANY)
    return pl.pallas_call(
        place_kernel,
        grid_spec=pltpu.PrefetchScalarGridSpec(
            num_scalar_prefetch=1,
            grid=(1,),
            in_specs=[anywhere],
            out_specs=[pl.BlockSpec(memory_space=pltpu.VMEM)] * 4,
            scratch_shapes=[pltpu.SemaphoreType.DMA((4,))],
        ),
        out_shape=[jax.ShapeDtypeStruct(shape, BF) for shape in matrix_shapes()],
        compiler_params=pltpu.CompilerParams(vmem_limit_bytes=48 * 1024 * 1024),
    )(owner, gathered)


def spread_kernel(sizes, slots_dev, owner, coords, g_qkv, g_out, g_up, g_down, blank, part_a, part_b, sems):
    grads = (g_qkv, g_out, g_up, g_down)
    parts = (part_a, part_b)
    nz, nx, ny, nc = sizes
    half = slots_dev // 2

    def one_slot(slot, carry):
        block = owner[slot]
        device = lax.div(slot, slots_dev)
        inner = lax.rem(slot, slots_dev)
        offs = []
        for axis, size in ((3, nc), (2, ny), (1, nx), (0, nz)):
            offs.append(lax.rem(lax.rem(device, size) - coords[axis] + size, size))
            device = lax.div(device, size)
        rc, ry, rx, rz = offs
        place_a = (((rc * nx + rx) * ny + ry) * nz + rz) * half + inner
        place_b = (((rc * ny + ry) * nx + rx) * nz + rz) * half + inner - half
        for part in range(2):
            chosen = (inner < half) if part == 0 else (inner >= half)
            place = place_a if part == 0 else place_b
            for which, (first, count, cols) in enumerate(matrix_places()):
                @pl.when(chosen & (block >= first) & (block < first + count))
                def _():
                    pltpu.make_async_copy(
                        tile_at(grads[which], block - first, cols), parts[part].at[place], sems.at[part]
                    ).start()

            @pl.when(chosen & (block >= MATRIX_BLOCKS))
            def _():
                pltpu.make_async_copy(blank, parts[part].at[place], sems.at[part]).start()
        return carry

    lax.fori_loop(0, nz * nx * ny * nc * slots_dev, one_slot, 0)
    for part in range(2):
        pltpu.make_async_copy(parts[part], parts[part], sems.at[part]).wait()


def spread_blocks(sizes, slots_dev, owner, coords, grads):
    anywhere = pl.BlockSpec(memory_space=pl.ANY)
    nz, nx, ny, nc = sizes
    half = slots_dev // 2
    shape = jax.ShapeDtypeStruct((nz * nx * ny * nc * half, BLOCK_SIDE, BLOCK_SIDE), BF)

    def kernel(*refs):
        spread_kernel(sizes, slots_dev, *refs)

    part_a, part_b = pl.pallas_call(
        kernel,
        grid_spec=pltpu.PrefetchScalarGridSpec(
            num_scalar_prefetch=2,
            grid=(1,),
            in_specs=[pl.BlockSpec(memory_space=pltpu.VMEM)] * 5,
            out_specs=[anywhere] * 2,
            scratch_shapes=[pltpu.SemaphoreType.DMA((2,))],
        ),
        out_shape=[shape, shape],
        compiler_params=pltpu.CompilerParams(vmem_limit_bytes=48 * 1024 * 1024),
    )(owner, coords, *grads, jnp.zeros((BLOCK_SIDE, BLOCK_SIDE), BF))
    tail = (half, BLOCK_SIDE, BLOCK_SIDE)
    return part_a.reshape((nc, nx, ny, nz) + tail), part_b.reshape((nc, ny, nx, nz) + tail)


def moved(value, axis, size, step):
    return lax.ppermute(value, axis, [(i, (i + step) % size) for i in range(size)])


def reduce_axis(buf, axis, size):
    total = buf[0].astype(F32)
    for step in range(1, size):
        total = total + moved(buf[step], axis, size, step).astype(F32)
    return total


def gather_axis(value, axis, size):
    return jnp.stack([value] + [moved(value, axis, size, -step) for step in range(1, size)])


def rolled(value, axis, size, step):
    return lax.dynamic_slice_in_dim(jnp.concatenate([value, value], axis), step, size, axis)


def attend_kernel(long_rows, q, k, v, bias, out):
    lanes = lax.broadcasted_iota(jnp.int32, (1, PAIR), 1)
    first = lanes < HD
    total = k.shape[0]
    for frame, (lo, hi) in enumerate(((0, long_rows), (long_rows, total))):
        rows = slice(frame * PAD_ROWS, (frame + 1) * PAD_ROWS)
        query = q[rows, :]
        keys, values = k[lo:hi, :], v[lo:hi, :]
        results = []
        for side in range(2):
            chosen = jnp.where(first if side == 0 else ~first, query, jnp.zeros_like(query))
            scores = dot_low(chosen, keys, NT_) + bias[:, lo:hi]
            weights = jnp.exp(scores - jnp.max(scores, axis=1, keepdims=True))
            norm = jnp.sum(weights, axis=1, keepdims=True)
            results.append(dot_low(weights.astype(BF), values, NN) / norm)
        out[rows, :] = jnp.where(first, results[0], results[1]).astype(BF)


def attend_back_kernel(long_rows, q, k, v, bias, grad, dq, dk, dv):
    lanes = lax.broadcasted_iota(jnp.int32, (1, PAIR), 1)
    first = lanes < HD
    total = k.shape[0]
    for frame, (lo, hi) in enumerate(((0, long_rows), (long_rows, total))):
        rows = slice(frame * PAD_ROWS, (frame + 1) * PAD_ROWS)
        query, arriving = q[rows, :], grad[rows, :]
        keys, values = k[lo:hi, :], v[lo:hi, :]
        query_parts, key_total, value_total = [], 0.0, 0.0
        for side in range(2):
            mask = first if side == 0 else ~first
            chosen = jnp.where(mask, query, jnp.zeros_like(query))
            incoming = jnp.where(mask, arriving, jnp.zeros_like(arriving))
            scores = dot_low(keys, chosen, NT_) + bias[lo:hi, :]
            weights = jnp.exp(scores - jnp.max(scores, axis=0, keepdims=True))
            soft = weights * (1.0 / jnp.sum(weights, axis=0, keepdims=True))
            grad_soft = dot_low(values, incoming, NT_)
            delta = jnp.sum(soft * grad_soft, axis=0, keepdims=True)
            grad_scores = (soft * (grad_soft - delta)).astype(BF)
            key_total = key_total + dot_low(grad_scores, chosen, NN)
            value_total = value_total + dot_low(soft.astype(BF), incoming, NN)
            query_parts.append(dot_low(grad_scores, keys, TN))
        dq[rows, :] = (jnp.where(first, query_parts[0], query_parts[1]) * (1.0 / math.sqrt(HD))).astype(BF)
        dk[lo:hi, :] = key_total.astype(BF)
        dv[lo:hi, :] = value_total.astype(BF)


def pair_spec(rows, offset=0):
    return pl.BlockSpec((rows, PAIR), lambda i: (0, i + offset))


def attend(q, kv, bias):
    keys_total = kv.shape[0]
    long_rows = keys_total - 2 * PAD_ROWS

    def kernel(*refs):
        attend_kernel(long_rows, *refs)

    return pl.pallas_call(
        kernel,
        grid=(PAIRS,),
        in_specs=[
            pair_spec(2 * PAD_ROWS),
            pair_spec(keys_total),
            pair_spec(keys_total, PAIRS),
            pl.BlockSpec((1, keys_total), lambda i: (0, 0)),
        ],
        out_specs=pair_spec(2 * PAD_ROWS),
        out_shape=jax.ShapeDtypeStruct((2 * PAD_ROWS, D), BF),
        compiler_params=pltpu.CompilerParams(vmem_limit_bytes=48 * 1024 * 1024),
    )(q, kv, kv, bias.reshape(1, -1))


def attend_back(q, kv, bias, grad):
    keys_total = kv.shape[0]
    long_rows = keys_total - 2 * PAD_ROWS

    def kernel(*refs):
        attend_back_kernel(long_rows, *refs)

    return pl.pallas_call(
        kernel,
        grid=(PAIRS,),
        in_specs=[
            pair_spec(2 * PAD_ROWS),
            pair_spec(keys_total),
            pair_spec(keys_total, PAIRS),
            pl.BlockSpec((keys_total, 1), lambda i: (0, 0)),
            pair_spec(2 * PAD_ROWS),
        ],
        out_specs=[pair_spec(2 * PAD_ROWS), pair_spec(keys_total), pair_spec(keys_total)],
        out_shape=[
            jax.ShapeDtypeStruct((2 * PAD_ROWS, D), BF),
            jax.ShapeDtypeStruct((keys_total, D), BF),
            jax.ShapeDtypeStruct((keys_total, D), BF),
        ],
        compiler_params=pltpu.CompilerParams(vmem_limit_bytes=48 * 1024 * 1024),
    )(q, kv, kv, bias.reshape(-1, 1), grad)


def pad_frames(values):
    frames = values.reshape(2, FRAME_ROWS, values.shape[-1])
    return jnp.pad(frames, ((0, 0), (0, PAD_ROWS - FRAME_ROWS), (0, 0)))


def unpad_frames(values):
    frames = values.reshape(2, PAD_ROWS, values.shape[-1])[:, :FRAME_ROWS]
    return frames.reshape(2 * FRAME_ROWS, values.shape[-1])


def normalized(values):
    centered = values - jnp.mean(values, -1, keepdims=True)
    spread = lax.rsqrt(jnp.mean(centered * centered, -1, keepdims=True) + NORM_EPSILON)
    return centered * spread, spread


def on_device(
    tokens,
    cotangent,
    clip_lengths,
    clip_order,
    block_owner,
    master,
    moment1,
    moment2,
    stat_left,
    stat_right,
    basis_left,
    basis_right,
    small_params,
    small_moment1,
    small_moment2,
):
    sizes = tuple(lax.axis_size(name) for name in ALL_AXES)
    coords = [lax.axis_index(name) for name in ALL_AXES]
    nz, nx, ny, nc = sizes
    device_count = nz * nx * ny * nc
    frame_count = nz * nx
    frame_index = coords[0] * nx + coords[1]
    slots_dev = master.shape[0]
    params_split = unpack(small_params)

    segment_slots = clip_segments(
        clip_lengths[0], clip_order[0], 2 * frame_count, 2, frame_count
    ).reshape(frame_count, 2)
    ordered_len = clip_lengths[0][clip_order[0]]
    longest = jnp.argmax(ordered_len).astype(jnp.int32)
    second_long = segment_slots[:, 1] == longest
    short_segment = jnp.where(second_long, segment_slots[:, 0], segment_slots[:, 1])
    swap = second_long[frame_index]
    padded_segment = jnp.pad(short_segment, (1, 1), constant_values=-1)
    near = lax.dynamic_slice_in_dim(padded_segment, frame_index, 3)
    with_previous = near[0] == near[1]
    with_next = near[2] == near[1]

    own_frames = pad_frames(tokens[0])
    own_frames = jnp.where(swap, own_frames[::-1], own_frames)
    long_frame, short_frame = own_frames[0], own_frames[1]
    frame_perm = [(i, (i + 1) % frame_count) for i in range(frame_count)]
    back_perm = [(j, i) for i, j in frame_perm]
    from_previous = lax.ppermute(short_frame, FRAME_AXES, frame_perm)
    from_next = lax.ppermute(short_frame, FRAME_AXES, back_perm)
    partner = jnp.where(with_next, from_next, from_previous)
    long_frames = gather_axis(gather_axis(long_frame, "fx", nx), "fz", nz)
    frames_seen = frame_count + 2
    seen = jnp.concatenate(
        [long_frames.reshape(frame_count, PAD_ROWS, D), short_frame[None], partner[None]]
    ).reshape(frames_seen * PAD_ROWS, D)
    row_ids = jnp.arange(frames_seen * PAD_ROWS, dtype=jnp.int32)
    hidden_key = (row_ids % PAD_ROWS >= FRAME_ROWS) | (
        (row_ids >= (frames_seen - 1) * PAD_ROWS) & ~(with_previous | with_next)
    )
    key_bias = jnp.where(hidden_key, MASK_FLOOR, 0.0).astype(F32)

    gathered = lax.all_gather(master.astype(BF), ALL_AXES, axis=0, tiled=True)
    w_qkv, w_out, w_up, w_down = place_blocks(block_owner, gathered)

    seen_hat, seen_rstd = normalized(seen.astype(F32))
    seen_low = (seen_hat * params_split["gain_one"] + params_split["shift_one"]).astype(BF)

    def own_rows(rows):
        return jnp.concatenate(
            [rows[:PAD_ROWS], rows[frame_count * PAD_ROWS : (frame_count + 1) * PAD_ROWS]]
        )

    own_low = own_rows(seen_low)
    query = (
        jnp.dot(own_low, w_qkv[:, :D], preferred_element_type=F32) + params_split["bias_query"]
    ).astype(BF) * jnp.asarray(1.0 / math.sqrt(HD), BF)
    kv_bias = jnp.concatenate(
        [jnp.zeros_like(params_split["bias_value"]), params_split["bias_value"]]
    )
    key_value = (jnp.dot(seen_low, w_qkv[:, D:], preferred_element_type=F32) + kv_bias).astype(BF)
    attended_low = unpad_frames(attend(query, key_value, key_bias))
    own_inputs = unpad_frames(own_frames.astype(F32))

    mixed_sum = (
        own_inputs
        + jnp.dot(attended_low, w_out, preferred_element_type=F32)
        + params_split["bias_out"]
    )
    normed_two, norm_two_back = jax.vjp(
        layer_norm, mixed_sum, params_split["gain_two"], params_split["shift_two"]
    )
    normed_two_low = normed_two.astype(BF)
    hidden = jnp.dot(normed_two_low, w_up, preferred_element_type=F32) + params_split["bias_up"]
    activated, gelu_back = jax.vjp(gelu_exact, hidden)
    activated_low = activated.astype(BF)
    output_two = (
        mixed_sum
        + jnp.dot(activated_low, w_down, preferred_element_type=F32)
        + params_split["bias_down"]
    )
    normed_three, norm_three_back = jax.vjp(
        layer_norm, output_two, params_split["gain_three"], params_split["shift_three"]
    )
    normed_three_low = normed_three.astype(BF)
    conv_low = params_split["conv_first"].astype(BF).reshape(D, 9 * NT)
    taps = jnp.dot(normed_three_low, conv_low, preferred_element_type=F32).reshape(
        2, GRID, GRID, 9, NT
    )
    first_pre = taps_sum(taps) + params_split["conv_bias"][0]
    learned, tail_back = jax.vjp(
        learner_tail,
        first_pre,
        output_two,
        params_split["conv_second"],
        params_split["conv_third"],
        params_split["conv_fourth"],
        params_split["conv_bias"][1:],
    )
    arriving = cotangent[0].astype(F32).reshape(2, NT, D)
    arriving = jnp.where(swap, arriving[::-1], arriving).reshape(2 * NT, D)
    grad_first, grad_values, grad_second_w, grad_third_w, grad_fourth_w, grad_tail_bias = tail_back(
        arriving
    )
    learned = learned.reshape(2, NT, D)
    learned = jnp.where(swap, learned[::-1], learned).reshape(2 * NT, D)
    grad_first_low = grad_first.astype(BF)
    grad_bias_first = jnp.sum(grad_first_low, axis=(0, 1, 2), dtype=F32)
    grad_taps = taps_back(grad_first_low).reshape(2 * FRAME_ROWS, 9 * NT)
    grad_conv_first = jnp.einsum("nd,nt->dt", normed_three_low, grad_taps, preferred_element_type=F32)
    grad_normed_three = jnp.einsum("nt,dt->nd", grad_taps, conv_low, preferred_element_type=F32)
    grad_output_norm, grad_gain_three, grad_shift_three = norm_three_back(grad_normed_three)
    grad_output_two = grad_values + grad_output_norm
    grad_down_out = grad_output_two.astype(BF)
    grad_bias_down = jnp.sum(grad_down_out, 0, dtype=F32)
    grad_w_down = jnp.einsum(
        "nf,nd->fd", activated_low, grad_down_out, preferred_element_type=F32
    ).astype(BF)
    grad_activated = jnp.einsum("nd,fd->nf", grad_down_out, w_down, preferred_element_type=F32)
    (grad_hidden,) = gelu_back(grad_activated)
    grad_hidden_low = grad_hidden.astype(BF)
    grad_bias_up = jnp.sum(grad_hidden_low, 0, dtype=F32)
    grad_w_up = jnp.einsum(
        "nd,nf->df", normed_two_low, grad_hidden_low, preferred_element_type=F32
    ).astype(BF)
    grad_normed_two = jnp.einsum("nf,df->nd", grad_hidden_low, w_up, preferred_element_type=F32)
    grad_mixed_norm, grad_gain_two, grad_shift_two = norm_two_back(grad_normed_two)
    grad_mixed = grad_output_two + grad_mixed_norm
    grad_branch = grad_mixed.astype(BF)
    grad_bias_out = jnp.sum(grad_branch, 0, dtype=F32)
    grad_w_out = jnp.einsum(
        "nc,nd->cd", attended_low, grad_branch, preferred_element_type=F32
    ).astype(BF)
    grad_attended = jnp.einsum("nd,cd->nc", grad_branch, w_out, preferred_element_type=F32).astype(BF)
    grad_heads = pad_frames(grad_attended).reshape(2 * PAD_ROWS, D)

    grad_query, grad_key, grad_value = attend_back(query, key_value, key_bias, grad_heads)
    grad_bias_query = jnp.sum(grad_query, 0, dtype=F32)
    grad_bias_value = jnp.sum(grad_value, 0, dtype=F32)
    grad_kv = jnp.concatenate([grad_key, grad_value], 1)
    grad_w_qkv = jnp.concatenate(
        [
            jnp.einsum("nd,ne->de", own_low, grad_query, preferred_element_type=F32),
            jnp.einsum("nd,ne->de", seen_low, grad_kv, preferred_element_type=F32),
        ],
        1,
    ).astype(BF)
    grad_seen = jnp.einsum("ne,de->nd", grad_kv, w_qkv[:, D:], preferred_element_type=F32)
    grad_own = jnp.einsum("ne,de->nd", grad_query, w_qkv[:, :D], preferred_element_type=F32)
    own_hat = own_rows(seen_hat)
    grad_gain_one = jnp.sum(grad_seen * seen_hat, 0) + jnp.sum(grad_own * own_hat, 0)
    grad_shift_one = jnp.sum(grad_seen, 0) + jnp.sum(grad_own, 0)

    conv_bias_grad = jnp.concatenate([grad_bias_first[None, :], grad_tail_bias], 0)
    small_local = jnp.concatenate(
        [
            grad_gain_one,
            grad_shift_one,
            grad_gain_two,
            grad_shift_two,
            grad_gain_three,
            grad_shift_three,
            grad_bias_query,
            grad_bias_value,
            grad_bias_out,
            grad_bias_up,
            grad_bias_down,
            grad_conv_first.reshape(-1),
            grad_second_w.reshape(-1),
            grad_third_w.reshape(-1),
            grad_fourth_w.reshape(-1),
            conv_bias_grad.reshape(-1),
        ]
    )

    part_a, part_b = spread_blocks(
        sizes, slots_dev, block_owner, jnp.stack(coords).astype(jnp.int32),
        (grad_w_qkv, grad_w_out, grad_w_up, grad_w_down),
    )
    part_a = reduce_axis(part_a, "core", nc).astype(BF)
    part_b = reduce_axis(part_b, "core", nc).astype(BF)
    part_a = reduce_axis(part_a, "fx", nx).astype(BF)
    part_b = reduce_axis(part_b, "by", ny).astype(BF)
    part_a = reduce_axis(part_a, "by", ny).astype(BF)
    part_b = reduce_axis(part_b, "fx", nx).astype(BF)
    part_a = reduce_axis(part_a, "fz", nz)
    part_b = reduce_axis(part_b, "fz", nz)
    owned_grads = jnp.concatenate([part_a, part_b])

    small_total = small_local.shape[0]
    share = -(-small_total // (device_count * 128)) * 128
    padded_small = jnp.pad(small_local, (0, device_count * share - small_total))
    small_sum = padded_small.reshape(sizes + (share,))
    for axis, size in enumerate(sizes):
        small_sum = rolled(small_sum, axis, size, coords[axis])
    for axis in range(4):
        small_sum = reduce_axis(small_sum, ALL_AXES[axis], sizes[axis])
    squares = jnp.sum(owned_grads * owned_grads) + jnp.sum(small_sum * small_sum)
    carried = jnp.concatenate([small_sum, jnp.full((128,), squares, F32)])
    for axis in reversed(range(4)):
        carried = gather_axis(carried, ALL_AXES[axis], sizes[axis])
    for axis, size in enumerate(sizes):
        carried = rolled(carried, axis, size, size - coords[axis])
    carried = carried.reshape(device_count, share + 128)
    small_grad = carried[:, :share].reshape(-1)[:small_total]
    grad_norm = jnp.sqrt(jnp.sum(carried[:, share]))
    factor = 1.0 / jnp.maximum(grad_norm, CLIP_NORM)

    soap_out = soap(
        owned_grads, factor, master, moment1, moment2, stat_left, stat_right, basis_left, basis_right
    )
    small_first, small_second, small_new = adam_update(
        small_grad * factor, small_params, small_moment1, small_moment2
    )

    seen_frames = grad_seen.astype(BF).reshape(frames_seen, PAD_ROWS, D)
    long_terms = seen_frames[:frame_count].reshape(nz, nx, PAD_ROWS, D)
    long_terms = reduce_axis(long_terms.transpose(1, 0, 2, 3), "fx", nx).astype(BF)
    long_total = reduce_axis(long_terms, "fz", nz)
    partner_term = seen_frames[frame_count + 1]
    nothing = jnp.zeros_like(partner_term)
    to_previous = jnp.where(with_previous, partner_term, nothing)
    to_next = jnp.where(with_next, partner_term, nothing)
    short_total = (
        seen_frames[frame_count].astype(F32)
        + lax.ppermute(to_previous, FRAME_AXES, back_perm).astype(F32)
        + lax.ppermute(to_next, FRAME_AXES, frame_perm).astype(F32)
    )
    grad_normed_one = unpad_frames(jnp.concatenate([long_total, short_total]) + grad_own)
    hat, rstd = unpad_frames(own_hat), unpad_frames(own_rows(jnp.broadcast_to(seen_rstd, seen_hat.shape)))
    scaled = grad_normed_one * params_split["gain_one"]
    grad_inputs = grad_mixed + rstd * (
        scaled
        - jnp.mean(scaled, -1, keepdims=True)
        - hat * jnp.mean(scaled * hat, -1, keepdims=True)
    )
    grad_inputs = grad_inputs.reshape(2, FRAME_ROWS, D)
    grad_inputs = jnp.where(swap, grad_inputs[::-1], grad_inputs).reshape(2 * FRAME_ROWS, D)
    return (
        learned[None],
        grad_inputs[None],
        soap_out[0],
        soap_out[1],
        soap_out[2],
        soap_out[3],
        soap_out[4],
        soap_out[5],
        soap_out[6],
        small_first,
        small_second,
        small_new,
        grad_norm,
    )


def solution(mesh):
    frames, batches = mesh.shape["frame"], mesh.shape["batch"]
    split = Mesh(mesh.devices.reshape(frames // 2, 2, batches // 2, 2), ALL_AXES)
    batch = ("by", "core")
    slots = P(ALL_AXES, None, None)
    rows = P(batch, FRAME_AXES, None)
    return jax.shard_map(
        on_device,
        mesh=split,
        in_specs=(rows, rows, P(batch, None), P(batch, None), P()) + (slots,) * 7 + (P(),) * 3,
        out_specs=(rows, rows) + (slots,) * 7 + (P(),) * 4,
        check_vma=False,
    )
```

```python
import math

import jax
import jax.numpy as jnp
import numpy as np
from jax import lax
from jax.experimental import pallas as pl
from jax.experimental.pallas import tpu as pltpu
from jax.sharding import Mesh
from jax.sharding import PartitionSpec as P

D = 768
HEADS = 12
HD = 64
FF = 3072
GRID = 14
NT = 8
BLOCK_SIDE = 128
STEP = 10
MATRIX_BLOCKS = 432


FULL_PRECISION = lax.Precision.HIGHEST
NORM_EPSILON = 1e-06
BETA_ONE = 0.9
BETA_TWO = 0.95
STAT_DECAY = 0.95
LEARN_RATE = 0.1
WEIGHT_DECAY = 0.01
ADAM_EPSILON = 1e-08
CLIP_NORM = 1.0
MASK_FLOOR = -1e30


def layout():
    return [
        ("gain_one", (D,)),
        ("shift_one", (D,)),
        ("gain_two", (D,)),
        ("shift_two", (D,)),
        ("gain_three", (D,)),
        ("shift_three", (D,)),
        ("bias_query", (D,)),
        ("bias_value", (D,)),
        ("bias_out", (D,)),
        ("bias_up", (FF,)),
        ("bias_down", (D,)),
        ("conv_first", (D, 9, NT)),
        ("conv_second", (9, NT, NT)),
        ("conv_third", (9, NT, NT)),
        ("conv_fourth", (9, NT, NT)),
        ("conv_bias", (4, NT)),
    ]


def unpack(vector):
    params_split = {}
    offset = 0
    for part_name, part_shape in layout():
        entries = math.prod(part_shape)
        params_split[part_name] = vector[offset : offset + entries].reshape(part_shape)
        offset = offset + entries
    return params_split


def matrix_shapes():
    return [(D, 3 * D), (D, D), (D, FF), (FF, D)]


def to_blocks(matrix):
    row_count, col_count = matrix.shape
    tiled = matrix.reshape(row_count // BLOCK_SIDE, BLOCK_SIDE, col_count // BLOCK_SIDE, BLOCK_SIDE)
    return tiled.transpose(0, 2, 1, 3).reshape(-1, BLOCK_SIDE, BLOCK_SIDE)


def from_blocks(blocks):
    matrices = []
    offset = 0
    for row_count, col_count in matrix_shapes():
        tiles = row_count // BLOCK_SIDE * (col_count // BLOCK_SIDE)
        piece_tiles = blocks[offset : offset + tiles].reshape(
            row_count // BLOCK_SIDE, col_count // BLOCK_SIDE, BLOCK_SIDE, BLOCK_SIDE
        )
        matrices.append(piece_tiles.transpose(0, 2, 1, 3).reshape(row_count, col_count))
        offset = offset + tiles
    return matrices


def layer_norm(values, gain_vec, shift_vec):
    centre = jnp.mean(values, -1, keepdims=True)
    centered = values - centre
    spread = jnp.mean(centered * centered, -1, keepdims=True)
    return centered * lax.rsqrt(spread + NORM_EPSILON) * gain_vec + shift_vec


def gelu_exact(values):
    return jax.nn.gelu(values, approximate=False)


def taps_sum(taps):
    padded = jnp.pad(taps, ((0, 0), (1, 1), (1, 1), (0, 0), (0, 0)))
    summed = jnp.zeros(taps.shape[:3] + taps.shape[4:], taps.dtype)
    for tap_index in range(9):
        row_off = tap_index // 3 - 1
        col_off = tap_index % 3 - 1
        summed = (
            summed
            + padded[
                :, 1 + row_off : 1 + row_off + GRID, 1 + col_off : 1 + col_off + GRID, tap_index
            ]
        )
    return summed


def taps_back(grads):
    padded = jnp.pad(grads, ((0, 0), (1, 1), (1, 1), (0, 0)))
    shifted = []
    for tap_index in range(9):
        row_off = tap_index // 3 - 1
        col_off = tap_index % 3 - 1
        shifted.append(
            padded[:, 1 - row_off : 1 - row_off + GRID, 1 - col_off : 1 - col_off + GRID]
        )
    return jnp.stack(shifted, axis=3)


def conv_small(values, weight):
    taps = jnp.einsum("fyxc,tco->fyxto", values, weight, precision=FULL_PRECISION)
    return taps_sum(taps)


def learner_tail(first_pre, values, second_w, third_w, fourth_w, tail_bias):
    frames = first_pre.shape[0]
    act_one = gelu_exact(first_pre)
    act_two = gelu_exact(conv_small(act_one, second_w) + tail_bias[0])
    act_three = gelu_exact(conv_small(act_two, third_w) + tail_bias[1])
    maps = jax.nn.sigmoid(conv_small(act_three, fourth_w) + tail_bias[2])
    grid_values = values.reshape(frames, GRID, GRID, values.shape[-1])
    pooled = jnp.einsum("fyxk,fyxd->fkd", maps, grid_values, precision=FULL_PRECISION)
    return pooled.reshape(frames * NT, values.shape[-1])


def clip_segments(lengths, order_row, group_frames, frames_dev, frame_count):
    clip_ids = jnp.arange(lengths.shape[0], dtype=jnp.int32)
    ordered_len = jnp.sum(
        jnp.where(order_row[:, None] == clip_ids[None, :], lengths[None, :], 0), 1
    )
    ends = jnp.cumsum(ordered_len)
    slots = jnp.arange(group_frames, dtype=jnp.int32)
    places = slots % frames_dev * frame_count + slots // frames_dev
    return jnp.sum((ends[None, :] <= places[:, None]).astype(jnp.int32), 1)


F32=jnp.float32; BF=jnp.bfloat16
NN=(((1,),(0,)),((),()))
NT_=(((1,),(1,)),((),()))
TN=(((0,),(0,)),((),()))

def halves(a):
    high = a.astype(BF)
    return high, (a - high.astype(F32)).astype(BF)

def dot_low(a, b, dims):
    return lax.dot_general(a, b, dims, preferred_element_type=F32)

def dot_parts(a, b, dims):
    ah, al = a
    bh, bl = b
    return dot_low(ah, bh, dims) + (dot_low(ah, bl, dims) + dot_low(al, bh, dims))

def dot_wide(a, b, dims):
    return dot_parts(halves(a), halves(b), dims)

def stat_kernel(sl, sr, bl, br, ol, orr):
    ol[0] = STAT_DECAY * dot_wide(bl[0], sl[0], TN)
    orr[0] = STAT_DECAY * dot_wide(br[0], sr[0], TN)

def slot_spec():
    return pl.BlockSpec((1, BLOCK_SIDE, BLOCK_SIDE), lambda i: (i, 0, 0))

def stat_products(sl, sr, bl, br):
    n = sl.shape[0]
    shape = jax.ShapeDtypeStruct(sl.shape, F32)
    return pl.pallas_call(stat_kernel, grid=(n,), in_specs=[slot_spec()]*4, out_specs=[slot_spec()]*2, out_shape=[shape]*2)(sl, sr, bl, br)

def raw_kernel(g, bl, br, rot, gl, gr, ql, qr):
    gp = halves(g[0]); blp = halves(bl[0]); brp = halves(br[0])
    u = halves(dot_parts(blp, gp, TN))
    v = halves(dot_parts(gp, brp, NN))
    rot[0] = dot_parts(u, brp, NN)
    gl[0] = dot_parts(gp, gp, NT_)
    gr[0] = dot_parts(gp, gp, TN)
    ql[0] = dot_parts(u, gp, NT_)
    qr[0] = dot_parts(v, gp, TN)

def raw_products(ranks, g, bl, br):
    n = g.shape[0]
    shape = jax.ShapeDtypeStruct(g.shape, F32)
    here = pl.BlockSpec((1, BLOCK_SIDE, BLOCK_SIDE), lambda i, ranks: (i, 0, 0))
    ranked = pl.BlockSpec((1, BLOCK_SIDE, BLOCK_SIDE), lambda i, ranks: (ranks[i], 0, 0))

    def kernel(ranks, *refs):
        raw_kernel(*refs)

    return pl.pallas_call(
        kernel,
        grid_spec=pltpu.PrefetchScalarGridSpec(
            num_scalar_prefetch=1, grid=(n,), in_specs=[ranked, here, here], out_specs=[here] * 5
        ),
        out_shape=[shape] * 5,
    )(ranks, g, bl, br)


NB=32
def finish_kernel(factor, rot, gl, gr, ql, qr, pl_, pr_, sl, sr, bl, br, master, m1, m2,
                  o_master, o_m1, o_m2, o_left, o_right, o_bl, o_br, work, elim, mom):
    n = rot.shape[0]
    f = factor[0]
    f2 = (1.0 - STAT_DECAY) * f * f
    for s in range(n):
        r = f * rot[s]
        m = BETA_ONE * m1[s] + (1.0 - BETA_ONE) * r
        v = BETA_TWO * m2[s] + (1.0 - BETA_TWO) * r * r
        mom[s] = m
        o_m2[s] = v
        o_left[s] = STAT_DECAY * sl[s] + f2 * gl[s]
        o_right[s] = STAT_DECAY * sr[s] + f2 * gr[s]
        for side, (p_, q_) in enumerate(((pl_, ql), (pr_, qr))):
            at = p_[s] + f2 * q_[s]
            work[2*s+side, :, 128:] = at
            atp = halves(at)
            work[2*s+side, :, :128] = dot_parts(atp, atp, NT_)
    rows = lax.broadcasted_iota(jnp.int32, (1, 8, 2*NB), 1)
    lanes = lax.broadcasted_iota(jnp.int32, (1, 8, 2*NB), 2)
    count = 2*n

    def panel(p, carry):
        for q in range(128 // NB):
            @pl.when(p == q)
            def _(q=q):
                for t in range(NB // 8):
                    block = work[:, NB*q+8*t:NB*q+8*t+8, NB*q:NB*q+NB]
                    eye = jnp.where(lanes - NB == rows + 8*t, 1.0, 0.0).astype(F32)
                    eye = jnp.broadcast_to(eye, (count, 8, 2*NB))
                    elim[:, 8*t:8*t+8, :] = jnp.concatenate([block, eye[:, :, NB:]], axis=2)
        tiles = [elim[:, 8*t:8*t+8, :] for t in range(NB // 8)]
        for k in range(NB):
            t0, j = divmod(k, 8)
            pivot = tiles[t0][:, j:j+1, k:k+1]
            scale = lax.rsqrt(pivot)
            row = tiles[t0][:, j:j+1, :] * scale
            for t in range(t0, NB // 8):
                col = tiles[t][:, :, k:k+1] * scale
                new = tiles[t] - col * row
                if t == t0:
                    new = jnp.where(rows > j, new, jnp.where(rows == j, row, tiles[t]))
                tiles[t] = new
        for t in range(NB // 8):
            elim[:, 8*t:8*t+8, :] = tiles[t]
        for q in range(128 // NB):
            @pl.when(p == q)
            def _(q=q):
                lo, hi = NB*q, NB*q+NB
                for m in range(count):
                    inv = halves(elim[m, :, NB:])
                    y = dot_parts(inv, halves(work[m, lo:hi, :]), NN)
                    if m % 2 == 0:
                        o_bl[m // 2, lo:hi, :] = y[:, 128:]
                    else:
                        o_br[m // 2, lo:hi, :] = y[:, 128:]
                    if hi < 128:
                        yp = halves(y)
                        up = (yp[0][:, hi:128], yp[1][:, hi:128])
                        work[m, hi:, :] = work[m, hi:, :] - dot_parts(up, yp, TN)
        return carry
    lax.fori_loop(0, 128 // NB, panel, 0)

    for s in range(n):
        m = mom[s]
        v = o_m2[s]
        direction = m / (1.0 - BETA_ONE**STEP) / (jnp.sqrt(v / (1.0 - BETA_TWO**STEP)) + ADAM_EPSILON)
        blp, brp = halves(bl[s]), halves(br[s])
        back = halves(dot_parts(blp, halves(direction), NN))
        returned = dot_parts(back, brp, NT_)
        o_master[s] = master[s] - LEARN_RATE * (returned + WEIGHT_DECAY * master[s])
        qlt, qrt = o_bl[s], o_br[s]
        qltp, qrtp = halves(qlt), halves(qrt)
        turn_l = halves(dot_parts(qltp, blp, NN))
        turn_r = halves(dot_parts(qrtp, brp, NN))
        half = halves(dot_parts(turn_l, halves(m), NN))
        o_m1[s] = dot_parts(half, turn_r, NT_)
        o_bl[s] = qlt.T
        o_br[s] = qrt.T

def finish(factor, rot, gl, gr, ql, qr, pl_, pr_, sl, sr, bl, br, master, m1, m2):
    n = rot.shape[0]
    shape = jax.ShapeDtypeStruct(rot.shape, F32)
    vm = pl.BlockSpec(memory_space=pltpu.VMEM)
    return pl.pallas_call(finish_kernel,
        in_specs=[pl.BlockSpec(memory_space=pltpu.SMEM)] + [vm]*14, out_specs=[vm]*7, out_shape=[shape]*7,
        scratch_shapes=[pltpu.VMEM((2*n,128,256),F32), pltpu.VMEM((2*n,NB,2*NB),F32), pltpu.VMEM((n,128,128),F32)],
        compiler_params=pltpu.CompilerParams(vmem_limit_bytes=56*1024*1024),
    )(factor, rot, gl, gr, ql, qr, pl_, pr_, sl, sr, bl, br, master, m1, m2)

def soap(ranks, g, factor, stat_parts, master, m1, m2, sl, sr, bl, br):
    rot, gl, gr, ql, qr = raw_products(ranks, g, bl, br)
    return finish(factor.reshape(1), rot, gl, gr, ql, qr, *stat_parts, sl, sr, bl, br, master, m1, m2)


def adam_update(clipped, params_old, first_old, second_old):
    first_new = BETA_ONE * first_old + (1.0 - BETA_ONE) * clipped
    second_new = BETA_TWO * second_old + (1.0 - BETA_TWO) * clipped * clipped
    stepped = (
        first_new
        / (1.0 - BETA_ONE**STEP)
        / (jnp.sqrt(second_new / (1.0 - BETA_TWO**STEP)) + ADAM_EPSILON)
    )
    return (first_new, second_new, params_old - LEARN_RATE * stepped)


FRAME_ROWS = GRID * GRID
PAD_ROWS = 208
OWN_ROWS = 2 * PAD_ROWS
LANES = 512
PAIRS = HEADS // 2
PAIR = 2 * HD
QKV_BLOCKS = 108
CODE_BASE = 1 << 16
VMEM_MOST = 58 * 1024 * 1024
ALL_AXES = ("fz", "fx", "by", "core")
FRAME_AXES = ("fz", "fx")
TAP_OFFSETS = [(tap // 3 - 1) * GRID + tap % 3 - 1 for tap in range(9)]


def in_vmem():
    return pl.BlockSpec(memory_space=pltpu.VMEM)


def anywhere():
    return pl.BlockSpec(memory_space=pl.ANY)


def matrix_places():
    places = []
    first = 0
    for row_count, col_count in matrix_shapes():
        cols = col_count // BLOCK_SIDE
        count = row_count // BLOCK_SIDE * cols
        places.append((first, count, cols))
        first = first + count
    return places


def tile_at(ref, row, col):
    row = pl.multiple_of(row * BLOCK_SIDE, BLOCK_SIDE)
    col = pl.multiple_of(col * BLOCK_SIDE, BLOCK_SIDE)
    return ref.at[pl.ds(row, BLOCK_SIDE), pl.ds(col, BLOCK_SIDE)]


def load_matrix(which, codes, buffers, matrix, sem):
    first, count, cols = matrix_places()[which]

    def one_block(tile, carry):
        code = codes[first + tile]
        row, col = lax.div(tile, cols), lax.rem(tile, cols)
        for index, buffer in enumerate(buffers):
            @pl.when(lax.div(code, CODE_BASE) == index)
            def _():
                pltpu.make_async_copy(
                    buffer.at[lax.rem(code, CODE_BASE)], tile_at(matrix, row, col), sem
                ).start()
        return carry

    lax.fori_loop(0, count, one_block, 0)


def wait_whole(ref, sem):
    pltpu.make_async_copy(ref, ref, sem).wait()


def send_tile(code, buffers, tile, sem, first=0):
    for index, buffer in enumerate(buffers):
        @pl.when(lax.div(code, CODE_BASE) == first + index)
        def _():
            pltpu.make_async_copy(tile, buffer.at[lax.rem(code, CODE_BASE)], sem).start()


def normalized(values):
    centered = values - jnp.mean(values, -1, keepdims=True)
    spread = lax.rsqrt(jnp.mean(centered * centered, -1, keepdims=True) + NORM_EPSILON)
    return centered * spread, spread


def norm_back(grad, hat, spread, gain):
    scaled = grad * gain
    return spread * (
        scaled
        - jnp.mean(scaled, -1, keepdims=True)
        - hat * jnp.mean(scaled * hat, -1, keepdims=True)
    )


def project(codes, buffers, seen, rows14):
    rows = seen.shape[0]
    steps = rows // OWN_ROWS
    count = len(buffers)

    def kernel(codes, *refs):
        sources = refs[:count]
        seen, rows14, q, kv, low, own_low, w_qkv, sem = refs[count:]
        step = pl.program_id(0)

        @pl.when(step == 0)
        def _():
            load_matrix(0, codes, sources, w_qkv, sem)

        hat, _ = normalized(seen[...].astype(F32))
        normed = (hat * rows14[0:1] + rows14[1:2]).astype(BF)
        low[...] = normed

        @pl.when(step == 0)
        def _():
            wait_whole(w_qkv, sem)

        kv[:, :D] = dot_low(normed, w_qkv[:, D : 2 * D], NN).astype(BF)
        kv[:, D:] = (dot_low(normed, w_qkv[:, 2 * D :], NN) + rows14[7:8]).astype(BF)

        def own(place):
            part = normed[:PAD_ROWS]
            query = (dot_low(part, w_qkv[:, :D], NN) + rows14[6:7]).astype(BF)
            q[place : place + PAD_ROWS] = query * jnp.asarray(1.0 / math.sqrt(HD), BF)
            own_low[place : place + PAD_ROWS] = part

        @pl.when(step == 0)
        def _():
            own(0)

        @pl.when(step == steps - 1)
        def _():
            own(PAD_ROWS)

    def whole(shape):
        return pl.BlockSpec(shape, lambda i, codes: (0, 0))

    def moving(width):
        return pl.BlockSpec((OWN_ROWS, width), lambda i, codes: (i, 0))

    return pl.pallas_call(
        kernel,
        grid_spec=pltpu.PrefetchScalarGridSpec(
            num_scalar_prefetch=1,
            grid=(steps,),
            in_specs=[anywhere()] * count + [moving(D), whole((14, D))],
            out_specs=[whole((OWN_ROWS, D)), moving(2 * D), moving(D), whole((OWN_ROWS, D)), whole((D, 3 * D))],
            scratch_shapes=[pltpu.SemaphoreType.DMA],
        ),
        out_shape=[
            jax.ShapeDtypeStruct((OWN_ROWS, D), BF),
            jax.ShapeDtypeStruct((rows, 2 * D), BF),
            jax.ShapeDtypeStruct((rows, D), BF),
            jax.ShapeDtypeStruct((OWN_ROWS, D), BF),
            jax.ShapeDtypeStruct((D, 3 * D), BF),
        ],
        compiler_params=pltpu.CompilerParams(vmem_limit_bytes=VMEM_MOST),
    )(codes, *buffers, seen, rows14)


def attend_kernel(long_rows, q, k, v, bias, out):
    lanes = lax.broadcasted_iota(jnp.int32, (1, PAIR), 1)
    first = lanes < HD
    total = k.shape[0]
    for frame, (lo, hi) in enumerate(((0, long_rows), (long_rows, total))):
        rows = slice(frame * PAD_ROWS, (frame + 1) * PAD_ROWS)
        query = q[rows, :]
        keys, values = k[lo:hi, :], v[lo:hi, :]
        results = []
        for side in range(2):
            chosen = jnp.where(first if side == 0 else ~first, query, jnp.zeros_like(query))
            scores = dot_low(chosen, keys, NT_) + bias[:, lo:hi]
            weights = jnp.exp(scores - jnp.max(scores, axis=1, keepdims=True))
            norm = jnp.sum(weights, axis=1, keepdims=True)
            results.append(dot_low(weights.astype(BF), values, NN) / norm)
        out[rows, :] = jnp.where(first, results[0], results[1]).astype(BF)


def attend_back_kernel(long_rows, q, k, v, bias, grad, dq, dk, dv):
    lanes = lax.broadcasted_iota(jnp.int32, (1, PAIR), 1)
    first = lanes < HD
    total = k.shape[0]
    for frame, (lo, hi) in enumerate(((0, long_rows), (long_rows, total))):
        rows = slice(frame * PAD_ROWS, (frame + 1) * PAD_ROWS)
        query, arriving = q[rows, :], grad[rows, :]
        keys, values = k[lo:hi, :], v[lo:hi, :]
        query_parts, key_total, value_total = [], 0.0, 0.0
        for side in range(2):
            mask = first if side == 0 else ~first
            chosen = jnp.where(mask, query, jnp.zeros_like(query))
            incoming = jnp.where(mask, arriving, jnp.zeros_like(arriving))
            scores = dot_low(keys, chosen, NT_) + bias[lo:hi, :]
            weights = jnp.exp(scores - jnp.max(scores, axis=0, keepdims=True))
            soft = weights * (1.0 / jnp.sum(weights, axis=0, keepdims=True))
            grad_soft = dot_low(values, incoming, NT_)
            delta = jnp.sum(soft * grad_soft, axis=0, keepdims=True)
            grad_scores = (soft * (grad_soft - delta)).astype(BF)
            key_total = key_total + dot_low(grad_scores, chosen, NN)
            value_total = value_total + dot_low(soft.astype(BF), incoming, NN)
            query_parts.append(dot_low(grad_scores, keys, TN))
        dq[rows, :] = (jnp.where(first, query_parts[0], query_parts[1]) * (1.0 / math.sqrt(HD))).astype(BF)
        dk[lo:hi, :] = key_total.astype(BF)
        dv[lo:hi, :] = value_total.astype(BF)


def pair_spec(rows, offset=0):
    return pl.BlockSpec((rows, PAIR), lambda i: (0, i + offset))


def attend(q, kv, bias):
    keys_total = kv.shape[0]
    long_rows = keys_total - OWN_ROWS

    def kernel(*refs):
        attend_kernel(long_rows, *refs)

    return pl.pallas_call(
        kernel,
        grid=(PAIRS,),
        in_specs=[
            pair_spec(OWN_ROWS),
            pair_spec(keys_total),
            pair_spec(keys_total, PAIRS),
            pl.BlockSpec((1, keys_total), lambda i: (0, 0)),
        ],
        out_specs=pair_spec(OWN_ROWS),
        out_shape=jax.ShapeDtypeStruct((OWN_ROWS, D), BF),
        compiler_params=pltpu.CompilerParams(vmem_limit_bytes=48 * 1024 * 1024),
    )(q, kv, kv, bias.reshape(1, -1))


def attend_back(q, kv, bias, grad):
    keys_total = kv.shape[0]
    long_rows = keys_total - OWN_ROWS

    def kernel(*refs):
        attend_back_kernel(long_rows, *refs)

    return pl.pallas_call(
        kernel,
        grid=(PAIRS,),
        in_specs=[
            pair_spec(OWN_ROWS),
            pair_spec(keys_total),
            pair_spec(keys_total, PAIRS),
            pl.BlockSpec((keys_total, 1), lambda i: (0, 0)),
            pair_spec(OWN_ROWS),
        ],
        out_specs=[pair_spec(OWN_ROWS), pair_spec(keys_total), pair_spec(keys_total)],
        out_shape=[
            jax.ShapeDtypeStruct((OWN_ROWS, D), BF),
            jax.ShapeDtypeStruct((keys_total, D), BF),
            jax.ShapeDtypeStruct((keys_total, D), BF),
        ],
        compiler_params=pltpu.CompilerParams(vmem_limit_bytes=48 * 1024 * 1024),
    )(q, kv, kv, bias.reshape(-1, 1), grad)


def lane_masks():
    lane = np.arange(LANES)
    inner = lane % PAD_ROWS
    token = (lane < OWN_ROWS) & (inner < FRAME_ROWS)
    row, col = inner // GRID, inner % GRID
    masks = []
    for tap in range(9):
        far_row, far_col = row + tap // 3 - 1, col + tap % 3 - 1
        masks.append(token & (far_row >= 0) & (far_row < GRID) & (far_col >= 0) & (far_col < GRID))
    masks.append(token & (lane < PAD_ROWS))
    masks.append(token & (lane >= PAD_ROWS))
    masks = masks + [np.zeros(LANES, bool)] * (16 - len(masks))
    return np.stack(masks).astype(np.float32)


def ahead(values, offset):
    return values if offset == 0 else pltpu.roll(values, (-offset) % LANES, axis=1)


def cumulative(values):
    return 0.5 + 0.5 * lax.erf(values * math.sqrt(0.5))


def gelu_slope(values, portion):
    return portion + values * jnp.exp(-0.5 * values * values) * (1.0 / math.sqrt(2.0 * math.pi))


def column_sum(values):
    return jnp.sum(values, axis=0, keepdims=True)


def widened(values):
    return jnp.concatenate([values, jnp.zeros((values.shape[0], LANES - OWN_ROWS), values.dtype)], axis=1)


def middle_kernel(weight_count, codes, targets, *refs):
    sources = refs[:weight_count]
    (
        att, own, cot, rows14, conv_t, taps_forward, taps_backward, tail_bias, masks, blank,
        learned, grad_mixed, grad_att, vectors, grad_up_bias, grad_conv, grad_tail, grad_tail_bias,
    ) = refs[weight_count : weight_count + 18]
    buffers = refs[weight_count + 18 : -14]
    (
        w_out, w_up, w_down, d_out, d_up, d_down, activated, slopes, normed, hat_two, mixed, gathered_sum,
        load_sems, send_sems,
    ) = refs[-14:]
    chunks = FF // D
    load_matrix(1, codes, sources, w_out, load_sems.at[0])
    load_matrix(2, codes, sources, w_up, load_sems.at[1])
    load_matrix(3, codes, sources, w_down, load_sems.at[2])

    def one_blank(block, total):
        code = targets[block]
        early = lax.div(code, CODE_BASE) < 4
        filled = (block >= MATRIX_BLOCKS) | ((block < QKV_BLOCKS) & early)

        @pl.when(filled)
        def _():
            send_tile(code, buffers, blank, send_sems.at[3])

        return total + filled.astype(jnp.int32)

    blanks = lax.fori_loop(0, QKV_BLOCKS, one_blank, jnp.int32(0))
    blanks = lax.fori_loop(MATRIX_BLOCKS, targets.shape[0], one_blank, blanks)

    wait_whole(w_out, load_sems.at[0])
    start = own[...].astype(F32) + dot_low(att[...], w_out[...], NN) + rows14[8:9]
    mixed[...] = start
    hat, spread_two = normalized(start)
    hat_two[...] = hat
    normed[...] = (hat * rows14[2:3] + rows14[3:4]).astype(BF)
    gathered_sum[...] = start + rows14[13:14]
    wait_whole(w_up, load_sems.at[1])
    wait_whole(w_down, load_sems.at[2])

    for chunk in range(chunks):
        at = slice(chunk * D, (chunk + 1) * D)
        hidden = dot_low(normed[...], w_up[:, at], NN) + rows14[9 + chunk : 10 + chunk]
        portion = cumulative(hidden)
        active = (hidden * portion).astype(BF)
        activated[chunk] = active
        slopes[chunk] = gelu_slope(hidden, portion)
        gathered_sum[...] += dot_low(active, w_down[at, :], NN)

    out_two = gathered_sum[...]
    hat, spread_three = normalized(out_two)
    low_three = (hat * rows14[4:5] + rows14[5:6]).astype(BF)

    taps = widened(dot_low(conv_t[...], low_three, NT_))
    first = tail_bias[:, 0:1]
    for tap in range(9):
        first = first + ahead(taps[NT * tap : NT * (tap + 1)], TAP_OFFSETS[tap]) * masks[tap : tap + 1]

    def around(values, sign):
        order = range(9) if sign > 0 else range(8, -1, -1)
        return jnp.concatenate(
            [
                ahead(values, sign * TAP_OFFSETS[tap]) * masks[seen : seen + 1]
                for tap, seen in zip(range(9), order)
            ],
            axis=0,
        )

    before, stacks, portions = [first], [], []
    for layer in range(3):
        portions.append(cumulative(before[-1]))
        stacks.append(around(before[-1] * portions[-1], 1))
        before.append(dot_wide(taps_forward[layer], stacks[-1], NN) + tail_bias[:, layer + 1 : layer + 2])
    maps = 1.0 / (1.0 + jnp.exp(-before[3]))
    both = jnp.concatenate([maps * masks[9:10], maps * masks[10:11]], axis=0)[:, :OWN_ROWS]
    both = halves(both)
    out_parts = halves(out_two)
    arriving = cot[...]
    learned[...] = dot_parts(both, out_parts, NN)
    seen_maps = widened(dot_low(arriving, out_parts[0], NT_) + dot_low(arriving, out_parts[1], NT_))
    grad = (seen_maps[:NT] * masks[9:10] + seen_maps[NT:] * masks[10:11]) * maps * (1.0 - maps)
    sums = [None] * 4
    for layer in (2, 1, 0):
        sums[layer + 1] = jnp.sum(grad, axis=1, keepdims=True)
        grad_tail[layer] = dot_wide(stacks[layer], grad, NT_)
        grad = dot_wide(taps_backward[layer], around(grad, -1), NN)
        grad = grad * gelu_slope(before[layer], portions[layer])
    grad = grad.astype(BF).astype(F32)
    sums[0] = jnp.sum(grad, axis=1, keepdims=True)
    grad_tail_bias[...] = jnp.concatenate(sums, axis=1)
    grad_taps = around(grad, -1)[:, :OWN_ROWS].astype(BF)
    grad_conv[...] = dot_low(grad_taps, low_three, NN)
    grad_norm_three = dot_low(grad_taps, conv_t[...], TN)
    vectors[2:3] = column_sum(grad_norm_three * hat)
    vectors[3:4] = column_sum(grad_norm_three)
    grad_out = (
        norm_back(grad_norm_three, hat, spread_three, rows14[4:5])
        + dot_low(both[0], arriving, TN)
        + dot_low(both[1], arriving, TN)
    )
    grad_down = grad_out.astype(BF)
    vectors[5:6] = column_sum(grad_down.astype(F32))

    for chunk in range(chunks):
        at = slice(chunk * D, (chunk + 1) * D)
        grad_active = dot_low(grad_down, w_down[at, :], NT_)
        grad_hidden = (grad_active * slopes[chunk]).astype(BF)
        grad_up_bias[chunk : chunk + 1] = column_sum(grad_hidden.astype(F32))
        part = dot_low(grad_hidden, w_up[:, at], NT_)
        if chunk == 0:
            gathered_sum[...] = part
        else:
            gathered_sum[...] += part
        d_down[at, :] = dot_low(activated[chunk], grad_down, TN).astype(BF)
        d_up[:, at] = dot_low(normed[...], grad_hidden, TN).astype(BF)
        side = D // BLOCK_SIDE

        def one_tile(tile, carry, chunk=chunk):
            row, col = lax.div(tile, side), lax.rem(tile, side)
            first_up, first_down = matrix_places()[2][0], matrix_places()[3][0]
            up_block = first_up + row * (FF // BLOCK_SIDE) + chunk * side + col
            send_tile(targets[up_block], buffers, tile_at(d_up, row, chunk * side + col), send_sems.at[1])
            down_block = first_down + (chunk * side + row) * side + col
            send_tile(targets[down_block], buffers, tile_at(d_down, chunk * side + row, col), send_sems.at[2])
            return carry

        lax.fori_loop(0, side * side, one_tile, 0)

    grad_norm_two = gathered_sum[...]
    vectors[0:1] = column_sum(grad_norm_two * hat_two[...])
    vectors[1:2] = column_sum(grad_norm_two)
    total = grad_out + norm_back(grad_norm_two, hat_two[...], spread_two, rows14[2:3])
    grad_mixed[...] = total
    branch = total.astype(BF)
    vectors[4:5] = column_sum(branch.astype(F32))
    d_out[...] = dot_low(att[...], branch, TN).astype(BF)

    def one_out(tile, carry):
        side = D // BLOCK_SIDE
        code = targets[matrix_places()[1][0] + tile]
        send_tile(code, buffers, tile_at(d_out, lax.div(tile, side), lax.rem(tile, side)), send_sems.at[0])
        return carry

    lax.fori_loop(0, matrix_places()[1][1], one_out, 0)
    grad_att[...] = dot_low(branch, w_out[...], NT_).astype(BF)
    wait_whole(d_out, send_sems.at[0])
    wait_whole(d_up, send_sems.at[1])
    wait_whole(d_down, send_sems.at[2])

    def one_wait(index, carry):
        wait_whole(blank, send_sems.at[3])
        return carry

    lax.fori_loop(0, blanks, one_wait, 0)


def middle(codes, targets, weights, buffer_shapes, att, own, cot, rows14, conv_t, taps_forward, taps_backward, tail_bias):
    count = len(weights)

    def kernel(*refs):
        middle_kernel(count, *refs)

    def f32(*shape):
        return jax.ShapeDtypeStruct(shape, F32)

    outs = [
        f32(2 * NT, D), f32(OWN_ROWS, D), jax.ShapeDtypeStruct((OWN_ROWS, D), BF), f32(8, D),
        f32(FF // D, D), f32(9 * NT, D), f32(3, 9 * NT, NT), f32(NT, 4),
    ]
    results = pl.pallas_call(
        kernel,
        grid_spec=pltpu.PrefetchScalarGridSpec(
            num_scalar_prefetch=2,
            grid=(1,),
            in_specs=[anywhere()] * count + [in_vmem()] * 10,
            out_specs=[in_vmem()] * len(outs) + [anywhere()] * len(buffer_shapes),
            scratch_shapes=[
                pltpu.VMEM((D, D), BF),
                pltpu.VMEM((D, FF), BF),
                pltpu.VMEM((FF, D), BF),
                pltpu.VMEM((D, D), BF),
                pltpu.VMEM((D, FF), BF),
                pltpu.VMEM((FF, D), BF),
                pltpu.VMEM((FF // D, OWN_ROWS, D), BF),
                pltpu.VMEM((FF // D, OWN_ROWS, D), F32),
                pltpu.VMEM((OWN_ROWS, D), BF),
                pltpu.VMEM((OWN_ROWS, D), F32),
                pltpu.VMEM((OWN_ROWS, D), F32),
                pltpu.VMEM((OWN_ROWS, D), F32),
                pltpu.SemaphoreType.DMA((3,)),
                pltpu.SemaphoreType.DMA((4,)),
            ],
        ),
        out_shape=outs + buffer_shapes,
        compiler_params=pltpu.CompilerParams(vmem_limit_bytes=VMEM_MOST),
    )(
        codes, targets, *weights, att, own, cot, rows14, conv_t, taps_forward, taps_backward, tail_bias,
        jnp.asarray(lane_masks()), jnp.zeros((BLOCK_SIDE, BLOCK_SIDE), BF),
    )
    return results[: len(outs)], results[len(outs) :]


def qkv_grads(targets, low, own_low, dq, dk, dv, buffers, late):
    steps = low.shape[0] // OWN_ROWS
    count = len(buffers)

    def kernel(targets, low, own_low, dq, dk, dv, *refs):
        filled = refs[count : 2 * count]
        matrix = refs[2 * count]
        totals, sem = refs[2 * count + 1 :]
        step = pl.program_id(0)

        @pl.when(step == 0)
        def _():
            totals[...] = jnp.zeros_like(totals)
            matrix[:, :D] = dot_low(own_low[...], dq[...], TN).astype(BF)

        totals[:, :D] += dot_low(low[...], dk[...], TN)
        totals[:, D:] += dot_low(low[...], dv[...], TN)

        @pl.when(step == steps - 1)
        def _():
            matrix[:, D:] = totals[...].astype(BF)
            cols = 3 * D // BLOCK_SIDE

            def one_tile(tile, sent):
                code = targets[tile]
                send_tile(code, filled, tile_at(matrix, lax.div(tile, cols), lax.rem(tile, cols)), sem, late)
                return sent + (lax.div(code, CODE_BASE) >= late).astype(jnp.int32)

            sent = lax.fori_loop(0, QKV_BLOCKS, one_tile, jnp.int32(0))

            def one_wait(index, carry):
                wait_whole(tile_at(matrix, 0, 0), sem)
                return carry

            lax.fori_loop(0, sent, one_wait, 0)

    def whole(shape):
        return pl.BlockSpec(shape, lambda i, targets: (0, 0))

    def moving(width):
        return pl.BlockSpec((OWN_ROWS, width), lambda i, targets: (i, 0))

    results = pl.pallas_call(
        kernel,
        grid_spec=pltpu.PrefetchScalarGridSpec(
            num_scalar_prefetch=1,
            grid=(steps,),
            in_specs=[moving(D), whole((OWN_ROWS, D)), whole((OWN_ROWS, D)), moving(D), moving(D)]
            + [anywhere()] * count,
            out_specs=[anywhere()] * count + [whole((D, 3 * D))],
            scratch_shapes=[pltpu.VMEM((D, 2 * D), F32), pltpu.SemaphoreType.DMA],
        ),
        out_shape=[jax.ShapeDtypeStruct(b.shape, b.dtype) for b in buffers]
        + [jax.ShapeDtypeStruct((D, 3 * D), BF)],
        input_output_aliases={6 + i: i for i in range(count)},
        compiler_params=pltpu.CompilerParams(vmem_limit_bytes=VMEM_MOST),
    )(targets, low, own_low, dq, dk, dv, *buffers)
    return results[:count], results[count]


def input_grads(seen, own, dq, dk, dv, w_qkv):
    rows = seen.shape[0]
    steps = rows // OWN_ROWS

    def kernel(seen, own, dq, dk, dv, w_qkv, grad_seen, grad_own, sums):
        step = pl.program_id(0)

        @pl.when(step == 0)
        def _():
            grad = dot_low(dq[...], w_qkv[:, :D], NT_)
            grad_own[...] = grad
            hat, _ = normalized(own[...].astype(F32))
            sums[...] = jnp.zeros_like(sums)
            sums[0:1] = column_sum(grad * hat)
            sums[1:2] = column_sum(grad)
            sums[2:3] = column_sum(dq[...].astype(F32))

        grad = dot_low(dk[...], w_qkv[:, D : 2 * D], NT_) + dot_low(dv[...], w_qkv[:, 2 * D :], NT_)
        grad_seen[...] = grad.astype(BF)
        hat, _ = normalized(seen[...].astype(F32))
        sums[0:1] += column_sum(grad * hat)
        sums[1:2] += column_sum(grad)
        sums[3:4] += column_sum(dv[...].astype(F32))

    def whole(shape):
        return pl.BlockSpec(shape, lambda i: (0, 0))

    moving = pl.BlockSpec((OWN_ROWS, D), lambda i: (i, 0))
    return pl.pallas_call(
        kernel,
        grid=(steps,),
        in_specs=[moving, whole((OWN_ROWS, D)), whole((OWN_ROWS, D)), moving, moving, whole((D, 3 * D))],
        out_specs=[moving, whole((OWN_ROWS, D)), whole((8, D))],
        out_shape=[
            jax.ShapeDtypeStruct((rows, D), BF),
            jax.ShapeDtypeStruct((OWN_ROWS, D), F32),
            jax.ShapeDtypeStruct((8, D), F32),
        ],
        compiler_params=pltpu.CompilerParams(vmem_limit_bytes=VMEM_MOST),
    )(seen, own, dq, dk, dv, w_qkv)


def moved(value, axis, size, step):
    return lax.ppermute(value, axis, [(i, (i + step) % size) for i in range(size)])


def reduce_axis(terms, axis, size):
    total = terms[0].astype(F32)
    for step in range(1, size):
        total = total + moved(terms[step], axis, size, step).astype(F32)
    return total


def gather_axis(value, axis, size):
    return jnp.stack([value] + [moved(value, axis, size, -step) for step in range(1, size)])


def rolled(value, axis, size, step):
    return lax.dynamic_slice_in_dim(jnp.concatenate([value, value], axis), step, size, axis)


def slot_chunks(slots_dev):
    early = slots_dev * 3 // 14
    late = slots_dev - 2 * early
    chunks = []
    first = 0
    for index, count in enumerate((early, early, late - late // 2, late // 2)):
        chunks.append((first, count, ("fx", "by", "fz") if index % 2 == 0 else ("by", "fx", "fz")))
        first = first + count
    return chunks


def send_table(block_owner, sizes, coords, slots_dev):
    nz, nx, ny, nc = sizes
    slots = jnp.arange(block_owner.shape[0], dtype=jnp.int32)
    device = slots // slots_dev
    place = {}
    for axis in range(3, -1, -1):
        place[ALL_AXES[axis]] = (device % sizes[axis] - coords[axis] + sizes[axis]) % sizes[axis]
        device = device // sizes[axis]
    is_late = (block_owner < QKV_BLOCKS).astype(jnp.int32).reshape(-1, slots_dev)
    late_before = jnp.cumsum(is_late, 1) - is_late
    early_before = jnp.arange(slots_dev, dtype=jnp.int32)[None] - late_before
    late_count = jnp.sum(is_late, 1, keepdims=True)
    ranks = jnp.where(is_late == 1, slots_dev - late_count + late_before, early_before)
    rank = ranks.reshape(-1)
    size_of = dict(zip(ALL_AXES, sizes))
    code = jnp.zeros_like(slots)
    for index, (first, count, axes) in enumerate(slot_chunks(slots_dev)):
        at = jnp.zeros_like(slots)
        for name in axes:
            at = at * size_of[name] + place[name]
        at = at * count + rank - first
        inside = (rank >= first) & (rank < first + count)
        code = jnp.where(inside, (2 * index + place["core"]) * CODE_BASE + at, code)
    owned = block_owner[:, None] == slots[None, :]
    table = jnp.sum(jnp.where(owned, code[:, None], 0), 0)
    return table, ranks, jnp.max(late_count)


def reduce_chunk(kept, sent, count, axes, sizes):
    size_of = dict(zip(ALL_AXES, sizes))
    total = kept.astype(F32) + moved(sent, "core", 2, 1).astype(F32)
    total = total.astype(BF).reshape([size_of[name] for name in axes] + [count, BLOCK_SIDE, BLOCK_SIDE])
    for name in axes:
        total = reduce_axis(total, name, size_of[name])
        if name != axes[-1]:
            total = total.astype(BF)
    return total


def spread_early(targets, matrix, buffer_shapes):
    count = len(buffer_shapes)

    def kernel(targets, matrix, blank, *refs):
        buffers, sem = refs[:count], refs[count]

        def one_block(block, sent):
            code = targets[block]
            cols = 3 * D // BLOCK_SIDE
            early = lax.div(code, CODE_BASE) < count

            @pl.when(early & (block < QKV_BLOCKS))
            def _():
                tile = tile_at(matrix, lax.div(block, cols), lax.rem(block, cols))
                send_tile(code, buffers, tile, sem)

            @pl.when(early & (block >= QKV_BLOCKS))
            def _():
                send_tile(code, buffers, blank, sem)

            return sent + early.astype(jnp.int32)

        sent = lax.fori_loop(0, targets.shape[0], one_block, jnp.int32(0))

        def one_wait(index, carry):
            wait_whole(blank, sem)
            return carry

        lax.fori_loop(0, sent, one_wait, 0)

    return pl.pallas_call(
        kernel,
        grid_spec=pltpu.PrefetchScalarGridSpec(
            num_scalar_prefetch=1,
            grid=(1,),
            in_specs=[in_vmem()] * 2,
            out_specs=[anywhere()] * count,
            scratch_shapes=[pltpu.SemaphoreType.DMA],
        ),
        out_shape=buffer_shapes,
        compiler_params=pltpu.CompilerParams(vmem_limit_bytes=VMEM_MOST),
    )(targets, matrix, jnp.zeros((BLOCK_SIDE, BLOCK_SIDE), BF))


def pad_frames(values):
    frames = values.reshape(2, FRAME_ROWS, values.shape[-1])
    return jnp.pad(frames, ((0, 0), (0, PAD_ROWS - FRAME_ROWS), (0, 0)))


def on_device(
    tokens,
    cotangent,
    clip_lengths,
    clip_order,
    block_owner,
    master,
    moment1,
    moment2,
    stat_left,
    stat_right,
    basis_left,
    basis_right,
    small_params,
    small_moment1,
    small_moment2,
):
    sizes = tuple(lax.axis_size(name) for name in ALL_AXES)
    coords = [lax.axis_index(name) for name in ALL_AXES]
    nz, nx, ny, nc = sizes
    device_count = nz * nx * ny * nc
    frame_count = nz * nx
    frame_index = coords[0] * nx + coords[1]
    slots_dev = master.shape[0]

    segment_slots = clip_segments(
        clip_lengths[0], clip_order[0], 2 * frame_count, 2, frame_count
    ).reshape(frame_count, 2)
    ordered_len = clip_lengths[0][clip_order[0]]
    longest = jnp.argmax(ordered_len).astype(jnp.int32)
    second_long = segment_slots[:, 1] == longest
    short_segment = jnp.where(second_long, segment_slots[:, 0], segment_slots[:, 1])
    swap = second_long[frame_index]
    padded_segment = jnp.pad(short_segment, (1, 1), constant_values=-1)
    near = lax.dynamic_slice_in_dim(padded_segment, frame_index, 3)
    with_previous = near[0] == near[1]
    with_next = near[2] == near[1]

    own_frames = pad_frames(tokens[0])
    own_frames = jnp.where(swap, own_frames[::-1], own_frames)
    long_frame, short_frame = own_frames[0], own_frames[1]
    frame_perm = [(i, (i + 1) % frame_count) for i in range(frame_count)]
    back_perm = [(j, i) for i, j in frame_perm]
    from_previous = lax.ppermute(short_frame, FRAME_AXES, frame_perm)
    from_next = lax.ppermute(short_frame, FRAME_AXES, back_perm)
    partner = jnp.where(with_next, from_next, from_previous)
    long_frames = gather_axis(gather_axis(long_frame, "fz", nz), "fx", nx)
    frames_seen = frame_count + 2
    seen = jnp.concatenate(
        [long_frames.reshape(frame_count, PAD_ROWS, D), short_frame[None], partner[None]]
    ).reshape(frames_seen * PAD_ROWS, D)
    own = own_frames.reshape(OWN_ROWS, D)
    row_ids = jnp.arange(frames_seen * PAD_ROWS, dtype=jnp.int32)
    hidden_key = (row_ids % PAD_ROWS >= FRAME_ROWS) | (
        (row_ids >= (frames_seen - 1) * PAD_ROWS) & ~(with_previous | with_next)
    )
    key_bias = jnp.where(hidden_key, MASK_FLOOR, 0.0).astype(F32)

    slot_ids = jnp.arange(block_owner.shape[0], dtype=jnp.int32)
    weight_codes = jnp.sum(jnp.where(block_owner[:, None] == slot_ids[None, :], slot_ids[:, None], 0), 0)
    targets, ranks, late_most = send_table(block_owner, sizes, coords, slots_dev)
    device_index = ((coords[0] * nx + coords[1]) * ny + coords[2]) * nc + coords[3]
    own_ranks = lax.dynamic_index_in_dim(ranks, device_index, 0, keepdims=False)
    chunks = slot_chunks(slots_dev)

    split = unpack(small_params)
    rows14 = small_params[: 14 * D].reshape(14, D)
    conv_t = split["conv_first"].astype(BF).reshape(D, 9 * NT).T
    tail = jnp.stack([split["conv_second"], split["conv_third"], split["conv_fourth"]])
    taps_forward = tail.transpose(0, 3, 1, 2).reshape(3, NT, 9 * NT)
    taps_backward = tail.transpose(0, 2, 1, 3).reshape(3, NT, 9 * NT)
    tail_bias = split["conv_bias"].T
    arriving = cotangent[0].reshape(2, NT, D)
    arriving = jnp.where(swap, arriving[::-1], arriving).reshape(2 * NT, D)

    gathered = lax.all_gather(master.astype(BF), ALL_AXES, axis=0, tiled=True)
    stat_parts = stat_products(stat_left, stat_right, basis_left, basis_right)

    query, key_value, low, own_low, w_qkv = project(weight_codes, [gathered], seen, rows14)
    attended = attend(query, key_value, key_bias)
    buffer_shapes = []
    for first, count, axes in chunks:
        shape = jax.ShapeDtypeStruct((device_count // nc * max(count, 1), BLOCK_SIDE, BLOCK_SIDE), BF)
        buffer_shapes = buffer_shapes + [shape, shape]
    (learned, grad_mixed, grad_att, vectors, grad_up_bias, grad_conv, grad_tail, grad_tail_bias), buffers = middle(
        weight_codes, targets, [gathered], buffer_shapes, attended, own, arriving, rows14, conv_t,
        taps_forward, taps_backward, tail_bias,
    )
    learned = learned.reshape(2, NT, D)
    learned = jnp.where(swap, learned[::-1], learned).reshape(2 * NT, D)

    reduced = []
    for index in range(2):
        first, count, axes = chunks[index]
        if count:
            reduced.append(reduce_chunk(buffers[2 * index], buffers[2 * index + 1], count, axes, sizes))

    grad_query, grad_key, grad_value = attend_back(query, key_value, key_bias, grad_att)
    late_buffers, grad_w_qkv = qkv_grads(
        targets, low, own_low, grad_query, grad_key, grad_value, list(buffers[4:]), 4
    )
    grad_seen, grad_own, sums = input_grads(seen, own, grad_query, grad_key, grad_value, w_qkv)

    if reduced:
        def whole_early(early):
            shapes = buffer_shapes[:4]
            extra = spread_early(targets, grad_w_qkv, shapes)
            return [
                part + reduce_chunk(extra[2 * i], extra[2 * i + 1], chunks[i][1], chunks[i][2], sizes)
                for i, part in enumerate(early)
            ]

        late_room = chunks[2][1] + chunks[3][1]
        reduced = lax.cond(late_most <= late_room, lambda early: early, whole_early, reduced)
    for index in (2, 3):
        first, count, axes = chunks[index]
        reduced.append(reduce_chunk(late_buffers[2 * index - 4], late_buffers[2 * index - 3], count, axes, sizes))
    owned_grads = jnp.concatenate(reduced)

    small_local = jnp.concatenate(
        [
            sums[:2].reshape(-1),
            vectors[:4].reshape(-1),
            sums[2:4].reshape(-1),
            vectors[4],
            grad_up_bias.reshape(-1),
            vectors[5],
            grad_conv.T.reshape(-1),
            grad_tail.reshape(-1),
            grad_tail_bias.T.reshape(-1),
        ]
    )
    small_total = small_local.shape[0]
    share = -(-small_total // (device_count * 128)) * 128
    padded_small = jnp.pad(small_local, (0, device_count * share - small_total))
    small_sum = padded_small.reshape(sizes + (share,))
    for axis, size in enumerate(sizes):
        small_sum = rolled(small_sum, axis, size, coords[axis])
    for axis in range(4):
        small_sum = reduce_axis(small_sum, ALL_AXES[axis], sizes[axis])
    squares = jnp.sum(owned_grads * owned_grads) + jnp.sum(small_sum * small_sum)
    carried = jnp.concatenate([small_sum, jnp.full((128,), squares, F32)])
    for axis in reversed(range(4)):
        carried = gather_axis(carried, ALL_AXES[axis], sizes[axis])
    for axis, size in enumerate(sizes):
        carried = rolled(carried, axis, size, size - coords[axis])
    carried = carried.reshape(device_count, share + 128)
    small_grad = carried[:, :share].reshape(-1)[:small_total]
    grad_norm = jnp.sqrt(jnp.sum(carried[:, share]))
    factor = 1.0 / jnp.maximum(grad_norm, CLIP_NORM)

    soap_out = soap(
        own_ranks, owned_grads, factor, stat_parts, master, moment1, moment2, stat_left, stat_right,
        basis_left, basis_right,
    )
    small_first, small_second, small_new = adam_update(
        small_grad * factor, small_params, small_moment1, small_moment2
    )

    grad_seen, _ = lax.optimization_barrier((grad_seen, owned_grads))
    seen_frames = grad_seen.reshape(frames_seen, PAD_ROWS, D)
    long_terms = seen_frames[:frame_count].reshape(nx, nz, PAD_ROWS, D)
    long_terms = reduce_axis(long_terms, "fx", nx).astype(BF)
    long_total = reduce_axis(long_terms, "fz", nz)
    partner_term = seen_frames[frame_count + 1]
    nothing = jnp.zeros_like(partner_term)
    to_previous = jnp.where(with_previous, partner_term, nothing)
    to_next = jnp.where(with_next, partner_term, nothing)
    short_total = (
        seen_frames[frame_count].astype(F32)
        + lax.ppermute(to_previous, FRAME_AXES, back_perm).astype(F32)
        + lax.ppermute(to_next, FRAME_AXES, frame_perm).astype(F32)
    )
    grad_normed_one = jnp.concatenate([long_total, short_total]) + grad_own
    hat, spread = normalized(own.astype(F32))
    grad_inputs = grad_mixed + norm_back(grad_normed_one, hat, spread, rows14[0:1])
    grad_inputs = grad_inputs.reshape(2, PAD_ROWS, D)[:, :FRAME_ROWS]
    grad_inputs = jnp.where(swap, grad_inputs[::-1], grad_inputs).reshape(2 * FRAME_ROWS, D)
    return (
        learned[None],
        grad_inputs[None],
        soap_out[0],
        soap_out[1],
        soap_out[2],
        soap_out[3],
        soap_out[4],
        soap_out[5],
        soap_out[6],
        small_first,
        small_second,
        small_new,
        grad_norm,
    )


def solution(mesh):
    frames, batches = mesh.shape["frame"], mesh.shape["batch"]
    split = Mesh(mesh.devices.reshape(frames // 2, 2, batches // 2, 2), ALL_AXES)
    batch = ("by", "core")
    slots = P(ALL_AXES, None, None)
    rows = P(batch, FRAME_AXES, None)
    return jax.shard_map(
        on_device,
        mesh=split,
        in_specs=(rows, rows, P(batch, None), P(batch, None), P()) + (slots,) * 7 + (P(),) * 3,
        out_specs=(rows, rows) + (slots,) * 7 + (P(),) * 4,
        check_vma=False,
    )
```

```python
import math

import jax
import jax.numpy as jnp
import numpy as np
from jax import lax
from jax.experimental import pallas as pl
from jax.experimental.pallas import tpu as pltpu
from jax.sharding import Mesh
from jax.sharding import PartitionSpec as P

D = 768
HEADS = 12
HD = 64
FF = 3072
GRID = 14
NT = 8
BLOCK_SIDE = 128
STEP = 10
MATRIX_BLOCKS = 432


FULL_PRECISION = lax.Precision.HIGHEST
NORM_EPSILON = 1e-06
BETA_ONE = 0.9
BETA_TWO = 0.95
STAT_DECAY = 0.95
LEARN_RATE = 0.1
WEIGHT_DECAY = 0.01
ADAM_EPSILON = 1e-08
CLIP_NORM = 1.0
MASK_FLOOR = -1e30


def layout():
    return [
        ("gain_one", (D,)),
        ("shift_one", (D,)),
        ("gain_two", (D,)),
        ("shift_two", (D,)),
        ("gain_three", (D,)),
        ("shift_three", (D,)),
        ("bias_query", (D,)),
        ("bias_value", (D,)),
        ("bias_out", (D,)),
        ("bias_up", (FF,)),
        ("bias_down", (D,)),
        ("conv_first", (D, 9, NT)),
        ("conv_second", (9, NT, NT)),
        ("conv_third", (9, NT, NT)),
        ("conv_fourth", (9, NT, NT)),
        ("conv_bias", (4, NT)),
    ]


def unpack(vector):
    params_split = {}
    offset = 0
    for part_name, part_shape in layout():
        entries = math.prod(part_shape)
        params_split[part_name] = vector[offset : offset + entries].reshape(part_shape)
        offset = offset + entries
    return params_split


def matrix_shapes():
    return [(D, 3 * D), (D, D), (D, FF), (FF, D)]


def to_blocks(matrix):
    row_count, col_count = matrix.shape
    tiled = matrix.reshape(row_count // BLOCK_SIDE, BLOCK_SIDE, col_count // BLOCK_SIDE, BLOCK_SIDE)
    return tiled.transpose(0, 2, 1, 3).reshape(-1, BLOCK_SIDE, BLOCK_SIDE)


def from_blocks(blocks):
    matrices = []
    offset = 0
    for row_count, col_count in matrix_shapes():
        tiles = row_count // BLOCK_SIDE * (col_count // BLOCK_SIDE)
        piece_tiles = blocks[offset : offset + tiles].reshape(
            row_count // BLOCK_SIDE, col_count // BLOCK_SIDE, BLOCK_SIDE, BLOCK_SIDE
        )
        matrices.append(piece_tiles.transpose(0, 2, 1, 3).reshape(row_count, col_count))
        offset = offset + tiles
    return matrices


def layer_norm(values, gain_vec, shift_vec):
    centre = jnp.mean(values, -1, keepdims=True)
    centered = values - centre
    spread = jnp.mean(centered * centered, -1, keepdims=True)
    return centered * lax.rsqrt(spread + NORM_EPSILON) * gain_vec + shift_vec


def gelu_exact(values):
    return jax.nn.gelu(values, approximate=False)


def taps_sum(taps):
    padded = jnp.pad(taps, ((0, 0), (1, 1), (1, 1), (0, 0), (0, 0)))
    summed = jnp.zeros(taps.shape[:3] + taps.shape[4:], taps.dtype)
    for tap_index in range(9):
        row_off = tap_index // 3 - 1
        col_off = tap_index % 3 - 1
        summed = (
            summed
            + padded[
                :, 1 + row_off : 1 + row_off + GRID, 1 + col_off : 1 + col_off + GRID, tap_index
            ]
        )
    return summed


def taps_back(grads):
    padded = jnp.pad(grads, ((0, 0), (1, 1), (1, 1), (0, 0)))
    shifted = []
    for tap_index in range(9):
        row_off = tap_index // 3 - 1
        col_off = tap_index % 3 - 1
        shifted.append(
            padded[:, 1 - row_off : 1 - row_off + GRID, 1 - col_off : 1 - col_off + GRID]
        )
    return jnp.stack(shifted, axis=3)


def conv_small(values, weight):
    taps = jnp.einsum("fyxc,tco->fyxto", values, weight, precision=FULL_PRECISION)
    return taps_sum(taps)


def learner_tail(first_pre, values, second_w, third_w, fourth_w, tail_bias):
    frames = first_pre.shape[0]
    act_one = gelu_exact(first_pre)
    act_two = gelu_exact(conv_small(act_one, second_w) + tail_bias[0])
    act_three = gelu_exact(conv_small(act_two, third_w) + tail_bias[1])
    maps = jax.nn.sigmoid(conv_small(act_three, fourth_w) + tail_bias[2])
    grid_values = values.reshape(frames, GRID, GRID, values.shape[-1])
    pooled = jnp.einsum("fyxk,fyxd->fkd", maps, grid_values, precision=FULL_PRECISION)
    return pooled.reshape(frames * NT, values.shape[-1])


def clip_segments(lengths, order_row, group_frames, frames_dev, frame_count):
    clip_ids = jnp.arange(lengths.shape[0], dtype=jnp.int32)
    ordered_len = jnp.sum(
        jnp.where(order_row[:, None] == clip_ids[None, :], lengths[None, :], 0), 1
    )
    ends = jnp.cumsum(ordered_len)
    slots = jnp.arange(group_frames, dtype=jnp.int32)
    places = slots % frames_dev * frame_count + slots // frames_dev
    return jnp.sum((ends[None, :] <= places[:, None]).astype(jnp.int32), 1)


F32=jnp.float32; BF=jnp.bfloat16
NN=(((1,),(0,)),((),()))
NT_=(((1,),(1,)),((),()))
TN=(((0,),(0,)),((),()))

def halves(a):
    high = a.astype(BF)
    return high, (a - high.astype(F32)).astype(BF)

def dot_low(a, b, dims):
    return lax.dot_general(a, b, dims, preferred_element_type=F32)

def dot_parts(a, b, dims):
    ah, al = a
    bh, bl = b
    return dot_low(ah, bh, dims) + (dot_low(ah, bl, dims) + dot_low(al, bh, dims))

def dot_wide(a, b, dims):
    return dot_parts(halves(a), halves(b), dims)

def slots_step(n):
    return 7 if n % 7 == 0 else 2 if n % 2 == 0 else 1


def stat_products(sl, sr, bl, br):
    n = sl.shape[0]
    many = slots_step(n)
    spec = pl.BlockSpec((many, BLOCK_SIDE, BLOCK_SIDE), lambda i: (i, 0, 0))

    def kernel(sl, sr, bl, br, out_left, out_right):
        for s in range(many):
            out_left[s] = STAT_DECAY * dot_wide(bl[s], sl[s], TN)
            out_right[s] = STAT_DECAY * dot_wide(br[s], sr[s], TN)

    return pl.pallas_call(
        kernel,
        grid=(n // many,),
        in_specs=[spec] * 4,
        out_specs=[spec] * 2,
        out_shape=[jax.ShapeDtypeStruct(sl.shape, F32)] * 2,
        cost_estimate=about(7),
    )(sl, sr, bl, br)


def raw_products(ranks, g, bl, br):
    n = g.shape[0]
    many = slots_step(n)
    here = pl.BlockSpec((many, BLOCK_SIDE, BLOCK_SIDE), lambda i, ranks: (i, 0, 0))

    def ranked(s):
        return pl.BlockSpec((1, BLOCK_SIDE, BLOCK_SIDE), lambda i, ranks: (ranks[i * many + s], 0, 0))

    def kernel(ranks, *refs):
        grads, (bl, br, rot, gl, gr, ql, qr) = refs[:many], refs[many:]
        each = range(many)
        gp = [halves(grads[s][0]) for s in each]
        blp, brp = [halves(bl[s]) for s in each], [halves(br[s]) for s in each]
        u = [halves(dot_parts(blp[s], gp[s], TN)) for s in each]
        v = [halves(dot_parts(gp[s], brp[s], NN)) for s in each]
        for s in each:
            gl[s] = dot_parts(gp[s], gp[s], NT_)
        for s in each:
            gr[s] = dot_parts(gp[s], gp[s], TN)
        for s in each:
            rot[s] = dot_parts(u[s], brp[s], NN)
        for s in each:
            ql[s] = dot_parts(u[s], gp[s], NT_)
        for s in each:
            qr[s] = dot_parts(v[s], gp[s], TN)

    return pl.pallas_call(
        kernel,
        grid_spec=pltpu.PrefetchScalarGridSpec(
            num_scalar_prefetch=1,
            grid=(n // many,),
            in_specs=[ranked(s) for s in range(many)] + [here, here],
            out_specs=[here] * 5,
        ),
        out_shape=[jax.ShapeDtypeStruct(g.shape, F32)] * 5,
        cost_estimate=about(8),
    )(ranks, *([g] * many), bl, br)


NB=32
def tall(parts, order):
    return jnp.concatenate([parts[which] for which in order], axis=0)


def wide(parts, order):
    return jnp.concatenate([parts[which] for which in order], axis=1)


def finish_kernel(factor, *refs):
    inputs, refs = refs[:14], refs[14:]
    results, refs = refs[:7], refs[7:]
    held, made = refs[:14], refs[14:21]
    work, elim, load_sems, store_sems = refs[21:]
    p_l, p_r, ql, qr, rot, gl, gr, sl, sr, bl, br, master, m1, m2 = held
    o_master, o_m1, o_m2, o_left, o_right, o_bl, o_br = made
    for index in range(14):
        pltpu.make_async_copy(inputs[index], held[index], load_sems.at[index]).start()

    def ready(*indices):
        for index in indices:
            pltpu.make_async_copy(inputs[index], held[index], load_sems.at[index]).wait()

    def store(*indices):
        for index in indices:
            pltpu.make_async_copy(made[index], results[index], store_sems.at[index]).start()

    n = rot.shape[0]
    count = 2 * n
    f = factor[0]
    f2 = (1.0 - STAT_DECAY) * f * f
    ready(0, 1, 2, 3)
    group = 7 if n % 7 == 0 else n
    for start in range(0, n, group):
        members = range(start, start + group)
        sums = [p_[s] + f2 * q_[s] for s in members for p_, q_ in ((p_l, ql), (p_r, qr))]
        parts = [halves(at) for at in sums]
        grams = [dot_parts(atp, atp, NT_) for atp in parts]
        for i in range(2 * group):
            work[2 * start + i, :, BLOCK_SIDE:] = sums[i]
            work[2 * start + i, :, :BLOCK_SIDE] = grams[i]

    rows = lax.broadcasted_iota(jnp.int32, (1, 8, 2 * NB), 1)
    lanes = lax.broadcasted_iota(jnp.int32, (1, 8, 2 * NB), 2)
    panels = BLOCK_SIDE // NB
    tile_count = NB // 8

    def panel(p, carry):
        for q in range(panels):
            @pl.when(p == q)
            def _(q=q):
                for t in range(tile_count):
                    block = work[:, NB * q + 8 * t : NB * q + 8 * t + 8, NB * q : NB * q + NB]
                    eye = jnp.where(lanes - NB == rows + 8 * t, 1.0, 0.0).astype(F32)
                    eye = jnp.broadcast_to(eye, (count, 8, 2 * NB))
                    elim[:, 8 * t : 8 * t + 8, :] = jnp.concatenate([block, eye[:, :, NB:]], axis=2)
        tiles = [elim[:, 8 * t : 8 * t + 8, :] for t in range(tile_count)]
        for k in range(NB):
            t0, j = divmod(k, 8)
            columns = [jnp.broadcast_to(tiles[t][:, :, k : k + 1], tiles[t].shape) for t in range(t0, tile_count)]
            row = tiles[t0][:, j : j + 1, :] * (1.0 / columns[0][:, j : j + 1, :])
            for t in range(t0, tile_count):
                new = tiles[t] - columns[t - t0] * row
                if t == t0:
                    new = jnp.where(rows > j, new, tiles[t])
                tiles[t] = new
        for t in range(tile_count):
            pivots = jnp.sum(jnp.where(lanes == rows + 8 * t, tiles[t], 0.0), axis=2, keepdims=True)
            elim[:, 8 * t : 8 * t + 8, :] = tiles[t] * lax.rsqrt(pivots)
        for q in range(panels):
            @pl.when(p == q)
            def _(q=q):
                lo, hi = NB * q, NB * q + NB
                for start in range(0, count, group):
                    members = range(start, start + group)
                    inverses = [wide(halves(elim[m, :, NB:]), (0, 0, 1)) for m in members]
                    sources = [tall(halves(work[m, lo:hi, :]), (0, 1, 0)) for m in members]
                    solved = [dot_low(inverses[i], sources[i], NN) for i in range(group)]
                    for i, m in enumerate(members):
                        (o_bl if m % 2 == 0 else o_br)[m // 2, lo:hi, :] = solved[i][:, BLOCK_SIDE:]
                    if hi < BLOCK_SIDE:
                        parts = [halves(y) for y in solved]
                        updates = [
                            dot_low(tall(yp, (0, 0, 1))[:, :BLOCK_SIDE], tall(yp, (0, 1, 0)), TN) for yp in parts
                        ]
                        for i, m in enumerate(members):
                            work[m, hi:, :] = work[m, hi:, :] - updates[i][hi:]
        return carry

    lax.fori_loop(0, panels, panel, 0)

    ready(4, 5, 6, 7, 8, 9, 10, 11, 12, 13)
    for start in range(0, n, group):
        members = range(start, start + group)
        firsts, directions = [], []
        for s in members:
            r = f * rot[s]
            m = BETA_ONE * m1[s] + (1.0 - BETA_ONE) * r
            v = BETA_TWO * m2[s] + (1.0 - BETA_TWO) * r * r
            o_m2[s] = v
            o_left[s] = STAT_DECAY * sl[s] + f2 * gl[s]
            o_right[s] = STAT_DECAY * sr[s] + f2 * gr[s]
            firsts.append(halves(m))
            directions.append(
                halves(m / (1.0 - BETA_ONE**STEP) / (jnp.sqrt(v / (1.0 - BETA_TWO**STEP)) + ADAM_EPSILON))
            )
        old_left = [halves(bl[s]) for s in members]
        old_right = [halves(br[s]) for s in members]
        new_left = [o_bl[s] for s in members]
        new_right = [o_br[s] for s in members]
        each = range(group)
        backs = [halves(dot_parts(old_left[i], directions[i], NN)) for i in each]
        turns_left = [halves(dot_parts(halves(new_left[i]), old_left[i], NN)) for i in each]
        turns_right = [halves(dot_parts(halves(new_right[i]), old_right[i], NN)) for i in each]
        returned = [dot_parts(backs[i], old_right[i], NT_) for i in each]
        parts = [halves(dot_parts(turns_left[i], firsts[i], NN)) for i in each]
        moved_firsts = [dot_parts(parts[i], turns_right[i], NT_) for i in each]
        for i, s in enumerate(members):
            o_master[s] = master[s] - LEARN_RATE * (returned[i] + WEIGHT_DECAY * master[s])
            o_m1[s] = moved_firsts[i]
            o_bl[s] = new_left[i].T
            o_br[s] = new_right[i].T
    store(0, 1, 2, 3, 4, 5, 6)
    for index in range(7):
        pltpu.make_async_copy(made[index], results[index], store_sems.at[index]).wait()


def finish(factor, rot, gl, gr, ql, qr, p_l, p_r, sl, sr, bl, br, master, m1, m2):
    n = rot.shape[0]
    shape = jax.ShapeDtypeStruct(rot.shape, F32)
    hbm = pl.BlockSpec(memory_space=pl.ANY)
    block = pltpu.VMEM((n, BLOCK_SIDE, BLOCK_SIDE), F32)
    return pl.pallas_call(
        finish_kernel,
        in_specs=[pl.BlockSpec(memory_space=pltpu.SMEM)] + [hbm] * 14,
        out_specs=[hbm] * 7,
        out_shape=[shape] * 7,
        scratch_shapes=[block] * 21
        + [
            pltpu.VMEM((2 * n, BLOCK_SIDE, 2 * BLOCK_SIDE), F32),
            pltpu.VMEM((2 * n, NB, 2 * NB), F32),
            pltpu.SemaphoreType.DMA((14,)),
            pltpu.SemaphoreType.DMA((7,)),
        ],
        compiler_params=pltpu.CompilerParams(vmem_limit_bytes=56 * 1024 * 1024),
        cost_estimate=about(30),
    )(factor, p_l, p_r, ql, qr, rot, gl, gr, sl, sr, bl, br, master, m1, m2)


def soap(ranks, g, factor, stat_parts, master, m1, m2, sl, sr, bl, br):
    rot, gl, gr, ql, qr = raw_products(ranks, g, bl, br)
    return finish(factor.reshape(1), rot, gl, gr, ql, qr, *stat_parts, sl, sr, bl, br, master, m1, m2)


def adam_update(clipped, params_old, first_old, second_old):
    first_new = BETA_ONE * first_old + (1.0 - BETA_ONE) * clipped
    second_new = BETA_TWO * second_old + (1.0 - BETA_TWO) * clipped * clipped
    stepped = (
        first_new
        / (1.0 - BETA_ONE**STEP)
        / (jnp.sqrt(second_new / (1.0 - BETA_TWO**STEP)) + ADAM_EPSILON)
    )
    return (first_new, second_new, params_old - LEARN_RATE * stepped)


FRAME_ROWS = GRID * GRID
PAD_ROWS = 208
OWN_ROWS = 2 * PAD_ROWS
LANES = 512
PAIRS = HEADS // 2
PAIR = 2 * HD
QKV_BLOCKS = 108
CODE_BASE = 1 << 16
VMEM_MOST = 58 * 1024 * 1024
ALL_AXES = ("fz", "fx", "by", "core")
FRAME_AXES = ("fz", "fx")
TAP_OFFSETS = [(tap // 3 - 1) * GRID + tap % 3 - 1 for tap in range(9)]


def about(microseconds):
    return pl.CostEstimate(flops=0, bytes_accessed=int(microseconds * 3e6), transcendentals=0)


def in_vmem():
    return pl.BlockSpec(memory_space=pltpu.VMEM)


def anywhere():
    return pl.BlockSpec(memory_space=pl.ANY)


def matrix_places():
    places = []
    first = 0
    for row_count, col_count in matrix_shapes():
        cols = col_count // BLOCK_SIDE
        count = row_count // BLOCK_SIDE * cols
        places.append((first, count, cols))
        first = first + count
    return places


def tile_at(ref, row, col):
    row = pl.multiple_of(row * BLOCK_SIDE, BLOCK_SIDE)
    col = pl.multiple_of(col * BLOCK_SIDE, BLOCK_SIDE)
    return ref.at[pl.ds(row, BLOCK_SIDE), pl.ds(col, BLOCK_SIDE)]


def load_matrix(which, codes, buffers, matrix, sem, first_buffer=0):
    first, count, cols = matrix_places()[which]

    def one_block(tile, carry):
        code = codes[first + tile]
        row, col = lax.div(tile, cols), lax.rem(tile, cols)
        for index, buffer in enumerate(buffers):
            @pl.when(lax.div(code, CODE_BASE) == first_buffer + index)
            def _():
                pltpu.make_async_copy(
                    buffer.at[lax.rem(code, CODE_BASE)], tile_at(matrix, row, col), sem
                ).start()
        return carry

    lax.fori_loop(0, count, one_block, 0)


def wait_whole(ref, sem):
    pltpu.make_async_copy(ref, ref, sem).wait()


def send_tile(code, buffers, tile, sem, first=0):
    for index, buffer in enumerate(buffers):
        @pl.when(lax.div(code, CODE_BASE) == first + index)
        def _():
            pltpu.make_async_copy(tile, buffer.at[lax.rem(code, CODE_BASE)], sem).start()


def normalized(values):
    centered = values - jnp.mean(values, -1, keepdims=True)
    spread = lax.rsqrt(jnp.mean(centered * centered, -1, keepdims=True) + NORM_EPSILON)
    return centered * spread, spread


def norm_back(grad, hat, spread, gain):
    scaled = grad * gain
    return spread * (
        scaled
        - jnp.mean(scaled, -1, keepdims=True)
        - hat * jnp.mean(scaled * hat, -1, keepdims=True)
    )


def project(codes, buffers, first_buffer, seen, rows14):
    rows = seen.shape[0]
    steps = rows // OWN_ROWS
    count = len(buffers)

    def kernel(codes, *refs):
        sources = refs[:count]
        seen, rows14, q, kv, low, own_low, w_qkv, sem = refs[count:]
        step = pl.program_id(0)

        @pl.when(step == 0)
        def _():
            load_matrix(0, codes, sources, w_qkv, sem, first_buffer)

        hat, _ = normalized(seen[...].astype(F32))
        normed = (hat * rows14[0:1] + rows14[1:2]).astype(BF)
        low[...] = normed

        @pl.when(step == 0)
        def _():
            wait_whole(w_qkv, sem)

        kv[:, :D] = dot_low(normed, w_qkv[:, D : 2 * D], NN).astype(BF)
        kv[:, D:] = (dot_low(normed, w_qkv[:, 2 * D :], NN) + rows14[7:8]).astype(BF)

        def own(place):
            part = normed[:PAD_ROWS]
            query = (dot_low(part, w_qkv[:, :D], NN) + rows14[6:7]).astype(BF)
            q[place : place + PAD_ROWS] = query * jnp.asarray(1.0 / math.sqrt(HD), BF)
            own_low[place : place + PAD_ROWS] = part

        @pl.when(step == 0)
        def _():
            own(0)

        @pl.when(step == steps - 1)
        def _():
            own(PAD_ROWS)

    def whole(shape):
        return pl.BlockSpec(shape, lambda i, codes: (0, 0))

    def moving(width):
        return pl.BlockSpec((OWN_ROWS, width), lambda i, codes: (i, 0))

    return pl.pallas_call(
        kernel,
        grid_spec=pltpu.PrefetchScalarGridSpec(
            num_scalar_prefetch=1,
            grid=(steps,),
            in_specs=[anywhere()] * count + [moving(D), whole((14, D))],
            out_specs=[whole((OWN_ROWS, D)), moving(2 * D), moving(D), whole((OWN_ROWS, D)), whole((D, 3 * D))],
            scratch_shapes=[pltpu.SemaphoreType.DMA],
        ),
        out_shape=[
            jax.ShapeDtypeStruct((OWN_ROWS, D), BF),
            jax.ShapeDtypeStruct((rows, 2 * D), BF),
            jax.ShapeDtypeStruct((rows, D), BF),
            jax.ShapeDtypeStruct((OWN_ROWS, D), BF),
            jax.ShapeDtypeStruct((D, 3 * D), BF),
        ],
        compiler_params=pltpu.CompilerParams(vmem_limit_bytes=VMEM_MOST),
        cost_estimate=about(15),
    )(codes, *buffers, seen, rows14)


ROW_STEP = 16


def stacked(values):
    first = lax.broadcasted_iota(jnp.int32, (1, PAIR), 1) < HD
    nothing = jnp.zeros_like(values)
    return jnp.concatenate([jnp.where(first, values, nothing), jnp.where(first, nothing, values)], axis=0)


def unstacked(values):
    first = lax.broadcasted_iota(jnp.int32, (1, PAIR), 1) < HD
    return jnp.where(first, values[:PAD_ROWS], values[PAD_ROWS:])


def attend_kernel(long_rows, q, k, v, bias, out, logs, scores, soft):
    total = k.shape[0]
    for frame, (lo, hi) in enumerate(((0, long_rows), (long_rows, total))):
        rows = slice(frame * PAD_ROWS, (frame + 1) * PAD_ROWS)
        width = hi - lo
        scores[:, :width] = dot_low(stacked(q[rows, :]), k[lo:hi, :], NT_)
        norms, peaks = [], []
        for row in range(0, OWN_ROWS, ROW_STEP):
            block = scores[row : row + ROW_STEP, :width] + bias[:, lo:hi]
            peak = jnp.max(block, axis=1, keepdims=True)
            weights = jnp.exp(block - peak)
            norms.append(jnp.sum(weights, axis=1, keepdims=True))
            peaks.append(peak)
            soft[row : row + ROW_STEP, :width] = weights.astype(BF)
        norm = jnp.concatenate(norms, axis=0)
        out[rows, :] = unstacked(dot_low(soft[:, :width], v[lo:hi, :], NN) / norm).astype(BF)
        logs[rows, :] = unstacked(jnp.broadcast_to(jnp.concatenate(peaks, axis=0) + jnp.log(norm), (OWN_ROWS, PAIR)))


def attend_back_kernel(long_rows, q, k, v, bias, out, logs, grad, dq, dk, dv, scores, soft_grads, soft, changes):
    total = k.shape[0]
    for frame, (lo, hi) in enumerate(((0, long_rows), (long_rows, total))):
        rows = slice(frame * PAD_ROWS, (frame + 1) * PAD_ROWS)
        width = hi - lo
        query, arriving = stacked(q[rows, :]), stacked(grad[rows, :])
        products = stacked(grad[rows, :].astype(F32) * out[rows, :].astype(F32))
        delta = jnp.sum(products, axis=1, keepdims=True)
        log = jnp.concatenate([logs[rows, 0:1], logs[rows, HD : HD + 1]], axis=0)
        scores[:, :width] = dot_low(query, k[lo:hi, :], NT_)
        soft_grads[:, :width] = dot_low(arriving, v[lo:hi, :], NT_)
        for row in range(0, OWN_ROWS, ROW_STEP):
            here = slice(row, row + ROW_STEP)
            weights = jnp.exp(scores[here, :width] + bias[:, lo:hi] - log[here])
            soft[here, :width] = weights.astype(BF)
            changes[here, :width] = (weights * (soft_grads[here, :width] - delta[here])).astype(BF)
        part = unstacked(dot_low(changes[:, :width], k[lo:hi, :], NN))
        dq[rows, :] = (part * (1.0 / math.sqrt(HD))).astype(BF)
        dk[lo:hi, :] = dot_low(query, changes[:, :width], TN).T.astype(BF)
        dv[lo:hi, :] = dot_low(arriving, soft[:, :width], TN).T.astype(BF)


def pair_spec(rows, offset=0):
    return pl.BlockSpec((rows, PAIR), lambda i: (0, i + offset))


def attend(q, kv, bias):
    keys_total = kv.shape[0]
    long_rows = keys_total - OWN_ROWS

    def kernel(*refs):
        attend_kernel(long_rows, *refs)

    return pl.pallas_call(
        kernel,
        grid=(PAIRS,),
        in_specs=[
            pair_spec(OWN_ROWS),
            pair_spec(keys_total),
            pair_spec(keys_total, PAIRS),
            pl.BlockSpec((1, keys_total), lambda i: (0, 0)),
        ],
        out_specs=[pair_spec(OWN_ROWS)] * 2,
        out_shape=[jax.ShapeDtypeStruct((OWN_ROWS, D), BF), jax.ShapeDtypeStruct((OWN_ROWS, D), F32)],
        scratch_shapes=[pltpu.VMEM((OWN_ROWS, long_rows), F32), pltpu.VMEM((OWN_ROWS, long_rows), BF)],
        compiler_params=pltpu.CompilerParams(vmem_limit_bytes=VMEM_MOST),
        cost_estimate=about(12),
    )(q, kv, kv, bias.reshape(1, -1))


def attend_back(q, kv, bias, out, logs, grad):
    keys_total = kv.shape[0]
    long_rows = keys_total - OWN_ROWS

    def kernel(*refs):
        attend_back_kernel(long_rows, *refs)

    return pl.pallas_call(
        kernel,
        grid=(PAIRS,),
        in_specs=[
            pair_spec(OWN_ROWS),
            pair_spec(keys_total),
            pair_spec(keys_total, PAIRS),
            pl.BlockSpec((1, keys_total), lambda i: (0, 0)),
            pair_spec(OWN_ROWS),
            pair_spec(OWN_ROWS),
            pair_spec(OWN_ROWS),
        ],
        out_specs=[pair_spec(OWN_ROWS), pair_spec(keys_total), pair_spec(keys_total)],
        out_shape=[
            jax.ShapeDtypeStruct((OWN_ROWS, D), BF),
            jax.ShapeDtypeStruct((keys_total, D), BF),
            jax.ShapeDtypeStruct((keys_total, D), BF),
        ],
        scratch_shapes=[pltpu.VMEM((OWN_ROWS, long_rows), F32)] * 2 + [pltpu.VMEM((OWN_ROWS, long_rows), BF)] * 2,
        compiler_params=pltpu.CompilerParams(vmem_limit_bytes=VMEM_MOST),
        cost_estimate=about(24),
    )(q, kv, kv, bias.reshape(1, -1), out, logs, grad)


def lane_masks():
    lane = np.arange(LANES)
    inner = lane % PAD_ROWS
    token = (lane < OWN_ROWS) & (inner < FRAME_ROWS)
    row, col = inner // GRID, inner % GRID
    masks = []
    for tap in range(9):
        far_row, far_col = row + tap // 3 - 1, col + tap % 3 - 1
        masks.append(token & (far_row >= 0) & (far_row < GRID) & (far_col >= 0) & (far_col < GRID))
    masks.append(token & (lane < PAD_ROWS))
    masks.append(token & (lane >= PAD_ROWS))
    masks = masks + [np.zeros(LANES, bool)] * (16 - len(masks))
    return np.stack(masks).astype(np.float32)


def ahead(values, offset):
    return values if offset == 0 else pltpu.roll(values, (-offset) % LANES, axis=1)


def cumulative(values):
    return 0.5 + 0.5 * lax.erf(values * math.sqrt(0.5))


def gelu_slope(values, portion):
    return portion + values * jnp.exp(-0.5 * values * values) * (1.0 / math.sqrt(2.0 * math.pi))


def column_sum(values):
    return jnp.sum(values, axis=0, keepdims=True)


def widened(values):
    return jnp.concatenate([values, jnp.zeros((values.shape[0], LANES - OWN_ROWS), values.dtype)], axis=1)


def middle_kernel(weight_count, first_buffer, codes, targets, *refs):
    sources = refs[:weight_count]
    (
        att, own, cot, rows14, conv_t, taps_forward, taps_backward, tail_bias, masks, blank,
        learned, grad_mixed, grad_att, vectors, grad_up_bias, grad_conv, grad_tail, grad_tail_bias,
    ) = refs[weight_count : weight_count + 18]
    buffers = refs[weight_count + 18 : -14]
    (
        w_out, w_up, w_down, d_out, d_up, d_down, activated, slopes, normed, hat_two, mixed, gathered_sum,
        load_sems, send_sems,
    ) = refs[-14:]
    chunks = FF // D
    load_matrix(1, codes, sources, w_out, load_sems.at[0], first_buffer)
    load_matrix(2, codes, sources, w_up, load_sems.at[1], first_buffer)
    load_matrix(3, codes, sources, w_down, load_sems.at[2], first_buffer)

    def one_blank(block, total):
        code = targets[block]
        early = lax.div(code, CODE_BASE) < 4
        filled = (block >= MATRIX_BLOCKS) | ((block < QKV_BLOCKS) & early)

        @pl.when(filled)
        def _():
            send_tile(code, buffers, blank, send_sems.at[3])

        return total + filled.astype(jnp.int32)

    blanks = lax.fori_loop(0, QKV_BLOCKS, one_blank, jnp.int32(0))
    blanks = lax.fori_loop(MATRIX_BLOCKS, targets.shape[0], one_blank, blanks)

    wait_whole(w_out, load_sems.at[0])
    start = own[...].astype(F32) + dot_low(att[...], w_out[...], NN) + rows14[8:9]
    mixed[...] = start
    hat, spread_two = normalized(start)
    hat_two[...] = hat
    normed[...] = (hat * rows14[2:3] + rows14[3:4]).astype(BF)
    gathered_sum[...] = start + rows14[13:14]
    wait_whole(w_up, load_sems.at[1])
    wait_whole(w_down, load_sems.at[2])

    for chunk in range(chunks):
        at = slice(chunk * D, (chunk + 1) * D)
        hidden = dot_low(normed[...], w_up[:, at], NN) + rows14[9 + chunk : 10 + chunk]
        portion = cumulative(hidden)
        active = (hidden * portion).astype(BF)
        activated[chunk] = active
        slopes[chunk] = gelu_slope(hidden, portion)
        gathered_sum[...] += dot_low(active, w_down[at, :], NN)

    out_two = gathered_sum[...]
    hat, spread_three = normalized(out_two)
    low_three = (hat * rows14[4:5] + rows14[5:6]).astype(BF)

    taps = widened(dot_low(conv_t[...], low_three, NT_))
    first = tail_bias[:, 0:1]
    for tap in range(9):
        first = first + ahead(taps[NT * tap : NT * (tap + 1)], TAP_OFFSETS[tap]) * masks[tap : tap + 1]

    def around(values, sign):
        order = range(9) if sign > 0 else range(8, -1, -1)
        return jnp.concatenate(
            [
                ahead(values, sign * TAP_OFFSETS[tap]) * masks[seen : seen + 1]
                for tap, seen in zip(range(9), order)
            ],
            axis=0,
        )

    before, stacks, portions = [first], [], []
    for layer in range(3):
        portions.append(cumulative(before[-1]))
        stacks.append(around(before[-1] * portions[-1], 1))
        before.append(dot_wide(taps_forward[layer], stacks[-1], NN) + tail_bias[:, layer + 1 : layer + 2])
    maps = 1.0 / (1.0 + jnp.exp(-before[3]))
    both = jnp.concatenate([maps * masks[9:10], maps * masks[10:11]], axis=0)[:, :OWN_ROWS]
    both = halves(both)
    out_parts = halves(out_two)
    arriving = cot[...]
    learned[...] = dot_parts(both, out_parts, NN)
    seen_maps = widened(dot_low(arriving, out_parts[0], NT_) + dot_low(arriving, out_parts[1], NT_))
    grad = (seen_maps[:NT] * masks[9:10] + seen_maps[NT:] * masks[10:11]) * maps * (1.0 - maps)
    sums = [None] * 4
    for layer in (2, 1, 0):
        sums[layer + 1] = jnp.sum(grad, axis=1, keepdims=True)
        grad_tail[layer] = dot_wide(stacks[layer], grad, NT_)
        grad = dot_wide(taps_backward[layer], around(grad, -1), NN)
        grad = grad * gelu_slope(before[layer], portions[layer])
    grad = grad.astype(BF).astype(F32)
    sums[0] = jnp.sum(grad, axis=1, keepdims=True)
    grad_tail_bias[...] = jnp.concatenate(sums, axis=1)
    grad_taps = around(grad, -1)[:, :OWN_ROWS].astype(BF)
    grad_conv[...] = dot_low(grad_taps, low_three, NN)
    grad_norm_three = dot_low(grad_taps, conv_t[...], TN)
    vectors[2:3] = column_sum(grad_norm_three * hat)
    vectors[3:4] = column_sum(grad_norm_three)
    grad_out = (
        norm_back(grad_norm_three, hat, spread_three, rows14[4:5])
        + dot_low(both[0], arriving, TN)
        + dot_low(both[1], arriving, TN)
    )
    grad_down = grad_out.astype(BF)
    vectors[5:6] = column_sum(grad_down.astype(F32))

    for chunk in range(chunks):
        at = slice(chunk * D, (chunk + 1) * D)
        grad_active = dot_low(grad_down, w_down[at, :], NT_)
        grad_hidden = (grad_active * slopes[chunk]).astype(BF)
        grad_up_bias[chunk : chunk + 1] = column_sum(grad_hidden.astype(F32))
        part = dot_low(grad_hidden, w_up[:, at], NT_)
        if chunk == 0:
            gathered_sum[...] = part
        else:
            gathered_sum[...] += part
        d_down[at, :] = dot_low(activated[chunk], grad_down, TN).astype(BF)
        d_up[:, at] = dot_low(normed[...], grad_hidden, TN).astype(BF)
        side = D // BLOCK_SIDE

        def one_tile(tile, carry, chunk=chunk):
            row, col = lax.div(tile, side), lax.rem(tile, side)
            first_up, first_down = matrix_places()[2][0], matrix_places()[3][0]
            up_block = first_up + row * (FF // BLOCK_SIDE) + chunk * side + col
            send_tile(targets[up_block], buffers, tile_at(d_up, row, chunk * side + col), send_sems.at[1])
            down_block = first_down + (chunk * side + row) * side + col
            send_tile(targets[down_block], buffers, tile_at(d_down, chunk * side + row, col), send_sems.at[2])
            return carry

        lax.fori_loop(0, side * side, one_tile, 0)

    grad_norm_two = gathered_sum[...]
    vectors[0:1] = column_sum(grad_norm_two * hat_two[...])
    vectors[1:2] = column_sum(grad_norm_two)
    total = grad_out + norm_back(grad_norm_two, hat_two[...], spread_two, rows14[2:3])
    grad_mixed[...] = total
    branch = total.astype(BF)
    vectors[4:5] = column_sum(branch.astype(F32))
    d_out[...] = dot_low(att[...], branch, TN).astype(BF)

    def one_out(tile, carry):
        side = D // BLOCK_SIDE
        code = targets[matrix_places()[1][0] + tile]
        send_tile(code, buffers, tile_at(d_out, lax.div(tile, side), lax.rem(tile, side)), send_sems.at[0])
        return carry

    lax.fori_loop(0, matrix_places()[1][1], one_out, 0)
    grad_att[...] = dot_low(branch, w_out[...], NT_).astype(BF)
    wait_whole(d_out, send_sems.at[0])
    wait_whole(d_up, send_sems.at[1])
    wait_whole(d_down, send_sems.at[2])

    def one_wait(index, carry):
        wait_whole(blank, send_sems.at[3])
        return carry

    lax.fori_loop(0, blanks, one_wait, 0)


def middle(codes, targets, weights, first_buffer, buffer_shapes, att, own, cot, rows14, conv_t, taps_forward, taps_backward, tail_bias):
    count = len(weights)

    def kernel(*refs):
        middle_kernel(count, first_buffer, *refs)

    def f32(*shape):
        return jax.ShapeDtypeStruct(shape, F32)

    outs = [
        f32(2 * NT, D), f32(OWN_ROWS, D), jax.ShapeDtypeStruct((OWN_ROWS, D), BF), f32(8, D),
        f32(FF // D, D), f32(9 * NT, D), f32(3, 9 * NT, NT), f32(NT, 4),
    ]
    results = pl.pallas_call(
        kernel,
        grid_spec=pltpu.PrefetchScalarGridSpec(
            num_scalar_prefetch=2,
            grid=(1,),
            in_specs=[anywhere()] * count + [in_vmem()] * 10,
            out_specs=[in_vmem()] * len(outs) + [anywhere()] * len(buffer_shapes),
            scratch_shapes=[
                pltpu.VMEM((D, D), BF),
                pltpu.VMEM((D, FF), BF),
                pltpu.VMEM((FF, D), BF),
                pltpu.VMEM((D, D), BF),
                pltpu.VMEM((D, FF), BF),
                pltpu.VMEM((FF, D), BF),
                pltpu.VMEM((FF // D, OWN_ROWS, D), BF),
                pltpu.VMEM((FF // D, OWN_ROWS, D), F32),
                pltpu.VMEM((OWN_ROWS, D), BF),
                pltpu.VMEM((OWN_ROWS, D), F32),
                pltpu.VMEM((OWN_ROWS, D), F32),
                pltpu.VMEM((OWN_ROWS, D), F32),
                pltpu.SemaphoreType.DMA((3,)),
                pltpu.SemaphoreType.DMA((4,)),
            ],
        ),
        out_shape=outs + buffer_shapes,
        compiler_params=pltpu.CompilerParams(vmem_limit_bytes=VMEM_MOST),
        cost_estimate=about(40),
    )(
        codes, targets, *weights, att, own, cot, rows14, conv_t, taps_forward, taps_backward, tail_bias,
        jnp.asarray(lane_masks()), jnp.zeros((BLOCK_SIDE, BLOCK_SIDE), BF),
    )
    return results[: len(outs)], results[len(outs) :]


def qkv_grads(targets, low, own_low, dq, dk, dv, buffers, late):
    steps = low.shape[0] // OWN_ROWS
    count = len(buffers)

    def kernel(targets, low, own_low, dq, dk, dv, *refs):
        filled = refs[count : 2 * count]
        matrix = refs[2 * count]
        totals, sem = refs[2 * count + 1 :]
        step = pl.program_id(0)

        @pl.when(step == 0)
        def _():
            totals[...] = jnp.zeros_like(totals)
            matrix[:, :D] = dot_low(own_low[...], dq[...], TN).astype(BF)

        totals[:, :D] += dot_low(low[...], dk[...], TN)
        totals[:, D:] += dot_low(low[...], dv[...], TN)

        @pl.when(step == steps - 1)
        def _():
            matrix[:, D:] = totals[...].astype(BF)
            cols = 3 * D // BLOCK_SIDE

            def one_tile(tile, sent):
                code = targets[tile]
                send_tile(code, filled, tile_at(matrix, lax.div(tile, cols), lax.rem(tile, cols)), sem, late)
                return sent + (lax.div(code, CODE_BASE) >= late).astype(jnp.int32)

            sent = lax.fori_loop(0, QKV_BLOCKS, one_tile, jnp.int32(0))

            def one_wait(index, carry):
                wait_whole(tile_at(matrix, 0, 0), sem)
                return carry

            lax.fori_loop(0, sent, one_wait, 0)

    def whole(shape):
        return pl.BlockSpec(shape, lambda i, targets: (0, 0))

    def moving(width):
        return pl.BlockSpec((OWN_ROWS, width), lambda i, targets: (i, 0))

    results = pl.pallas_call(
        kernel,
        grid_spec=pltpu.PrefetchScalarGridSpec(
            num_scalar_prefetch=1,
            grid=(steps,),
            in_specs=[moving(D), whole((OWN_ROWS, D)), whole((OWN_ROWS, D)), moving(D), moving(D)]
            + [anywhere()] * count,
            out_specs=[anywhere()] * count + [whole((D, 3 * D))],
            scratch_shapes=[pltpu.VMEM((D, 2 * D), F32), pltpu.SemaphoreType.DMA],
        ),
        out_shape=[jax.ShapeDtypeStruct(b.shape, b.dtype) for b in buffers]
        + [jax.ShapeDtypeStruct((D, 3 * D), BF)],
        input_output_aliases={6 + i: i for i in range(count)},
        compiler_params=pltpu.CompilerParams(vmem_limit_bytes=VMEM_MOST),
        cost_estimate=about(14),
    )(targets, low, own_low, dq, dk, dv, *buffers)
    return results[:count], results[count]


def input_grads(seen, own, dq, dk, dv, w_qkv):
    rows = seen.shape[0]
    steps = rows // OWN_ROWS

    def kernel(seen, own, dq, dk, dv, w_qkv, grad_seen, grad_own, sums):
        step = pl.program_id(0)

        @pl.when(step == 0)
        def _():
            grad = dot_low(dq[...], w_qkv[:, :D], NT_)
            grad_own[...] = grad
            hat, _ = normalized(own[...].astype(F32))
            sums[...] = jnp.zeros_like(sums)
            sums[0:1] = column_sum(grad * hat)
            sums[1:2] = column_sum(grad)
            sums[2:3] = column_sum(dq[...].astype(F32))

        grad = dot_low(dk[...], w_qkv[:, D : 2 * D], NT_) + dot_low(dv[...], w_qkv[:, 2 * D :], NT_)
        grad_seen[...] = grad.astype(BF)
        hat, _ = normalized(seen[...].astype(F32))
        sums[0:1] += column_sum(grad * hat)
        sums[1:2] += column_sum(grad)
        sums[3:4] += column_sum(dv[...].astype(F32))

    def whole(shape):
        return pl.BlockSpec(shape, lambda i: (0, 0))

    moving = pl.BlockSpec((OWN_ROWS, D), lambda i: (i, 0))
    return pl.pallas_call(
        kernel,
        grid=(steps,),
        in_specs=[moving, whole((OWN_ROWS, D)), whole((OWN_ROWS, D)), moving, moving, whole((D, 3 * D))],
        out_specs=[moving, whole((OWN_ROWS, D)), whole((8, D))],
        out_shape=[
            jax.ShapeDtypeStruct((rows, D), BF),
            jax.ShapeDtypeStruct((OWN_ROWS, D), F32),
            jax.ShapeDtypeStruct((8, D), F32),
        ],
        compiler_params=pltpu.CompilerParams(vmem_limit_bytes=VMEM_MOST),
        cost_estimate=about(12),
    )(seen, own, dq, dk, dv, w_qkv)


def moved(value, axis, size, step):
    return lax.ppermute(value, axis, [(i, (i + step) % size) for i in range(size)])


def reduce_axis(terms, axis, size, dim=0):
    total = lax.index_in_dim(terms, 0, dim, keepdims=False).astype(F32)
    for step in range(1, size):
        term = lax.index_in_dim(terms, step, dim, keepdims=False)
        total = total + moved(term, axis, size, step).astype(F32)
    return total


def after(value, *others):
    return lax.optimization_barrier((value, others))[0]


def gather_axis(value, axis, size):
    return jnp.stack([value] + [moved(value, axis, size, -step) for step in range(1, size)])


def rolled(value, axis, size, step):
    return lax.dynamic_slice_in_dim(jnp.concatenate([value, value], axis), step, size, axis)


def early_slots(slots_dev):
    return slots_dev * 6 // 14


def slot_chunks(slots_dev):
    early = early_slots(slots_dev)
    late = slots_dev - early
    chunks = []
    first = 0
    for index, count in enumerate((early - early // 2, early // 2, late - late // 2, late // 2)):
        chunks.append((first, count, ("fx", "by", "fz") if index % 2 == 0 else ("by", "fx", "fz")))
        first = first + count
    return chunks


def send_table(block_owner, sizes, coords, slots_dev):
    nz, nx, ny, nc = sizes
    slots = jnp.arange(block_owner.shape[0], dtype=jnp.int32)
    device = slots // slots_dev
    place = {}
    for axis in range(3, -1, -1):
        place[ALL_AXES[axis]] = (device % sizes[axis] - coords[axis] + sizes[axis]) % sizes[axis]
        device = device // sizes[axis]
    is_late = (block_owner < QKV_BLOCKS).astype(jnp.int32).reshape(-1, slots_dev)
    late_before = jnp.cumsum(is_late, 1) - is_late
    early_before = jnp.arange(slots_dev, dtype=jnp.int32)[None] - late_before
    late_count = jnp.sum(is_late, 1, keepdims=True)
    ranks = jnp.where(is_late == 1, slots_dev - late_count + late_before, early_before)
    rank = ranks.reshape(-1)
    size_of = dict(zip(ALL_AXES, sizes))
    code = jnp.zeros_like(slots)
    for index, (first, count, axes) in enumerate(slot_chunks(slots_dev)):
        at = jnp.zeros_like(slots)
        for name in axes:
            at = at * size_of[name] + place[name]
        at = at * count + rank - first
        inside = (rank >= first) & (rank < first + count)
        code = jnp.where(inside, (2 * index + place["core"]) * CODE_BASE + at, code)
    owned = block_owner[:, None] == slots[None, :]
    table = jnp.sum(jnp.where(owned, code[:, None], 0), 0)
    early = early_slots(slots_dev)
    gathered = jnp.where(rank < early, slots // slots_dev * early + rank, code - 3 * CODE_BASE)
    weight_table = jnp.sum(jnp.where(owned, gathered[:, None], 0), 0)
    return table, weight_table, ranks, jnp.max(late_count)


def reduce_core(kept, sent, count, axes, sizes):
    size_of = dict(zip(ALL_AXES, sizes))
    total = (kept.astype(F32) + moved(sent, "core", 2, 1).astype(F32)).astype(BF)
    return total.reshape([size_of[name] for name in axes] + [count, BLOCK_SIDE, BLOCK_SIDE])


def reduce_stage(total, axes, stage, sizes):
    name = axes[stage]
    total = reduce_axis(total, name, sizes[ALL_AXES.index(name)])
    return total if stage == len(axes) - 1 else total.astype(BF)


def reduce_rest(total, axes, sizes):
    for stage in range(len(axes)):
        total = reduce_stage(total, axes, stage, sizes)
    return total


def reduce_chunk(kept, sent, count, axes, sizes):
    return reduce_rest(reduce_core(kept, sent, count, axes, sizes), axes, sizes)


def gather_stage(shard, axes, stage, sizes):
    name = axes[len(axes) - 1 - stage]
    return gather_axis(shard, name, sizes[ALL_AXES.index(name)])


def gather_core(shard):
    shard = shard.reshape(-1, BLOCK_SIDE, BLOCK_SIDE)
    return [shard, moved(shard, "core", 2, 1)]


def gather_chunk(shard, axes, sizes):
    for stage in range(len(axes)):
        shard = gather_stage(shard, axes, stage, sizes)
    return gather_core(shard)


def sorted_shards(device_index, block_owner, master):
    slots_dev = master.shape[0]
    chunks = [(0, early_slots(slots_dev), ())] + slot_chunks(slots_dev)[2:]

    def kernel(where, owner, blocks, *outs):
        base = where[0] * slots_dev
        late_count = jnp.int32(0)
        for slot in range(slots_dev):
            late_count = late_count + (owner[base + slot] < QKV_BLOCKS).astype(jnp.int32)
        early_at, late_at = jnp.int32(0), slots_dev - late_count
        for slot in range(slots_dev):
            late = owner[base + slot] < QKV_BLOCKS
            rank = jnp.where(late, late_at, early_at)
            late_at = late_at + late.astype(jnp.int32)
            early_at = early_at + 1 - late.astype(jnp.int32)
            for index, (first, count, axes) in enumerate(chunks):
                if count == 0:
                    continue

                @pl.when((rank >= first) & (rank < first + count))
                def _(index=index, first=first):
                    outs[index][rank - first] = blocks[slot].astype(BF)

    return pl.pallas_call(
        kernel,
        grid_spec=pltpu.PrefetchScalarGridSpec(
            num_scalar_prefetch=2,
            grid=(1,),
            in_specs=[in_vmem()],
            out_specs=[in_vmem()] * len(chunks),
        ),
        out_shape=[
            jax.ShapeDtypeStruct((max(count, 1), BLOCK_SIDE, BLOCK_SIDE), BF) for first, count, axes in chunks
        ],
        cost_estimate=about(3),
    )(device_index.reshape(1), block_owner, master)


def spread_early(targets, matrix, buffer_shapes):
    count = len(buffer_shapes)

    def kernel(targets, matrix, blank, *refs):
        buffers, sem = refs[:count], refs[count]

        def one_block(block, sent):
            code = targets[block]
            cols = 3 * D // BLOCK_SIDE
            early = lax.div(code, CODE_BASE) < 4

            @pl.when(early & (block < QKV_BLOCKS))
            def _():
                tile = tile_at(matrix, lax.div(block, cols), lax.rem(block, cols))
                send_tile(code, buffers, tile, sem)

            @pl.when(early & (block >= QKV_BLOCKS))
            def _():
                send_tile(code, buffers, blank, sem)

            return sent + early.astype(jnp.int32)

        sent = lax.fori_loop(0, targets.shape[0], one_block, jnp.int32(0))

        def one_wait(index, carry):
            wait_whole(blank, sem)
            return carry

        lax.fori_loop(0, sent, one_wait, 0)

    return pl.pallas_call(
        kernel,
        grid_spec=pltpu.PrefetchScalarGridSpec(
            num_scalar_prefetch=1,
            grid=(1,),
            in_specs=[in_vmem()] * 2,
            out_specs=[anywhere()] * count,
            scratch_shapes=[pltpu.SemaphoreType.DMA],
        ),
        out_shape=buffer_shapes,
        compiler_params=pltpu.CompilerParams(vmem_limit_bytes=VMEM_MOST),
    )(targets, matrix, jnp.zeros((BLOCK_SIDE, BLOCK_SIDE), BF))


def pad_frames(values):
    frames = values.reshape(2, FRAME_ROWS, values.shape[-1])
    return jnp.pad(frames, ((0, 0), (0, PAD_ROWS - FRAME_ROWS), (0, 0)))


def on_device(
    tokens,
    cotangent,
    clip_lengths,
    clip_order,
    block_owner,
    master,
    moment1,
    moment2,
    stat_left,
    stat_right,
    basis_left,
    basis_right,
    small_params,
    small_moment1,
    small_moment2,
):
    sizes = tuple(lax.axis_size(name) for name in ALL_AXES)
    coords = [lax.axis_index(name) for name in ALL_AXES]
    nz, nx, ny, nc = sizes
    device_count = nz * nx * ny * nc
    frame_count = nz * nx
    frame_index = coords[0] * nx + coords[1]
    slots_dev = master.shape[0]

    segment_slots = clip_segments(
        clip_lengths[0], clip_order[0], 2 * frame_count, 2, frame_count
    ).reshape(frame_count, 2)
    ordered_len = clip_lengths[0][clip_order[0]]
    longest = jnp.argmax(ordered_len).astype(jnp.int32)
    second_long = segment_slots[:, 1] == longest
    short_segment = jnp.where(second_long, segment_slots[:, 0], segment_slots[:, 1])
    swap = second_long[frame_index]
    padded_segment = jnp.pad(short_segment, (1, 1), constant_values=-1)
    near = lax.dynamic_slice_in_dim(padded_segment, frame_index, 3)
    with_previous = near[0] == near[1]
    with_next = near[2] == near[1]

    device_index = ((coords[0] * nx + coords[1]) * ny + coords[2]) * nc + coords[3]
    early = early_slots(slots_dev)
    chunks = slot_chunks(slots_dev)
    shards = sorted_shards(device_index, block_owner, master)
    orders = [axes for first, count, axes in chunks]
    late_shards = [gather_stage(shards[1 + i], orders[2 + i], 0, sizes) for i in range(2)]

    own_frames = pad_frames(tokens[0])
    own_frames = jnp.where(swap, own_frames[::-1], own_frames)
    long_frame, short_frame = own_frames[0], own_frames[1]
    frame_perm = [(i, (i + 1) % frame_count) for i in range(frame_count)]
    back_perm = [(j, i) for i, j in frame_perm]
    def gather_early(shard):
        return lax.all_gather(shard, ALL_AXES, axis=0, tiled=True)

    weights = [gather_early(shards[0])] if early else []
    long_pair = gather_axis(long_frame, "fx", nx)
    long_pair, late_shards = lax.optimization_barrier((long_pair, late_shards))
    late_shards = [gather_stage(part, orders[2 + i], 1, sizes) for i, part in enumerate(late_shards)]
    long_frames = [long_pair] + [moved(long_pair, "fz", nz, -step) for step in range(1, nz)]
    late_shards, long_frames[1] = lax.optimization_barrier((late_shards, long_frames[1]))
    late_shards = [gather_stage(part, orders[2 + i], 2, sizes) for i, part in enumerate(late_shards)]
    from_previous = lax.ppermute(short_frame, FRAME_AXES, frame_perm)
    from_next = lax.ppermute(short_frame, FRAME_AXES, back_perm)
    late_shards, long_frames, from_previous, from_next = lax.optimization_barrier(
        (late_shards, long_frames, from_previous, from_next)
    )
    weights = weights + gather_core(late_shards[0]) + gather_core(late_shards[1])
    long_frames = jnp.stack(long_frames)
    partner = jnp.where(with_next, from_next, from_previous)

    frames_seen = frame_count + 2
    seen = jnp.concatenate(
        [long_frames.reshape(frame_count, PAD_ROWS, D), short_frame[None], partner[None]]
    ).reshape(frames_seen * PAD_ROWS, D)
    own = own_frames.reshape(OWN_ROWS, D)
    row_ids = jnp.arange(frames_seen * PAD_ROWS, dtype=jnp.int32)
    hidden_key = (row_ids % PAD_ROWS >= FRAME_ROWS) | (
        (row_ids >= (frames_seen - 1) * PAD_ROWS) & ~(with_previous | with_next)
    )
    key_bias = jnp.where(hidden_key, MASK_FLOOR, 0.0).astype(F32)

    targets, weight_codes, ranks, late_most = send_table(block_owner, sizes, coords, slots_dev)
    own_ranks = lax.dynamic_index_in_dim(ranks, device_index, 0, keepdims=False)
    late_fits = late_most <= slots_dev - early

    split = unpack(small_params)
    rows14 = small_params[: 14 * D].reshape(14, D)
    conv_t = split["conv_first"].astype(BF).reshape(D, 9 * NT).T
    tail = jnp.stack([split["conv_second"], split["conv_third"], split["conv_fourth"]])
    taps_forward = tail.transpose(0, 3, 1, 2).reshape(3, NT, 9 * NT)
    taps_backward = tail.transpose(0, 2, 1, 3).reshape(3, NT, 9 * NT)
    tail_bias = split["conv_bias"].T
    arriving = cotangent[0].reshape(2, NT, D)
    arriving = jnp.where(swap, arriving[::-1], arriving).reshape(2 * NT, D)

    first_buffer = 0 if early else 1
    stat_parts = stat_products(stat_left, stat_right, basis_left, basis_right)
    weights, stat_parts = lax.optimization_barrier((weights, stat_parts))
    query, key_value, low, own_low, w_qkv = project(weight_codes, weights, first_buffer, seen, rows14)
    attended, logs = attend(query, key_value, key_bias)
    buffer_shapes = []
    for first, count, axes in chunks:
        shape = jax.ShapeDtypeStruct((device_count // nc * max(count, 1), BLOCK_SIDE, BLOCK_SIDE), BF)
        buffer_shapes = buffer_shapes + [shape, shape]
    (learned, grad_mixed, grad_att, vectors, grad_up_bias, grad_conv, grad_tail, grad_tail_bias), buffers = middle(
        weight_codes, targets, weights, first_buffer, buffer_shapes, attended, own, arriving, rows14, conv_t,
        taps_forward, taps_backward, tail_bias,
    )
    learned = learned.reshape(2, NT, D)
    learned = jnp.where(swap, learned[::-1], learned).reshape(2 * NT, D)

    used = [index for index in range(2) if chunks[index][1]]
    halfway = [
        reduce_core(buffers[2 * i], buffers[2 * i + 1], chunks[i][1], orders[i], sizes) for i in used
    ]
    grad_query, grad_key, grad_value = attend_back(query, key_value, key_bias, attended, logs, grad_att)
    grad_query, halfway = lax.optimization_barrier((grad_query, halfway))
    halfway = [reduce_stage(part, orders[i], 0, sizes) for i, part in zip(used, halfway)]
    late_buffers, grad_w_qkv = qkv_grads(
        targets, low, own_low, grad_query, grad_key, grad_value, list(buffers[4:]), 4
    )
    late_buffers, halfway = lax.optimization_barrier((late_buffers, halfway))
    halfway = [reduce_stage(part, orders[i], 1, sizes) for i, part in zip(used, halfway)]
    late_parts = []
    for index in range(2):
        kept, sent = late_buffers[2 * index : 2 * index + 2]
        late_parts.append(reduce_core(kept, sent, chunks[2 + index][1], orders[2 + index], sizes))
    grad_query, late_buffers = lax.optimization_barrier((grad_query, late_buffers))
    grad_seen, grad_own, sums = input_grads(seen, own, grad_query, grad_key, grad_value, w_qkv)
    late_parts, halfway, grad_seen, sums = lax.optimization_barrier((late_parts, halfway, grad_seen, sums))

    seen_frames = grad_seen.reshape(frames_seen, PAD_ROWS, D)
    long_terms = seen_frames[:frame_count].reshape(nz, nx, PAD_ROWS, D)
    late_parts = [reduce_stage(part, orders[2 + i], 0, sizes) for i, part in enumerate(late_parts)]
    reduced = [reduce_stage(part, orders[i], 2, sizes) for i, part in zip(used, halfway)]
    late_parts, reduced, long_terms = lax.optimization_barrier((late_parts, reduced, long_terms))
    late_parts = [reduce_stage(part, orders[2 + i], 1, sizes) for i, part in enumerate(late_parts)]
    late_parts, long_terms = lax.optimization_barrier((late_parts, long_terms))
    late_parts = [reduce_stage(part, orders[2 + i], 2, sizes) for i, part in enumerate(late_parts)]
    long_terms = reduce_axis(long_terms, "fx", nx, 1).astype(BF)
    late_parts, long_terms = lax.optimization_barrier((late_parts, long_terms))
    if used:
        def whole_early(early):
            extra = spread_early(targets, grad_w_qkv, buffer_shapes[:4])
            return [
                part + reduce_chunk(extra[2 * i], extra[2 * i + 1], chunks[i][1], orders[i], sizes)
                for i, part in zip(used, early)
            ]

        reduced = lax.cond(late_fits, lambda early: early, whole_early, reduced)
    owned_grads = jnp.concatenate(list(reduced) + late_parts)

    small_local = jnp.concatenate(
        [
            sums[:2].reshape(-1),
            vectors[:4].reshape(-1),
            sums[2:4].reshape(-1),
            vectors[4],
            grad_up_bias.reshape(-1),
            vectors[5],
            grad_conv.T.reshape(-1),
            grad_tail.reshape(-1),
            grad_tail_bias.T.reshape(-1),
        ]
    )
    small_total = small_local.shape[0]
    share = -(-small_total // (device_count * 128)) * 128
    padded_small = jnp.pad(small_local, (0, device_count * share - small_total))
    small_sum = padded_small.reshape(sizes + (share,))
    for axis, size in enumerate(sizes):
        small_sum = rolled(small_sum, axis, size, coords[axis])
    for axis in range(4):
        small_sum = reduce_axis(small_sum, ALL_AXES[axis], sizes[axis])
    squares = jnp.sum(owned_grads * owned_grads) + jnp.sum(small_sum * small_sum)
    carried = jnp.concatenate([small_sum, jnp.full((128,), squares, F32)])
    for axis in reversed(range(4)):
        carried = gather_axis(carried, ALL_AXES[axis], sizes[axis])
    for axis, size in enumerate(sizes):
        carried = rolled(carried, axis, size, size - coords[axis])
    carried = carried.reshape(device_count, share + 128)
    small_grad = carried[:, :share].reshape(-1)[:small_total]
    grad_norm = jnp.sqrt(jnp.sum(carried[:, share]))
    factor = 1.0 / jnp.maximum(grad_norm, CLIP_NORM)

    small_first, small_second, small_new = adam_update(
        small_grad * factor, small_params, small_moment1, small_moment2
    )

    long_terms, partner_term, factor = lax.optimization_barrier(
        (long_terms, seen_frames[frame_count + 1], factor)
    )
    long_total = reduce_axis(long_terms, "fz", nz)
    soap_out = soap(
        own_ranks, owned_grads, factor, stat_parts, master, moment1, moment2, stat_left, stat_right,
        basis_left, basis_right,
    )
    nothing = jnp.zeros_like(partner_term)
    to_previous = jnp.where(with_previous, partner_term, nothing)
    to_next = jnp.where(with_next, partner_term, nothing)
    short_total = (
        seen_frames[frame_count].astype(F32)
        + lax.ppermute(to_previous, FRAME_AXES, back_perm).astype(F32)
        + lax.ppermute(to_next, FRAME_AXES, frame_perm).astype(F32)
    )
    grad_normed_one = jnp.concatenate([long_total, short_total]) + grad_own
    hat, spread = normalized(own.astype(F32))
    grad_inputs = grad_mixed + norm_back(grad_normed_one, hat, spread, rows14[0:1])
    grad_inputs = grad_inputs.reshape(2, PAD_ROWS, D)[:, :FRAME_ROWS]
    grad_inputs = jnp.where(swap, grad_inputs[::-1], grad_inputs).reshape(2 * FRAME_ROWS, D)
    return (
        learned[None],
        grad_inputs[None],
        soap_out[0],
        soap_out[1],
        soap_out[2],
        soap_out[3],
        soap_out[4],
        soap_out[5],
        soap_out[6],
        small_first,
        small_second,
        small_new,
        grad_norm,
    )


def solution(mesh):
    frames, batches = mesh.shape["frame"], mesh.shape["batch"]
    split = Mesh(mesh.devices.reshape(frames // 2, 2, batches // 2, 2), ALL_AXES)
    batch = ("by", "core")
    slots = P(ALL_AXES, None, None)
    rows = P(batch, FRAME_AXES, None)
    return jax.shard_map(
        on_device,
        mesh=split,
        in_specs=(rows, rows, P(batch, None), P(batch, None), P()) + (slots,) * 7 + (P(),) * 3,
        out_specs=(rows, rows) + (slots,) * 7 + (P(),) * 4,
        check_vma=False,
    )
```

```python
import math

import jax
import jax.numpy as jnp
import numpy as np
from jax import lax
from jax.experimental import pallas as pl
from jax.experimental.pallas import tpu as pltpu
from jax.sharding import Mesh
from jax.sharding import PartitionSpec as P

D = 768
HEADS = 12
HD = 64
FF = 3072
GRID = 14
NT = 8
BLOCK_SIDE = 128
STEP = 10
MATRIX_BLOCKS = 432


FULL_PRECISION = lax.Precision.HIGHEST
NORM_EPSILON = 1e-06
BETA_ONE = 0.9
BETA_TWO = 0.95
STAT_DECAY = 0.95
LEARN_RATE = 0.1
WEIGHT_DECAY = 0.01
ADAM_EPSILON = 1e-08
CLIP_NORM = 1.0
MASK_FLOOR = -1e30


def layout():
    return [
        ("gain_one", (D,)),
        ("shift_one", (D,)),
        ("gain_two", (D,)),
        ("shift_two", (D,)),
        ("gain_three", (D,)),
        ("shift_three", (D,)),
        ("bias_query", (D,)),
        ("bias_value", (D,)),
        ("bias_out", (D,)),
        ("bias_up", (FF,)),
        ("bias_down", (D,)),
        ("conv_first", (D, 9, NT)),
        ("conv_second", (9, NT, NT)),
        ("conv_third", (9, NT, NT)),
        ("conv_fourth", (9, NT, NT)),
        ("conv_bias", (4, NT)),
    ]


def unpack(vector):
    params_split = {}
    offset = 0
    for part_name, part_shape in layout():
        entries = math.prod(part_shape)
        params_split[part_name] = vector[offset : offset + entries].reshape(part_shape)
        offset = offset + entries
    return params_split


def matrix_shapes():
    return [(D, 3 * D), (D, D), (D, FF), (FF, D)]


def to_blocks(matrix):
    row_count, col_count = matrix.shape
    tiled = matrix.reshape(row_count // BLOCK_SIDE, BLOCK_SIDE, col_count // BLOCK_SIDE, BLOCK_SIDE)
    return tiled.transpose(0, 2, 1, 3).reshape(-1, BLOCK_SIDE, BLOCK_SIDE)


def from_blocks(blocks):
    matrices = []
    offset = 0
    for row_count, col_count in matrix_shapes():
        tiles = row_count // BLOCK_SIDE * (col_count // BLOCK_SIDE)
        piece_tiles = blocks[offset : offset + tiles].reshape(
            row_count // BLOCK_SIDE, col_count // BLOCK_SIDE, BLOCK_SIDE, BLOCK_SIDE
        )
        matrices.append(piece_tiles.transpose(0, 2, 1, 3).reshape(row_count, col_count))
        offset = offset + tiles
    return matrices


def layer_norm(values, gain_vec, shift_vec):
    centre = jnp.mean(values, -1, keepdims=True)
    centered = values - centre
    spread = jnp.mean(centered * centered, -1, keepdims=True)
    return centered * lax.rsqrt(spread + NORM_EPSILON) * gain_vec + shift_vec


def gelu_exact(values):
    return jax.nn.gelu(values, approximate=False)


def taps_sum(taps):
    padded = jnp.pad(taps, ((0, 0), (1, 1), (1, 1), (0, 0), (0, 0)))
    summed = jnp.zeros(taps.shape[:3] + taps.shape[4:], taps.dtype)
    for tap_index in range(9):
        row_off = tap_index // 3 - 1
        col_off = tap_index % 3 - 1
        summed = (
            summed
            + padded[
                :, 1 + row_off : 1 + row_off + GRID, 1 + col_off : 1 + col_off + GRID, tap_index
            ]
        )
    return summed


def taps_back(grads):
    padded = jnp.pad(grads, ((0, 0), (1, 1), (1, 1), (0, 0)))
    shifted = []
    for tap_index in range(9):
        row_off = tap_index // 3 - 1
        col_off = tap_index % 3 - 1
        shifted.append(
            padded[:, 1 - row_off : 1 - row_off + GRID, 1 - col_off : 1 - col_off + GRID]
        )
    return jnp.stack(shifted, axis=3)


def conv_small(values, weight):
    taps = jnp.einsum("fyxc,tco->fyxto", values, weight, precision=FULL_PRECISION)
    return taps_sum(taps)


def learner_tail(first_pre, values, second_w, third_w, fourth_w, tail_bias):
    frames = first_pre.shape[0]
    act_one = gelu_exact(first_pre)
    act_two = gelu_exact(conv_small(act_one, second_w) + tail_bias[0])
    act_three = gelu_exact(conv_small(act_two, third_w) + tail_bias[1])
    maps = jax.nn.sigmoid(conv_small(act_three, fourth_w) + tail_bias[2])
    grid_values = values.reshape(frames, GRID, GRID, values.shape[-1])
    pooled = jnp.einsum("fyxk,fyxd->fkd", maps, grid_values, precision=FULL_PRECISION)
    return pooled.reshape(frames * NT, values.shape[-1])


def clip_segments(lengths, order_row, group_frames, frames_dev, frame_count):
    clip_ids = jnp.arange(lengths.shape[0], dtype=jnp.int32)
    ordered_len = jnp.sum(
        jnp.where(order_row[:, None] == clip_ids[None, :], lengths[None, :], 0), 1
    )
    ends = jnp.cumsum(ordered_len)
    slots = jnp.arange(group_frames, dtype=jnp.int32)
    places = slots % frames_dev * frame_count + slots // frames_dev
    return jnp.sum((ends[None, :] <= places[:, None]).astype(jnp.int32), 1)


F32=jnp.float32; BF=jnp.bfloat16
NN=(((1,),(0,)),((),()))
NT_=(((1,),(1,)),((),()))
TN=(((0,),(0,)),((),()))

def halves(a):
    high = a.astype(BF)
    return high, (a - high.astype(F32)).astype(BF)

def dot_low(a, b, dims):
    return lax.dot_general(a, b, dims, preferred_element_type=F32)

def dot_parts(a, b, dims):
    ah, al = a
    bh, bl = b
    return dot_low(ah, bh, dims) + (dot_low(ah, bl, dims) + dot_low(al, bh, dims))

def dot_wide(a, b, dims):
    return dot_parts(halves(a), halves(b), dims)

def slots_step(n):
    return 7 if n % 7 == 0 else 2 if n % 2 == 0 else 1


def stat_products(sl, sr, bl, br):
    n = sl.shape[0]
    many = slots_step(n)
    spec = pl.BlockSpec((many, BLOCK_SIDE, BLOCK_SIDE), lambda i: (i, 0, 0))

    def kernel(sl, sr, bl, br, out_left, out_right):
        for s in range(many):
            out_left[s] = STAT_DECAY * dot_wide(bl[s], sl[s], TN)
            out_right[s] = STAT_DECAY * dot_wide(br[s], sr[s], TN)

    return pl.pallas_call(
        kernel,
        grid=(n // many,),
        in_specs=[spec] * 4,
        out_specs=[spec] * 2,
        out_shape=[jax.ShapeDtypeStruct(sl.shape, F32)] * 2,
        cost_estimate=about(7),
    )(sl, sr, bl, br)


def raw_products(ranks, g, bl, br):
    n = g.shape[0]
    many = slots_step(n)
    here = pl.BlockSpec((many, BLOCK_SIDE, BLOCK_SIDE), lambda i, ranks: (i, 0, 0))

    def ranked(s):
        return pl.BlockSpec((1, BLOCK_SIDE, BLOCK_SIDE), lambda i, ranks: (ranks[i * many + s], 0, 0))

    def kernel(ranks, *refs):
        grads, (bl, br, rot, gl, gr, ql, qr) = refs[:many], refs[many:]
        each = range(many)
        gp = [halves(grads[s][0]) for s in each]
        blp, brp = [halves(bl[s]) for s in each], [halves(br[s]) for s in each]
        u = [halves(dot_parts(blp[s], gp[s], TN)) for s in each]
        v = [halves(dot_parts(gp[s], brp[s], NN)) for s in each]
        for s in each:
            gl[s] = dot_parts(gp[s], gp[s], NT_)
        for s in each:
            gr[s] = dot_parts(gp[s], gp[s], TN)
        for s in each:
            rot[s] = dot_parts(u[s], brp[s], NN)
        for s in each:
            ql[s] = dot_parts(u[s], gp[s], NT_)
        for s in each:
            qr[s] = dot_parts(v[s], gp[s], TN)

    return pl.pallas_call(
        kernel,
        grid_spec=pltpu.PrefetchScalarGridSpec(
            num_scalar_prefetch=1,
            grid=(n // many,),
            in_specs=[ranked(s) for s in range(many)] + [here, here],
            out_specs=[here] * 5,
        ),
        out_shape=[jax.ShapeDtypeStruct(g.shape, F32)] * 5,
        cost_estimate=about(8),
    )(ranks, *([g] * many), bl, br)


NB=32
def tall(parts, order):
    return jnp.concatenate([parts[which] for which in order], axis=0)


def wide(parts, order):
    return jnp.concatenate([parts[which] for which in order], axis=1)


def finish_kernel(factor, *refs):
    inputs, refs = refs[:14], refs[14:]
    results, refs = refs[:7], refs[7:]
    held, made = refs[:14], refs[14:21]
    work, elim, load_sems, store_sems = refs[21:]
    p_l, p_r, ql, qr, rot, gl, gr, sl, sr, bl, br, master, m1, m2 = held
    o_master, o_m1, o_m2, o_left, o_right, o_bl, o_br = made
    for index in range(14):
        pltpu.make_async_copy(inputs[index], held[index], load_sems.at[index]).start()

    def ready(*indices):
        for index in indices:
            pltpu.make_async_copy(inputs[index], held[index], load_sems.at[index]).wait()

    def store(*indices):
        for index in indices:
            pltpu.make_async_copy(made[index], results[index], store_sems.at[index]).start()

    n = rot.shape[0]
    count = 2 * n
    f = factor[0]
    f2 = (1.0 - STAT_DECAY) * f * f
    ready(0, 1, 2, 3)
    group = 7 if n % 7 == 0 else n
    for start in range(0, n, group):
        members = range(start, start + group)
        sums = [p_[s] + f2 * q_[s] for s in members for p_, q_ in ((p_l, ql), (p_r, qr))]
        parts = [halves(at) for at in sums]
        grams = [dot_parts(atp, atp, NT_) for atp in parts]
        for i in range(2 * group):
            work[2 * start + i, :, BLOCK_SIDE:] = sums[i]
            work[2 * start + i, :, :BLOCK_SIDE] = grams[i]

    rows = lax.broadcasted_iota(jnp.int32, (1, 8, 2 * NB), 1)
    lanes = lax.broadcasted_iota(jnp.int32, (1, 8, 2 * NB), 2)
    panels = BLOCK_SIDE // NB
    tile_count = NB // 8

    def panel(p, carry):
        for q in range(panels):
            @pl.when(p == q)
            def _(q=q):
                for t in range(tile_count):
                    block = work[:, NB * q + 8 * t : NB * q + 8 * t + 8, NB * q : NB * q + NB]
                    eye = jnp.where(lanes - NB == rows + 8 * t, 1.0, 0.0).astype(F32)
                    eye = jnp.broadcast_to(eye, (count, 8, 2 * NB))
                    elim[:, 8 * t : 8 * t + 8, :] = jnp.concatenate([block, eye[:, :, NB:]], axis=2)
        tiles = [elim[:, 8 * t : 8 * t + 8, :] for t in range(tile_count)]
        for k in range(NB):
            t0, j = divmod(k, 8)
            columns = [jnp.broadcast_to(tiles[t][:, :, k : k + 1], tiles[t].shape) for t in range(t0, tile_count)]
            row = tiles[t0][:, j : j + 1, :] * (1.0 / columns[0][:, j : j + 1, :])
            for t in range(t0, tile_count):
                new = tiles[t] - columns[t - t0] * row
                if t == t0:
                    new = jnp.where(rows > j, new, tiles[t])
                tiles[t] = new
        for t in range(tile_count):
            pivots = jnp.sum(jnp.where(lanes == rows + 8 * t, tiles[t], 0.0), axis=2, keepdims=True)
            elim[:, 8 * t : 8 * t + 8, :] = tiles[t] * lax.rsqrt(pivots)
        for q in range(panels):
            @pl.when(p == q)
            def _(q=q):
                lo, hi = NB * q, NB * q + NB
                for start in range(0, count, group):
                    members = range(start, start + group)
                    inverses = [wide(halves(elim[m, :, NB:]), (0, 0, 1)) for m in members]
                    sources = [tall(halves(work[m, lo:hi, :]), (0, 1, 0)) for m in members]
                    solved = [dot_low(inverses[i], sources[i], NN) for i in range(group)]
                    for i, m in enumerate(members):
                        (o_bl if m % 2 == 0 else o_br)[m // 2, lo:hi, :] = solved[i][:, BLOCK_SIDE:]
                    if hi < BLOCK_SIDE:
                        parts = [halves(y) for y in solved]
                        updates = [
                            dot_low(tall(yp, (0, 0, 1))[:, :BLOCK_SIDE], tall(yp, (0, 1, 0)), TN) for yp in parts
                        ]
                        for i, m in enumerate(members):
                            work[m, hi:, :] = work[m, hi:, :] - updates[i][hi:]
        return carry

    lax.fori_loop(0, panels, panel, 0)

    ready(4, 5, 6, 7, 8, 9, 10, 11, 12, 13)
    for start in range(0, n, group):
        members = range(start, start + group)
        firsts, directions = [], []
        for s in members:
            r = f * rot[s]
            m = BETA_ONE * m1[s] + (1.0 - BETA_ONE) * r
            v = BETA_TWO * m2[s] + (1.0 - BETA_TWO) * r * r
            o_m2[s] = v
            o_left[s] = STAT_DECAY * sl[s] + f2 * gl[s]
            o_right[s] = STAT_DECAY * sr[s] + f2 * gr[s]
            firsts.append(halves(m))
            directions.append(
                halves(m / (1.0 - BETA_ONE**STEP) / (jnp.sqrt(v / (1.0 - BETA_TWO**STEP)) + ADAM_EPSILON))
            )
        old_left = [halves(bl[s]) for s in members]
        old_right = [halves(br[s]) for s in members]
        new_left = [o_bl[s] for s in members]
        new_right = [o_br[s] for s in members]
        each = range(group)
        backs = [halves(dot_parts(old_left[i], directions[i], NN)) for i in each]
        turns_left = [halves(dot_parts(halves(new_left[i]), old_left[i], NN)) for i in each]
        turns_right = [halves(dot_parts(halves(new_right[i]), old_right[i], NN)) for i in each]
        returned = [dot_parts(backs[i], old_right[i], NT_) for i in each]
        parts = [halves(dot_parts(turns_left[i], firsts[i], NN)) for i in each]
        moved_firsts = [dot_parts(parts[i], turns_right[i], NT_) for i in each]
        for i, s in enumerate(members):
            o_master[s] = master[s] - LEARN_RATE * (returned[i] + WEIGHT_DECAY * master[s])
            o_m1[s] = moved_firsts[i]
            o_bl[s] = new_left[i].T
            o_br[s] = new_right[i].T
    store(0, 1, 2, 3, 4, 5, 6)
    for index in range(7):
        pltpu.make_async_copy(made[index], results[index], store_sems.at[index]).wait()


def finish(factor, rot, gl, gr, ql, qr, p_l, p_r, sl, sr, bl, br, master, m1, m2):
    n = rot.shape[0]
    shape = jax.ShapeDtypeStruct(rot.shape, F32)
    hbm = pl.BlockSpec(memory_space=pl.ANY)
    block = pltpu.VMEM((n, BLOCK_SIDE, BLOCK_SIDE), F32)
    return pl.pallas_call(
        finish_kernel,
        in_specs=[pl.BlockSpec(memory_space=pltpu.SMEM)] + [hbm] * 14,
        out_specs=[hbm] * 7,
        out_shape=[shape] * 7,
        scratch_shapes=[block] * 21
        + [
            pltpu.VMEM((2 * n, BLOCK_SIDE, 2 * BLOCK_SIDE), F32),
            pltpu.VMEM((2 * n, NB, 2 * NB), F32),
            pltpu.SemaphoreType.DMA((14,)),
            pltpu.SemaphoreType.DMA((7,)),
        ],
        compiler_params=pltpu.CompilerParams(vmem_limit_bytes=56 * 1024 * 1024),
        cost_estimate=about(30),
    )(factor, p_l, p_r, ql, qr, rot, gl, gr, sl, sr, bl, br, master, m1, m2)


def adam_update(clipped, params_old, first_old, second_old):
    first_new = BETA_ONE * first_old + (1.0 - BETA_ONE) * clipped
    second_new = BETA_TWO * second_old + (1.0 - BETA_TWO) * clipped * clipped
    stepped = (
        first_new
        / (1.0 - BETA_ONE**STEP)
        / (jnp.sqrt(second_new / (1.0 - BETA_TWO**STEP)) + ADAM_EPSILON)
    )
    return (first_new, second_new, params_old - LEARN_RATE * stepped)


FRAME_ROWS = GRID * GRID
PAD_ROWS = 208
OWN_ROWS = 2 * PAD_ROWS
LANES = 512
PAIRS = HEADS // 2
PAIR = 2 * HD
QKV_BLOCKS = 108
CODE_BASE = 1 << 16
UP_ROWS = (D + FF) // BLOCK_SIDE
BLANK_ROW = (D + 2 * FF) // BLOCK_SIDE
ALL_ROWS = BLANK_ROW * BLOCK_SIDE
VMEM_MOST = 58 * 1024 * 1024
ALL_AXES = ("fz", "fx", "by", "core")
FRAME_AXES = ("fz", "fx")
TAP_OFFSETS = [(tap // 3 - 1) * GRID + tap % 3 - 1 for tap in range(9)]


def about(microseconds):
    return pl.CostEstimate(flops=0, bytes_accessed=int(microseconds * 3e6), transcendentals=0)


def in_vmem():
    return pl.BlockSpec(memory_space=pltpu.VMEM)


def anywhere():
    return pl.BlockSpec(memory_space=pl.ANY)


def matrix_places():
    places = []
    first = 0
    for row_count, col_count in matrix_shapes():
        cols = col_count // BLOCK_SIDE
        count = row_count // BLOCK_SIDE * cols
        places.append((first, count, cols))
        first = first + count
    return places


def tile_at(ref, row, col):
    row = pl.multiple_of(row * BLOCK_SIDE, BLOCK_SIDE)
    col = pl.multiple_of(col * BLOCK_SIDE, BLOCK_SIDE)
    return ref.at[pl.ds(row, BLOCK_SIDE), pl.ds(col, BLOCK_SIDE)]


def tile_of(matrix, code):
    return tile_at(matrix, lax.bitwise_and(lax.shift_right_logical(code, 5), 63), lax.bitwise_and(code, 31))


def load_blocks(tiles, buffers, matrix, sems, matrices, base=0, count=None):
    for buffer in buffers:
        def one_load(place, carry, buffer=buffer, base=base):
            code = tiles[base + place]
            which = lax.shift_right_logical(code, 11)

            @pl.when(which < matrices)
            def _():
                pltpu.make_async_copy(buffer.at[place], tile_of(matrix, code), sems.at[which]).start()

            return carry

        if count is None:
            lax.fori_loop(0, buffer.shape[0], one_load, 0, unroll=4)
        else:
            lax.fori_loop(0, count, one_load, 0)
        base = base + buffer.shape[0]


def wait_whole(ref, sem):
    pltpu.make_async_copy(ref, ref, sem).wait()


def send_tile(code, buffers, tile, sem, first=0):
    for index, buffer in enumerate(buffers):
        @pl.when(lax.div(code, CODE_BASE) == first + index)
        def _():
            pltpu.make_async_copy(tile, buffer.at[lax.rem(code, CODE_BASE)], sem).start()


def normalized(values):
    centered = values - jnp.mean(values, -1, keepdims=True)
    spread = lax.rsqrt(jnp.mean(centered * centered, -1, keepdims=True) + NORM_EPSILON)
    return centered * spread, spread


def norm_back(grad, hat, spread, gain):
    scaled = grad * gain
    return spread * (
        scaled
        - jnp.mean(scaled, -1, keepdims=True)
        - hat * jnp.mean(scaled * hat, -1, keepdims=True)
    )


def project(tiles, early, buffers, early_buffers, seen, rows14):
    rows = seen.shape[0]
    steps = rows // OWN_ROWS
    count = len(buffers)

    def kernel(tiles, early, *refs):
        sources = refs[:count]
        seen, rows14, q, kv, low, own_low, w_qkv, sems = refs[count:]
        step = pl.program_id(0)

        @pl.when(step == 0)
        def _():
            base = 0
            if early_buffers:
                load_blocks(tiles, sources[:1], w_qkv, sems, 1, 0, early[0])
                base = sources[0].shape[0]
            load_blocks(tiles, sources[early_buffers:], w_qkv, sems, 1, base)

        hat, _ = normalized(seen[...].astype(F32))
        normed = (hat * rows14[0:1] + rows14[1:2]).astype(BF)
        low[...] = normed

        @pl.when(step == 0)
        def _():
            wait_whole(w_qkv, sems.at[0])

        kv[:, :D] = dot_low(normed, w_qkv[:, D : 2 * D], NN).astype(BF)
        kv[:, D:] = (dot_low(normed, w_qkv[:, 2 * D :], NN) + rows14[7:8]).astype(BF)

        def own(place):
            part = normed[:PAD_ROWS]
            query = (dot_low(part, w_qkv[:, :D], NN) + rows14[6:7]).astype(BF)
            q[place : place + PAD_ROWS] = query * jnp.asarray(1.0 / math.sqrt(HD), BF)
            own_low[place : place + PAD_ROWS] = part

        @pl.when(step == 0)
        def _():
            own(0)

        @pl.when(step == steps - 1)
        def _():
            own(PAD_ROWS)

    def whole(shape):
        return pl.BlockSpec(shape, lambda i, tiles, early: (0, 0))

    def moving(width):
        return pl.BlockSpec((OWN_ROWS, width), lambda i, tiles, early: (i, 0))

    return pl.pallas_call(
        kernel,
        grid_spec=pltpu.PrefetchScalarGridSpec(
            num_scalar_prefetch=2,
            grid=(steps,),
            in_specs=[anywhere()] * count + [moving(D), whole((14, D))],
            out_specs=[whole((OWN_ROWS, D)), moving(2 * D), moving(D), whole((OWN_ROWS, D)), whole((D, 3 * D))],
            scratch_shapes=[pltpu.SemaphoreType.DMA((1,))],
        ),
        out_shape=[
            jax.ShapeDtypeStruct((OWN_ROWS, D), BF),
            jax.ShapeDtypeStruct((rows, 2 * D), BF),
            jax.ShapeDtypeStruct((rows, D), BF),
            jax.ShapeDtypeStruct((OWN_ROWS, D), BF),
            jax.ShapeDtypeStruct((D, 3 * D), BF),
        ],
        compiler_params=pltpu.CompilerParams(vmem_limit_bytes=VMEM_MOST),
        cost_estimate=about(15),
    )(tiles, early, *buffers, seen, rows14)


ROW_STEP = 16


def stacked(values):
    first = lax.broadcasted_iota(jnp.int32, (1, PAIR), 1) < HD
    nothing = jnp.zeros_like(values)
    return jnp.concatenate([jnp.where(first, values, nothing), jnp.where(first, nothing, values)], axis=0)


def unstacked(values):
    first = lax.broadcasted_iota(jnp.int32, (1, PAIR), 1) < HD
    return jnp.where(first, values[:PAD_ROWS], values[PAD_ROWS:])


def attend_kernel(long_rows, q, k, v, bias, out, logs, scores, soft):
    total = k.shape[0]
    for frame, (lo, hi) in enumerate(((0, long_rows), (long_rows, total))):
        rows = slice(frame * PAD_ROWS, (frame + 1) * PAD_ROWS)
        width = hi - lo
        scores[:, :width] = dot_low(stacked(q[rows, :]), k[lo:hi, :], NT_)
        norms, peaks = [], []
        for row in range(0, OWN_ROWS, ROW_STEP):
            block = scores[row : row + ROW_STEP, :width] + bias[:, lo:hi]
            peak = jnp.max(block, axis=1, keepdims=True)
            weights = jnp.exp(block - peak)
            norms.append(jnp.sum(weights, axis=1, keepdims=True))
            peaks.append(peak)
            soft[row : row + ROW_STEP, :width] = weights.astype(BF)
        norm = jnp.concatenate(norms, axis=0)
        out[rows, :] = unstacked(dot_low(soft[:, :width], v[lo:hi, :], NN) / norm).astype(BF)
        logs[rows, :] = unstacked(jnp.broadcast_to(jnp.concatenate(peaks, axis=0) + jnp.log(norm), (OWN_ROWS, PAIR)))


def attend_back_kernel(long_rows, q, k, v, bias, out, logs, grad, dq, dk, dv, scores, soft_grads, soft, changes):
    total = k.shape[0]
    for frame, (lo, hi) in enumerate(((0, long_rows), (long_rows, total))):
        rows = slice(frame * PAD_ROWS, (frame + 1) * PAD_ROWS)
        width = hi - lo
        query, arriving = stacked(q[rows, :]), stacked(grad[rows, :])
        products = stacked(grad[rows, :].astype(F32) * out[rows, :].astype(F32))
        delta = jnp.sum(products, axis=1, keepdims=True)
        log = jnp.concatenate([logs[rows, 0:1], logs[rows, HD : HD + 1]], axis=0)
        scores[:, :width] = dot_low(query, k[lo:hi, :], NT_)
        soft_grads[:, :width] = dot_low(arriving, v[lo:hi, :], NT_)
        for row in range(0, OWN_ROWS, ROW_STEP):
            here = slice(row, row + ROW_STEP)
            weights = jnp.exp(scores[here, :width] + bias[:, lo:hi] - log[here])
            soft[here, :width] = weights.astype(BF)
            changes[here, :width] = (weights * (soft_grads[here, :width] - delta[here])).astype(BF)
        part = unstacked(dot_low(changes[:, :width], k[lo:hi, :], NN))
        dq[rows, :] = (part * (1.0 / math.sqrt(HD))).astype(BF)
        dk[lo:hi, :] = dot_low(query, changes[:, :width], TN).T.astype(BF)
        dv[lo:hi, :] = dot_low(arriving, soft[:, :width], TN).T.astype(BF)


def pair_spec(rows, offset=0):
    return pl.BlockSpec((rows, PAIR), lambda i: (0, i + offset))


def attend(q, kv, bias):
    keys_total = kv.shape[0]
    long_rows = keys_total - OWN_ROWS

    def kernel(*refs):
        attend_kernel(long_rows, *refs)

    return pl.pallas_call(
        kernel,
        grid=(PAIRS,),
        in_specs=[
            pair_spec(OWN_ROWS),
            pair_spec(keys_total),
            pair_spec(keys_total, PAIRS),
            pl.BlockSpec((1, keys_total), lambda i: (0, 0)),
        ],
        out_specs=[pair_spec(OWN_ROWS)] * 2,
        out_shape=[jax.ShapeDtypeStruct((OWN_ROWS, D), BF), jax.ShapeDtypeStruct((OWN_ROWS, D), F32)],
        scratch_shapes=[pltpu.VMEM((OWN_ROWS, long_rows), F32), pltpu.VMEM((OWN_ROWS, long_rows), BF)],
        compiler_params=pltpu.CompilerParams(vmem_limit_bytes=VMEM_MOST),
        cost_estimate=about(12),
    )(q, kv, kv, bias.reshape(1, -1))


def attend_back(pairs, before, q, kv, bias, out, logs, grad):
    keys_total = kv.shape[0]
    long_rows = keys_total - OWN_ROWS
    start, count = pairs

    def kernel(*refs):
        attend_back_kernel(long_rows, *refs[:7], *refs[7 + len(before) :])

    def spec(rows, offset=0):
        return pair_spec(rows, offset + start)

    return pl.pallas_call(
        kernel,
        grid=(count,),
        in_specs=[
            spec(OWN_ROWS),
            spec(keys_total),
            spec(keys_total, PAIRS),
            pl.BlockSpec((1, keys_total), lambda i: (0, 0)),
            spec(OWN_ROWS),
            spec(OWN_ROWS),
            spec(OWN_ROWS),
        ]
        + [anywhere()] * len(before),
        out_specs=[spec(OWN_ROWS), spec(keys_total), spec(keys_total)],
        out_shape=[
            jax.ShapeDtypeStruct((OWN_ROWS, D), BF),
            jax.ShapeDtypeStruct((keys_total, D), BF),
            jax.ShapeDtypeStruct((keys_total, D), BF),
        ],
        scratch_shapes=[pltpu.VMEM((OWN_ROWS, long_rows), F32)] * 2 + [pltpu.VMEM((OWN_ROWS, long_rows), BF)] * 2,
        input_output_aliases={7 + i: i for i in range(len(before))},
        compiler_params=pltpu.CompilerParams(vmem_limit_bytes=VMEM_MOST),
        cost_estimate=about(4 * count),
    )(q, kv, kv, bias.reshape(1, -1), out, logs, grad, *before)


def lane_masks():
    lane = np.arange(LANES)
    inner = lane % PAD_ROWS
    token = (lane < OWN_ROWS) & (inner < FRAME_ROWS)
    row, col = inner // GRID, inner % GRID
    masks = []
    for tap in range(9):
        far_row, far_col = row + tap // 3 - 1, col + tap % 3 - 1
        masks.append(token & (far_row >= 0) & (far_row < GRID) & (far_col >= 0) & (far_col < GRID))
    masks.append(token & (lane < PAD_ROWS))
    masks.append(token & (lane >= PAD_ROWS))
    masks = masks + [np.zeros(LANES, bool)] * (16 - len(masks))
    return np.stack(masks).astype(np.float32)


def ahead(values, offset):
    return values if offset == 0 else pltpu.roll(values, (-offset) % LANES, axis=1)


def cumulative(values):
    return 0.5 + 0.5 * lax.erf(values * math.sqrt(0.5))


def gelu_slope(values, portion):
    return portion + values * jnp.exp(-0.5 * values * values) * (1.0 / math.sqrt(2.0 * math.pi))


def column_sum(values):
    return jnp.sum(values, axis=0, keepdims=True)


def widened(values):
    return jnp.concatenate([values, jnp.zeros((values.shape[0], LANES - OWN_ROWS), values.dtype)], axis=1)


def wait_tiles(matrix, count, sem):
    side = D // BLOCK_SIDE
    rest = count
    while rest >= side:
        rows = min(rest // side, BLANK_ROW)
        wait_whole(matrix.at[: rows * BLOCK_SIDE], sem)
        rest = rest - rows * side
    for _ in range(rest):
        wait_whole(tile_at(matrix, 0, 0), sem)


def middle_kernel(weight_count, first_buffer, held_tiles, sent_tiles, targets, *refs):
    sources = refs[:weight_count]
    (
        att, own, cot, rows14, conv_t, taps_forward, taps_backward, tail_bias, masks,
        learned, grad_mixed, grad_att, vectors, grad_up_bias, grad_conv, grad_tail, grad_tail_bias,
    ) = refs[weight_count : weight_count + 17]
    buffers = refs[weight_count + 17 : -10]
    (
        w_all, d_all, activated, slopes, normed, hat_two, mixed, gathered_sum, load_sems, send_sems,
    ) = refs[-10:]
    chunks = FF // D
    side = D // BLOCK_SIDE
    w_out = w_all.at[:D]
    w_up = [w_all.at[(1 + chunk) * D : (2 + chunk) * D] for chunk in range(chunks)]
    w_down = [w_all.at[(1 + chunks + chunk) * D : (2 + chunks + chunk) * D] for chunk in range(chunks)]
    d_out = d_all.at[:D]
    d_up = [d_all.at[(1 + chunk) * D : (2 + chunk) * D] for chunk in range(chunks)]
    d_down = [d_all.at[(1 + chunks + chunk) * D : (2 + chunks + chunk) * D] for chunk in range(chunks)]

    load_blocks(held_tiles, sources, w_all, load_sems, 3)
    d_all[ALL_ROWS:, :BLOCK_SIDE] = jnp.zeros((BLOCK_SIDE, BLOCK_SIDE), BF)
    wait_whole(w_out, load_sems.at[0])
    start = own[...].astype(F32) + dot_low(att[...], w_out[...], NN) + rows14[8:9]
    mixed[...] = start
    hat, spread_two = normalized(start)
    hat_two[...] = hat
    normed[...] = (hat * rows14[2:3] + rows14[3:4]).astype(BF)
    gathered_sum[...] = start + rows14[13:14]
    wait_whole(w_all.at[D : D + FF], load_sems.at[1])
    wait_whole(w_all.at[D + FF : D + 2 * FF], load_sems.at[2])

    for chunk in range(chunks):
        hidden = dot_low(normed[...], w_up[chunk][...], NN) + rows14[9 + chunk : 10 + chunk]
        portion = cumulative(hidden)
        active = (hidden * portion).astype(BF)
        activated[chunk] = active
        slopes[chunk] = gelu_slope(hidden, portion)
        gathered_sum[...] += dot_low(active, w_down[chunk][...], NN)

    out_two = gathered_sum[...]
    hat, spread_three = normalized(out_two)
    low_three = (hat * rows14[4:5] + rows14[5:6]).astype(BF)

    taps = widened(dot_low(conv_t[...], low_three, NT_))
    first = tail_bias[:, 0:1]
    for tap in range(9):
        first = first + ahead(taps[NT * tap : NT * (tap + 1)], TAP_OFFSETS[tap]) * masks[tap : tap + 1]

    def around(values, sign):
        order = range(9) if sign > 0 else range(8, -1, -1)
        return jnp.concatenate(
            [
                ahead(values, sign * TAP_OFFSETS[tap]) * masks[seen : seen + 1]
                for tap, seen in zip(range(9), order)
            ],
            axis=0,
        )

    before, stacks, portions = [first], [], []
    for layer in range(3):
        portions.append(cumulative(before[-1]))
        stacks.append(around(before[-1] * portions[-1], 1))
        before.append(dot_wide(taps_forward[layer], stacks[-1], NN) + tail_bias[:, layer + 1 : layer + 2])
    maps = 1.0 / (1.0 + jnp.exp(-before[3]))
    both = jnp.concatenate([maps * masks[9:10], maps * masks[10:11]], axis=0)[:, :OWN_ROWS]
    both = halves(both)
    out_parts = halves(out_two)
    arriving = cot[...]
    learned[...] = dot_parts(both, out_parts, NN)
    seen_maps = widened(dot_low(arriving, out_parts[0], NT_) + dot_low(arriving, out_parts[1], NT_))
    grad = (seen_maps[:NT] * masks[9:10] + seen_maps[NT:] * masks[10:11]) * maps * (1.0 - maps)
    sums = [None] * 4
    for layer in (2, 1, 0):
        sums[layer + 1] = jnp.sum(grad, axis=1, keepdims=True)
        grad_tail[layer] = dot_wide(stacks[layer], grad, NT_)
        grad = dot_wide(taps_backward[layer], around(grad, -1), NN)
        grad = grad * gelu_slope(before[layer], portions[layer])
    grad = grad.astype(BF).astype(F32)
    sums[0] = jnp.sum(grad, axis=1, keepdims=True)
    grad_tail_bias[...] = jnp.concatenate(sums, axis=1)
    grad_taps = around(grad, -1)[:, :OWN_ROWS].astype(BF)
    grad_conv[...] = dot_low(grad_taps, low_three, NN)
    grad_norm_three = dot_low(grad_taps, conv_t[...], TN)
    vectors[2:3] = column_sum(grad_norm_three * hat)
    vectors[3:4] = column_sum(grad_norm_three)
    grad_out = (
        norm_back(grad_norm_three, hat, spread_three, rows14[4:5])
        + dot_low(both[0], arriving, TN)
        + dot_low(both[1], arriving, TN)
    )
    grad_down = grad_out.astype(BF)
    vectors[5:6] = column_sum(grad_down.astype(F32))

    for chunk in range(chunks):
        grad_active = dot_low(grad_down, w_down[chunk][...], NT_)
        grad_hidden = (grad_active * slopes[chunk]).astype(BF)
        grad_up_bias[chunk : chunk + 1] = column_sum(grad_hidden.astype(F32))
        part = dot_low(grad_hidden, w_up[chunk][...], NT_)
        if chunk == 0:
            gathered_sum[...] = part
        else:
            gathered_sum[...] += part
        d_down[chunk][...] = dot_low(activated[chunk], grad_down, TN).astype(BF)
        d_up[chunk][...] = dot_low(normed[...], grad_hidden, TN).astype(BF)

    base = 0
    for buffer in buffers:
        def one_tile(place, carry, buffer=buffer, base=base):
            code = sent_tiles[base + place]

            @pl.when(code >= 2048)
            def _():
                pltpu.make_async_copy(tile_of(d_all, code), buffer.at[place], send_sems.at[1]).start()

            return carry

        lax.fori_loop(0, buffer.shape[0], one_tile, 0, unroll=4)
        base = base + buffer.shape[0]

    grad_norm_two = gathered_sum[...]
    vectors[0:1] = column_sum(grad_norm_two * hat_two[...])
    vectors[1:2] = column_sum(grad_norm_two)
    total = grad_out + norm_back(grad_norm_two, hat_two[...], spread_two, rows14[2:3])
    grad_mixed[...] = total
    branch = total.astype(BF)
    vectors[4:5] = column_sum(branch.astype(F32))
    d_out[...] = dot_low(att[...], branch, TN).astype(BF)

    def one_out(tile, carry):
        code = targets[matrix_places()[1][0] + tile]
        send_tile(code, buffers, tile_at(d_out, lax.div(tile, side), lax.rem(tile, side)), send_sems.at[0], first_buffer)
        return carry

    lax.fori_loop(0, matrix_places()[1][1], one_out, 0)
    grad_att[...] = dot_low(branch, w_out[...], NT_).astype(BF)
    wait_tiles(d_all, matrix_places()[1][1], send_sems.at[0])
    wait_tiles(d_all, targets.shape[0] - matrix_places()[1][1], send_sems.at[1])


def middle(held_tiles, sent_tiles, targets, weights, first_buffer, buffer_shapes, att, own, cot, rows14, conv_t, taps_forward, taps_backward, tail_bias):
    count = len(weights)

    def kernel(*refs):
        middle_kernel(count, first_buffer, *refs)

    def f32(*shape):
        return jax.ShapeDtypeStruct(shape, F32)

    outs = [
        f32(2 * NT, D), f32(OWN_ROWS, D), jax.ShapeDtypeStruct((OWN_ROWS, D), BF), f32(8, D),
        f32(FF // D, D), f32(9 * NT, D), f32(3, 9 * NT, NT), f32(NT, 4),
    ]
    results = pl.pallas_call(
        kernel,
        grid_spec=pltpu.PrefetchScalarGridSpec(
            num_scalar_prefetch=3,
            grid=(1,),
            in_specs=[anywhere()] * count + [in_vmem()] * 9,
            out_specs=[in_vmem()] * len(outs) + [anywhere()] * len(buffer_shapes),
            scratch_shapes=[
                pltpu.VMEM((ALL_ROWS + BLOCK_SIDE, D), BF),
                pltpu.VMEM((ALL_ROWS + BLOCK_SIDE, D), BF),
                pltpu.VMEM((FF // D, OWN_ROWS, D), BF),
                pltpu.VMEM((FF // D, OWN_ROWS, D), F32),
                pltpu.VMEM((OWN_ROWS, D), BF),
                pltpu.VMEM((OWN_ROWS, D), F32),
                pltpu.VMEM((OWN_ROWS, D), F32),
                pltpu.VMEM((OWN_ROWS, D), F32),
                pltpu.SemaphoreType.DMA((3,)),
                pltpu.SemaphoreType.DMA((2,)),
            ],
        ),
        out_shape=outs + buffer_shapes,
        compiler_params=pltpu.CompilerParams(vmem_limit_bytes=VMEM_MOST),
        cost_estimate=about(40),
    )(
        held_tiles, sent_tiles, targets, *weights, att, own, cot, rows14, conv_t, taps_forward, taps_backward, tail_bias,
        jnp.asarray(lane_masks()),
    )
    return results[: len(outs)], results[len(outs) :]


def qkv_grads(targets, low, own_low, dq, dk, dv, buffers, late):
    steps = low.shape[0] // OWN_ROWS
    count = len(buffers)

    def kernel(targets, low, own_low, dq, dk, dv, *refs):
        filled = refs[count : 2 * count]
        matrix = refs[2 * count]
        totals, sem = refs[2 * count + 1 :]
        step = pl.program_id(0)

        @pl.when(step == 0)
        def _():
            totals[...] = jnp.zeros_like(totals)
            matrix[:, :D] = dot_low(own_low[...], dq[...], TN).astype(BF)

        totals[:, :D] += dot_low(low[...], dk[...], TN)
        totals[:, D:] += dot_low(low[...], dv[...], TN)

        @pl.when(step == steps - 1)
        def _():
            matrix[:, D:] = totals[...].astype(BF)
            cols = 3 * D // BLOCK_SIDE

            def one_tile(tile, sent):
                code = targets[tile]
                send_tile(code, filled, tile_at(matrix, lax.div(tile, cols), lax.rem(tile, cols)), sem, late)
                return sent + (lax.div(code, CODE_BASE) >= late).astype(jnp.int32)

            sent = lax.fori_loop(0, QKV_BLOCKS, one_tile, jnp.int32(0))

            def one_wait(index, carry):
                wait_whole(tile_at(matrix, 0, 0), sem)
                return carry

            lax.fori_loop(0, sent, one_wait, 0)

    def whole(shape):
        return pl.BlockSpec(shape, lambda i, targets: (0, 0))

    def moving(width):
        return pl.BlockSpec((OWN_ROWS, width), lambda i, targets: (i, 0))

    results = pl.pallas_call(
        kernel,
        grid_spec=pltpu.PrefetchScalarGridSpec(
            num_scalar_prefetch=1,
            grid=(steps,),
            in_specs=[moving(D), whole((OWN_ROWS, D)), whole((OWN_ROWS, D)), moving(D), moving(D)]
            + [anywhere()] * count,
            out_specs=[anywhere()] * count + [whole((D, 3 * D))],
            scratch_shapes=[pltpu.VMEM((D, 2 * D), F32), pltpu.SemaphoreType.DMA],
        ),
        out_shape=[jax.ShapeDtypeStruct(b.shape, b.dtype) for b in buffers]
        + [jax.ShapeDtypeStruct((D, 3 * D), BF)],
        input_output_aliases={6 + i: i for i in range(count)},
        compiler_params=pltpu.CompilerParams(vmem_limit_bytes=VMEM_MOST),
        cost_estimate=about(14),
    )(targets, low, own_low, dq, dk, dv, *buffers)
    return results[:count], results[count]


def input_grads(seen, own, dq, dk, dv, w_qkv):
    rows = seen.shape[0]
    steps = rows // OWN_ROWS

    def kernel(seen, own, dq, dk, dv, w_qkv, grad_seen, grad_own, sums):
        step = pl.program_id(0)

        @pl.when(step == 0)
        def _():
            grad = dot_low(dq[...], w_qkv[:, :D], NT_)
            grad_own[...] = grad
            hat, _ = normalized(own[...].astype(F32))
            sums[...] = jnp.zeros_like(sums)
            sums[0:1] = column_sum(grad * hat)
            sums[1:2] = column_sum(grad)
            sums[2:3] = column_sum(dq[...].astype(F32))

        grad = dot_low(dk[...], w_qkv[:, D : 2 * D], NT_) + dot_low(dv[...], w_qkv[:, 2 * D :], NT_)
        grad_seen[...] = grad.astype(BF)
        hat, _ = normalized(seen[...].astype(F32))
        sums[0:1] += column_sum(grad * hat)
        sums[1:2] += column_sum(grad)
        sums[3:4] += column_sum(dv[...].astype(F32))

    def whole(shape):
        return pl.BlockSpec(shape, lambda i: (0, 0))

    moving = pl.BlockSpec((OWN_ROWS, D), lambda i: (i, 0))
    return pl.pallas_call(
        kernel,
        grid=(steps,),
        in_specs=[moving, whole((OWN_ROWS, D)), whole((OWN_ROWS, D)), moving, moving, whole((D, 3 * D))],
        out_specs=[moving, whole((OWN_ROWS, D)), whole((8, D))],
        out_shape=[
            jax.ShapeDtypeStruct((rows, D), BF),
            jax.ShapeDtypeStruct((OWN_ROWS, D), F32),
            jax.ShapeDtypeStruct((8, D), F32),
        ],
        compiler_params=pltpu.CompilerParams(vmem_limit_bytes=VMEM_MOST),
        cost_estimate=about(12),
    )(seen, own, dq, dk, dv, w_qkv)


def moved(value, axis, size, step):
    return lax.ppermute(value, axis, [(i, (i + step) % size) for i in range(size)])


def reduce_axis(terms, axis, size, dim=0):
    total = lax.index_in_dim(terms, 0, dim, keepdims=False).astype(F32)
    for step in range(1, size):
        term = lax.index_in_dim(terms, step, dim, keepdims=False)
        total = total + moved(term, axis, size, step).astype(F32)
    return total


def after(value, *others):
    return lax.optimization_barrier((value, others))[0]


def gather_axis(value, axis, size):
    return jnp.stack([value] + [moved(value, axis, size, -step) for step in range(1, size)])


def rolled(value, axis, size, step):
    return lax.dynamic_slice_in_dim(jnp.concatenate([value, value], axis), step, size, axis)


def small_shares(vector, sizes, coords):
    device_count = math.prod(sizes)
    share = -(-vector.shape[0] // (device_count * 128)) * 128
    shares = jnp.pad(vector, (0, device_count * share - vector.shape[0])).reshape(sizes + (share,))
    for axis, size in enumerate(sizes):
        shares = rolled(shares, axis, size, coords[axis])
    return shares.transpose(3, 1, 2, 0, 4)


def small_step(shares, axis, sizes):
    return reduce_axis(shares, ALL_AXES[axis], sizes[axis])


def early_slots(slots_dev):
    return slots_dev * 6 // 14


def slot_chunks(slots_dev):
    early = early_slots(slots_dev)
    late = slots_dev - early
    chunks = []
    first = 0
    for index, count in enumerate((early - early // 2, early // 2, late - late // 2, late // 2)):
        chunks.append((first, count, ("fx", "by", "fz") if index % 2 == 0 else ("by", "fx", "fz")))
        first = first + count
    return chunks


def send_table(block_owner, sizes, coords, slots_dev):
    nz, nx, ny, nc = sizes
    slots = jnp.arange(block_owner.shape[0], dtype=jnp.int32)
    device = slots // slots_dev
    place = {}
    for axis in range(3, -1, -1):
        place[ALL_AXES[axis]] = (device % sizes[axis] - coords[axis] + sizes[axis]) % sizes[axis]
        device = device // sizes[axis]
    is_late = (block_owner < QKV_BLOCKS).astype(jnp.int32).reshape(-1, slots_dev)
    late_before = jnp.cumsum(is_late, 1) - is_late
    early_before = jnp.arange(slots_dev, dtype=jnp.int32)[None] - late_before
    late_count = jnp.sum(is_late, 1, keepdims=True)
    ranks = jnp.where(is_late == 1, slots_dev - late_count + late_before, early_before)
    rank = ranks.reshape(-1)
    size_of = dict(zip(ALL_AXES, sizes))
    code = jnp.zeros_like(slots)
    chunks = slot_chunks(slots_dev)
    device_count = nz * nx * ny * nc
    for index, (first, count, axes) in enumerate(chunks):
        at = jnp.zeros_like(slots)
        for name in axes:
            at = at * size_of[name] + place[name]
        at = at * count + rank - first
        if index % 2:
            at = at + device_count // nc * chunks[index - 1][1]
        inside = (rank >= first) & (rank < first + count)
        code = jnp.where(inside, (index // 2 * 2 + place["core"]) * CODE_BASE + at, code)
    owned = block_owner[:, None] == slots[None, :]
    table = jnp.sum(jnp.where(owned, code[:, None], 0), 0)
    early = early_slots(slots_dev)
    late_size = device_count // nc * (slots_dev - early)
    early_size = device_count // nc * early
    buffer, at = code // CODE_BASE, code % CODE_BASE
    sent_at = jnp.where(buffer < 2, buffer * early_size, 2 * early_size + (buffer - 2) * late_size) + at
    held_at = jnp.where(buffer < 2, slots // slots_dev * early + rank, 2 * early_size + (buffer - 2) * late_size + at)
    tile = tile_code(block_owner)
    held_tiles = jnp.sum(jnp.where(held_at[:, None] == slots[None, :], tile[:, None], 0), 0)
    sent_tiles = jnp.sum(jnp.where(sent_at[:, None] == slots[None, :], tile[:, None], 0), 0)
    qkv_cols = 3 * D // BLOCK_SIDE
    qkv_tile = jnp.where(block_owner < QKV_BLOCKS, block_owner // qkv_cols * 32 + block_owner % qkv_cols, 2048)
    qkv_tiles = jnp.sum(jnp.where(held_at[:, None] == slots[None, :], qkv_tile[:, None], 0), 0)
    return table, qkv_tiles, held_tiles, sent_tiles, ranks, jnp.max(late_count)


def tile_code(block):
    side = D // BLOCK_SIDE
    out_tile = block - matrix_places()[1][0]
    up_tile = block - matrix_places()[2][0]
    down_tile = block - matrix_places()[3][0]
    up_row, up_col = up_tile // (FF // BLOCK_SIDE), up_tile % (FF // BLOCK_SIDE)
    row = jnp.where(
        up_tile < 0,
        out_tile // side,
        jnp.where(down_tile < 0, side + up_col // side * side + up_row, UP_ROWS + down_tile // side),
    )
    col = jnp.where(up_tile < 0, out_tile % side, jnp.where(down_tile < 0, up_col % side, down_tile % side))
    matrix = jnp.where(up_tile < 0, 0, jnp.where(down_tile < 0, 1, 2))
    used = (out_tile >= 0) & (block < MATRIX_BLOCKS)
    return jnp.where(used, matrix * 2048 + row * 32 + col, 3 * 2048 + BLANK_ROW * 32)


def reduce_core(kept, sent, chunks, sizes):
    size_of = dict(zip(ALL_AXES, sizes))
    total = (kept.astype(F32) + moved(sent, "core", 2, 1).astype(F32)).astype(BF)
    parts = []
    start = 0
    for first, count, axes in chunks:
        shape = [size_of[name] for name in axes] + [count, BLOCK_SIDE, BLOCK_SIDE]
        stop = start + math.prod(shape[:-2])
        parts.append(total[start:stop].reshape(shape))
        start = stop
    return parts


def reduce_stage(parts, chunks, stage, sizes):
    results = []
    for part, (first, count, axes) in zip(parts, chunks):
        name = axes[stage]
        results.append(reduce_axis(part, name, sizes[ALL_AXES.index(name)]).astype(BF))
    return results


def reduce_last(parts, sizes):
    return reduce_axis(jnp.concatenate(parts, axis=1), "fz", sizes[0])


def gather_stage(shard, axes, stage, sizes):
    name = axes[len(axes) - 1 - stage]
    return gather_axis(shard, name, sizes[ALL_AXES.index(name)])


def gather_last(shards, orders, sizes):
    pieces = []
    for shard, axes in zip(shards, orders):
        size = sizes[ALL_AXES.index(axes[0])]
        pieces = pieces + [shard] + [moved(shard, axes[0], size, -step) for step in range(1, size)]
    return [piece.reshape(-1, BLOCK_SIDE, BLOCK_SIDE) for piece in pieces]


def sorted_shards(device_index, block_owner, master):
    slots_dev = master.shape[0]
    early = early_slots(slots_dev)
    chunks = [(0, early, ()), (early, slots_dev - early, ())]

    def kernel(where, owner, blocks, *outs):
        base = where[0] * slots_dev
        late_count = jnp.int32(0)
        for slot in range(slots_dev):
            late_count = late_count + (owner[base + slot] < QKV_BLOCKS).astype(jnp.int32)
        early_at, late_at = jnp.int32(0), slots_dev - late_count
        for slot in range(slots_dev):
            late = owner[base + slot] < QKV_BLOCKS
            rank = jnp.where(late, late_at, early_at)
            late_at = late_at + late.astype(jnp.int32)
            early_at = early_at + 1 - late.astype(jnp.int32)
            for index, (first, count, axes) in enumerate(chunks):
                if count == 0:
                    continue

                @pl.when((rank >= first) & (rank < first + count))
                def _(index=index, first=first):
                    outs[index][rank - first] = blocks[slot].astype(BF)

    return pl.pallas_call(
        kernel,
        grid_spec=pltpu.PrefetchScalarGridSpec(
            num_scalar_prefetch=2,
            grid=(1,),
            in_specs=[in_vmem()],
            out_specs=[in_vmem()] * len(chunks),
        ),
        out_shape=[
            jax.ShapeDtypeStruct((max(count, 1), BLOCK_SIDE, BLOCK_SIDE), BF) for first, count, axes in chunks
        ],
        cost_estimate=about(3),
    )(device_index.reshape(1), block_owner, master)


def spread_early(targets, matrix, buffer_shapes):
    count = len(buffer_shapes)

    def kernel(targets, matrix, blank, *refs):
        buffers, sem = refs[:count], refs[count]

        def one_block(block, sent):
            code = targets[block]
            cols = 3 * D // BLOCK_SIDE
            early = lax.div(code, CODE_BASE) < 2

            @pl.when(early & (block < QKV_BLOCKS))
            def _():
                tile = tile_at(matrix, lax.div(block, cols), lax.rem(block, cols))
                send_tile(code, buffers, tile, sem)

            @pl.when(early & (block >= QKV_BLOCKS))
            def _():
                send_tile(code, buffers, blank, sem)

            return sent + early.astype(jnp.int32)

        sent = lax.fori_loop(0, targets.shape[0], one_block, jnp.int32(0))

        def one_wait(index, carry):
            wait_whole(blank, sem)
            return carry

        lax.fori_loop(0, sent, one_wait, 0)

    return pl.pallas_call(
        kernel,
        grid_spec=pltpu.PrefetchScalarGridSpec(
            num_scalar_prefetch=1,
            grid=(1,),
            in_specs=[in_vmem()] * 2,
            out_specs=[anywhere()] * count,
            scratch_shapes=[pltpu.SemaphoreType.DMA],
        ),
        out_shape=buffer_shapes,
        compiler_params=pltpu.CompilerParams(vmem_limit_bytes=VMEM_MOST),
    )(targets, matrix, jnp.zeros((BLOCK_SIDE, BLOCK_SIDE), BF))


def pad_frames(values):
    frames = values.reshape(2, FRAME_ROWS, values.shape[-1])
    return jnp.pad(frames, ((0, 0), (0, PAD_ROWS - FRAME_ROWS), (0, 0)))


def on_device(
    tokens,
    cotangent,
    clip_lengths,
    clip_order,
    block_owner,
    master,
    moment1,
    moment2,
    stat_left,
    stat_right,
    basis_left,
    basis_right,
    small_params,
    small_moment1,
    small_moment2,
):
    sizes = tuple(lax.axis_size(name) for name in ALL_AXES)
    coords = [lax.axis_index(name) for name in ALL_AXES]
    nz, nx, ny, nc = sizes
    device_count = nz * nx * ny * nc
    frame_count = nz * nx
    frame_index = coords[0] * nx + coords[1]
    slots_dev = master.shape[0]

    segment_slots = clip_segments(
        clip_lengths[0], clip_order[0], 2 * frame_count, 2, frame_count
    ).reshape(frame_count, 2)
    ordered_len = clip_lengths[0][clip_order[0]]
    longest = jnp.argmax(ordered_len).astype(jnp.int32)
    second_long = segment_slots[:, 1] == longest
    short_segment = jnp.where(second_long, segment_slots[:, 0], segment_slots[:, 1])
    swap = second_long[frame_index]
    padded_segment = jnp.pad(short_segment, (1, 1), constant_values=-1)
    near = lax.dynamic_slice_in_dim(padded_segment, frame_index, 3)
    with_previous = near[0] == near[1]
    with_next = near[2] == near[1]

    device_index = ((coords[0] * nx + coords[1]) * ny + coords[2]) * nc + coords[3]
    early = early_slots(slots_dev)
    chunks = slot_chunks(slots_dev)
    shards = sorted_shards(device_index, block_owner, master)
    orders = [axes for first, count, axes in chunks]
    late_shards = gather_axis(shards[1], "fz", nz)

    own_frames = pad_frames(tokens[0])
    own_frames = jnp.where(swap, own_frames[::-1], own_frames)
    long_frame, short_frame = own_frames[0], own_frames[1]
    frame_perm = [(i, (i + 1) % frame_count) for i in range(frame_count)]
    back_perm = [(j, i) for i, j in frame_perm]
    def gather_early(shard):
        return lax.all_gather(shard, ALL_AXES, axis=0, tiled=True)

    weights = [gather_early(shards[0])] if early else []
    long_pair = gather_axis(long_frame, "fx", nx)
    from_previous = lax.ppermute(short_frame, FRAME_AXES, frame_perm)
    from_next = lax.ppermute(short_frame, FRAME_AXES, back_perm)
    long_pair, late_shards, from_previous, from_next = lax.optimization_barrier(
        (long_pair, late_shards, from_previous, from_next)
    )
    late_shards = [late_shards[:, : chunks[2][1]], late_shards[:, chunks[2][1] :]]
    late_shards = [gather_stage(part, orders[2 + i], 1, sizes) for i, part in enumerate(late_shards)]
    long_frames = [long_pair] + [moved(long_pair, "fz", nz, -step) for step in range(1, nz)]
    late_shards, long_frames[1:-1] = lax.optimization_barrier((late_shards, long_frames[1:-1]))
    late_pieces = gather_last(late_shards, orders[2:], sizes)
    partner = jnp.where(with_next, from_next, from_previous)

    frames_seen = frame_count + 2
    own = own_frames.reshape(OWN_ROWS, D)
    row_ids = jnp.arange(frames_seen * PAD_ROWS, dtype=jnp.int32)
    hidden_key = (row_ids % PAD_ROWS >= FRAME_ROWS) | (
        (row_ids >= (frames_seen - 1) * PAD_ROWS) & ~(with_previous | with_next)
    )
    key_bias = jnp.where(hidden_key, MASK_FLOOR, 0.0).astype(F32)

    targets, qkv_tiles, held_tiles, sent_tiles, ranks, late_most = send_table(block_owner, sizes, coords, slots_dev)
    own_ranks = lax.dynamic_index_in_dim(ranks, device_index, 0, keepdims=False)
    late_fits = late_most <= slots_dev - early

    split = unpack(small_params)
    rows14 = small_params[: 14 * D].reshape(14, D)
    conv_t = split["conv_first"].astype(BF).reshape(D, 9 * NT).T
    tail = jnp.stack([split["conv_second"], split["conv_third"], split["conv_fourth"]])
    taps_forward = tail.transpose(0, 3, 1, 2).reshape(3, NT, 9 * NT)
    taps_backward = tail.transpose(0, 2, 1, 3).reshape(3, NT, 9 * NT)
    tail_bias = split["conv_bias"].T
    arriving = cotangent[0].reshape(2, NT, D)
    arriving = jnp.where(swap, arriving[::-1], arriving).reshape(2 * NT, D)

    stat_parts = stat_products(stat_left, stat_right, basis_left, basis_right)
    early_looked = jnp.where(late_fits, 0, device_count * early).astype(jnp.int32).reshape(1)

    (
        late_pieces, long_frames, partner, stat_parts, key_bias, targets, qkv_tiles, held_tiles, sent_tiles, own_ranks,
        early_looked, rows14, conv_t, taps_forward, taps_backward, tail_bias, arriving,
    ) = lax.optimization_barrier(
        (
            late_pieces, long_frames, partner, stat_parts, key_bias, targets, qkv_tiles, held_tiles, sent_tiles, own_ranks,
            early_looked, rows14, conv_t, taps_forward, taps_backward, tail_bias, arriving,
        )
    )
    weights = weights + late_pieces + [moved(piece, "core", nc, 1) for piece in late_pieces]
    seen = jnp.concatenate(
        [frames.reshape(-1, D) for frames in long_frames] + [short_frame, partner]
    )
    query, key_value, low, own_low, w_qkv = project(
        qkv_tiles, early_looked, weights, 1 if early else 0, seen, rows14
    )
    attended, logs = attend(query, key_value, key_bias)
    buffer_shapes = []
    for slots in (early, slots_dev - early):
        if slots:
            shape = jax.ShapeDtypeStruct((device_count // nc * slots, BLOCK_SIDE, BLOCK_SIDE), BF)
            buffer_shapes = buffer_shapes + [shape, shape]
    (learned, grad_mixed, grad_att, vectors, grad_up_bias, grad_conv, grad_tail, grad_tail_bias), buffers = middle(
        held_tiles, sent_tiles, targets, weights, 0 if early else 2, buffer_shapes, attended, own, arriving, rows14, conv_t,
        taps_forward, taps_backward, tail_bias,
    )
    learned = learned.reshape(2, NT, D)
    learned = jnp.where(swap, learned[::-1], learned).reshape(2 * NT, D)

    halfway = reduce_core(*buffers[:2], chunks[:2], sizes) if early else []
    back = attend_back((0, PAIRS // 2), [], query, key_value, key_bias, attended, logs, grad_att)
    back, halfway = lax.optimization_barrier((back, halfway))
    halfway = reduce_stage(halfway, chunks, 0, sizes)
    grad_query, grad_key, grad_value = attend_back(
        (PAIRS // 2, PAIRS - PAIRS // 2), back, query, key_value, key_bias, attended, logs, grad_att
    )
    grad_query, halfway = lax.optimization_barrier((grad_query, halfway))
    halfway = reduce_stage(halfway, chunks, 1, sizes)
    late_buffers, grad_w_qkv = qkv_grads(
        targets, low, own_low, grad_query, grad_key, grad_value, list(buffers[-2:]), 2
    )
    grad_query, late_buffers, halfway = lax.optimization_barrier((grad_query, late_buffers, halfway))
    reduced = [reduce_last(halfway, sizes)] if early else []
    late_parts = reduce_core(*late_buffers, chunks[2:], sizes)
    grad_seen, grad_own, sums = input_grads(seen, own, grad_query, grad_key, grad_value, w_qkv)
    late_parts, reduced, grad_seen, sums = lax.optimization_barrier((late_parts, reduced, grad_seen, sums))

    seen_frames = grad_seen.reshape(frames_seen, PAD_ROWS, D)
    long_terms = seen_frames[:frame_count].reshape(nz, nx, PAD_ROWS, D)
    partner_term = seen_frames[frame_count + 1]
    nothing = jnp.zeros_like(partner_term)
    to_previous = jnp.where(with_previous, partner_term, nothing)
    to_next = jnp.where(with_next, partner_term, nothing)
    late_parts = reduce_stage(late_parts, chunks[2:], 0, sizes)
    small_local = jnp.concatenate(
        [
            sums[:2].reshape(-1),
            vectors[:4].reshape(-1),
            sums[2:4].reshape(-1),
            vectors[4],
            grad_up_bias.reshape(-1),
            vectors[5],
            grad_conv.T.reshape(-1),
            grad_tail.reshape(-1),
            grad_tail_bias.T.reshape(-1),
        ]
    )
    small_total = small_local.shape[0]
    small = small_step(small_shares(small_local, sizes, coords), 3, sizes)
    late_parts, small = lax.optimization_barrier((late_parts, small))
    late_parts = reduce_stage(late_parts, chunks[2:], 1, sizes)
    small = small_step(small, 1, sizes)
    late_parts, small, long_terms = lax.optimization_barrier((late_parts, small, long_terms))
    late_total = reduce_last(late_parts, sizes)
    small = small_step(small_step(small, 2, sizes), 0, sizes)
    long_terms = reduce_axis(long_terms, "fx", nx, 1).astype(BF)
    late_total, small, long_terms = lax.optimization_barrier((late_total, small, long_terms))
    if early:
        def whole_early(share):
            extra = reduce_core(*spread_early(targets, grad_w_qkv, buffer_shapes[:2]), chunks[:2], sizes)
            for stage in range(2):
                extra = reduce_stage(extra, chunks, stage, sizes)
            return share + reduce_last(extra, sizes)

        reduced = [lax.cond(late_fits, lambda share: share, whole_early, reduced[0])]
    owned_grads = jnp.concatenate(reduced + [late_total])

    squares = jnp.sum(owned_grads * owned_grads) + jnp.sum(small * small)
    carried = jnp.concatenate([small, jnp.full((128,), squares, F32)])
    carried = gather_axis(carried, "fz", nz)
    carried = gather_axis(carried, "fx", nx)
    raw = raw_products(own_ranks, owned_grads, basis_left, basis_right)
    carried = gather_axis(carried, "by", ny)
    carried, raw = lax.optimization_barrier((carried, raw))
    carried = gather_axis(carried, "core", nc)
    share = small.shape[0]
    grad_norm = jnp.sqrt(jnp.sum(carried[..., share]))
    factor = 1.0 / jnp.maximum(grad_norm, CLIP_NORM)
    long_terms, to_previous, to_next, factor = lax.optimization_barrier((long_terms, to_previous, to_next, factor))
    long_total = reduce_axis(long_terms, "fz", nz)
    from_next = lax.ppermute(to_previous, FRAME_AXES, back_perm)
    from_previous = lax.ppermute(to_next, FRAME_AXES, frame_perm)
    carried = carried[..., :share]
    for axis, size in enumerate(sizes):
        carried = rolled(carried, 3 - axis, size, size - coords[axis])
    small_grad = carried.transpose(3, 2, 1, 0, 4).reshape(-1)[:small_total]

    small_first, small_second, small_new = adam_update(
        small_grad * factor, small_params, small_moment1, small_moment2
    )

    soap_out = finish(
        factor.reshape(1), *raw, *stat_parts, stat_left, stat_right, basis_left, basis_right, master, moment1, moment2
    )
    short_total = seen_frames[frame_count].astype(F32) + from_next.astype(F32) + from_previous.astype(F32)
    grad_normed_one = jnp.concatenate([long_total, short_total]) + grad_own
    hat, spread = normalized(own.astype(F32))
    grad_inputs = grad_mixed + norm_back(grad_normed_one, hat, spread, rows14[0:1])
    grad_inputs = grad_inputs.reshape(2, PAD_ROWS, D)[:, :FRAME_ROWS]
    grad_inputs = jnp.where(swap, grad_inputs[::-1], grad_inputs).reshape(2 * FRAME_ROWS, D)
    return (
        learned[None],
        grad_inputs[None],
        soap_out[0],
        soap_out[1],
        soap_out[2],
        soap_out[3],
        soap_out[4],
        soap_out[5],
        soap_out[6],
        small_first,
        small_second,
        small_new,
        grad_norm,
    )


def solution(mesh):
    frames, batches = mesh.shape["frame"], mesh.shape["batch"]
    split = Mesh(mesh.devices.reshape(frames // 2, 2, batches // 2, 2), ALL_AXES)
    batch = ("by", "core")
    slots = P(ALL_AXES, None, None)
    rows = P(batch, FRAME_AXES, None)
    return jax.shard_map(
        on_device,
        mesh=split,
        in_specs=(rows, rows, P(batch, None), P(batch, None), P()) + (slots,) * 7 + (P(),) * 3,
        out_specs=(rows, rows) + (slots,) * 7 + (P(),) * 4,
        check_vma=False,
    )
```

```python
import math

import jax
import jax.numpy as jnp
import numpy as np
from jax import lax
from jax.experimental import pallas as pl
from jax.experimental.pallas import tpu as pltpu
from jax.sharding import Mesh
from jax.sharding import PartitionSpec as P

D = 768
HEADS = 12
HD = 64
FF = 3072
GRID = 14
NT = 8
BLOCK_SIDE = 128
STEP = 10
MATRIX_BLOCKS = 432


FULL_PRECISION = lax.Precision.HIGHEST
NORM_EPSILON = 1e-06
BETA_ONE = 0.9
BETA_TWO = 0.95
STAT_DECAY = 0.95
LEARN_RATE = 0.1
WEIGHT_DECAY = 0.01
ADAM_EPSILON = 1e-08
CLIP_NORM = 1.0
MASK_FLOOR = -1e30


def layout():
    return [
        ("gain_one", (D,)),
        ("shift_one", (D,)),
        ("gain_two", (D,)),
        ("shift_two", (D,)),
        ("gain_three", (D,)),
        ("shift_three", (D,)),
        ("bias_query", (D,)),
        ("bias_value", (D,)),
        ("bias_out", (D,)),
        ("bias_up", (FF,)),
        ("bias_down", (D,)),
        ("conv_first", (D, 9, NT)),
        ("conv_second", (9, NT, NT)),
        ("conv_third", (9, NT, NT)),
        ("conv_fourth", (9, NT, NT)),
        ("conv_bias", (4, NT)),
    ]


def unpack(vector):
    params_split = {}
    offset = 0
    for part_name, part_shape in layout():
        entries = math.prod(part_shape)
        params_split[part_name] = vector[offset : offset + entries].reshape(part_shape)
        offset = offset + entries
    return params_split


def matrix_shapes():
    return [(D, 3 * D), (D, D), (D, FF), (FF, D)]


def to_blocks(matrix):
    row_count, col_count = matrix.shape
    tiled = matrix.reshape(row_count // BLOCK_SIDE, BLOCK_SIDE, col_count // BLOCK_SIDE, BLOCK_SIDE)
    return tiled.transpose(0, 2, 1, 3).reshape(-1, BLOCK_SIDE, BLOCK_SIDE)


def from_blocks(blocks):
    matrices = []
    offset = 0
    for row_count, col_count in matrix_shapes():
        tiles = row_count // BLOCK_SIDE * (col_count // BLOCK_SIDE)
        piece_tiles = blocks[offset : offset + tiles].reshape(
            row_count // BLOCK_SIDE, col_count // BLOCK_SIDE, BLOCK_SIDE, BLOCK_SIDE
        )
        matrices.append(piece_tiles.transpose(0, 2, 1, 3).reshape(row_count, col_count))
        offset = offset + tiles
    return matrices


def layer_norm(values, gain_vec, shift_vec):
    centre = jnp.mean(values, -1, keepdims=True)
    centered = values - centre
    spread = jnp.mean(centered * centered, -1, keepdims=True)
    return centered * lax.rsqrt(spread + NORM_EPSILON) * gain_vec + shift_vec


def gelu_exact(values):
    return jax.nn.gelu(values, approximate=False)


def taps_sum(taps):
    padded = jnp.pad(taps, ((0, 0), (1, 1), (1, 1), (0, 0), (0, 0)))
    summed = jnp.zeros(taps.shape[:3] + taps.shape[4:], taps.dtype)
    for tap_index in range(9):
        row_off = tap_index // 3 - 1
        col_off = tap_index % 3 - 1
        summed = (
            summed
            + padded[
                :, 1 + row_off : 1 + row_off + GRID, 1 + col_off : 1 + col_off + GRID, tap_index
            ]
        )
    return summed


def taps_back(grads):
    padded = jnp.pad(grads, ((0, 0), (1, 1), (1, 1), (0, 0)))
    shifted = []
    for tap_index in range(9):
        row_off = tap_index // 3 - 1
        col_off = tap_index % 3 - 1
        shifted.append(
            padded[:, 1 - row_off : 1 - row_off + GRID, 1 - col_off : 1 - col_off + GRID]
        )
    return jnp.stack(shifted, axis=3)


def conv_small(values, weight):
    taps = jnp.einsum("fyxc,tco->fyxto", values, weight, precision=FULL_PRECISION)
    return taps_sum(taps)


def learner_tail(first_pre, values, second_w, third_w, fourth_w, tail_bias):
    frames = first_pre.shape[0]
    act_one = gelu_exact(first_pre)
    act_two = gelu_exact(conv_small(act_one, second_w) + tail_bias[0])
    act_three = gelu_exact(conv_small(act_two, third_w) + tail_bias[1])
    maps = jax.nn.sigmoid(conv_small(act_three, fourth_w) + tail_bias[2])
    grid_values = values.reshape(frames, GRID, GRID, values.shape[-1])
    pooled = jnp.einsum("fyxk,fyxd->fkd", maps, grid_values, precision=FULL_PRECISION)
    return pooled.reshape(frames * NT, values.shape[-1])


def clip_segments(lengths, order_row, group_frames, frames_dev, frame_count):
    clip_ids = jnp.arange(lengths.shape[0], dtype=jnp.int32)
    ordered_len = jnp.sum(
        jnp.where(order_row[:, None] == clip_ids[None, :], lengths[None, :], 0), 1
    )
    ends = jnp.cumsum(ordered_len)
    slots = jnp.arange(group_frames, dtype=jnp.int32)
    places = slots % frames_dev * frame_count + slots // frames_dev
    return jnp.sum((ends[None, :] <= places[:, None]).astype(jnp.int32), 1)


F32=jnp.float32; BF=jnp.bfloat16
NN=(((1,),(0,)),((),()))
NT_=(((1,),(1,)),((),()))
TN=(((0,),(0,)),((),()))

def halves(a):
    high = a.astype(BF)
    return high, (a - high.astype(F32)).astype(BF)

def dot_low(a, b, dims):
    return lax.dot_general(a, b, dims, preferred_element_type=F32)

def dot_parts(a, b, dims):
    ah, al = a
    bh, bl = b
    return dot_low(ah, bh, dims) + (dot_low(ah, bl, dims) + dot_low(al, bh, dims))

def dot_wide(a, b, dims):
    return dot_parts(halves(a), halves(b), dims)

def slots_step(n):
    return 7 if n % 7 == 0 else 2 if n % 2 == 0 else 1


def stat_products(sl, sr, bl, br):
    n = sl.shape[0]
    many = slots_step(n)
    spec = pl.BlockSpec((many, BLOCK_SIDE, BLOCK_SIDE), lambda i: (i, 0, 0))

    def kernel(sl, sr, bl, br, out_left, out_right):
        for s in range(many):
            out_left[s] = STAT_DECAY * dot_wide(bl[s], sl[s], TN)
            out_right[s] = STAT_DECAY * dot_wide(br[s], sr[s], TN)

    return pl.pallas_call(
        kernel,
        grid=(n // many,),
        in_specs=[spec] * 4,
        out_specs=[spec] * 2,
        out_shape=[jax.ShapeDtypeStruct(sl.shape, F32)] * 2,
        cost_estimate=about(7),
    )(sl, sr, bl, br)


def raw_products(ranks, g, bl, br):
    n = g.shape[0]
    many = slots_step(n)
    here = pl.BlockSpec((many, BLOCK_SIDE, BLOCK_SIDE), lambda i, ranks: (i, 0, 0))

    def ranked(s):
        return pl.BlockSpec((1, BLOCK_SIDE, BLOCK_SIDE), lambda i, ranks: (ranks[i * many + s], 0, 0))

    def kernel(ranks, *refs):
        grads, (bl, br, rot, gl, gr, ql, qr) = refs[:many], refs[many:]
        each = range(many)
        gp = [halves(grads[s][0]) for s in each]
        blp, brp = [halves(bl[s]) for s in each], [halves(br[s]) for s in each]
        u = [halves(dot_parts(blp[s], gp[s], TN)) for s in each]
        v = [halves(dot_parts(gp[s], brp[s], NN)) for s in each]
        for s in each:
            gl[s] = dot_parts(gp[s], gp[s], NT_)
        for s in each:
            gr[s] = dot_parts(gp[s], gp[s], TN)
        for s in each:
            rot[s] = dot_parts(u[s], brp[s], NN)
        for s in each:
            ql[s] = dot_parts(u[s], gp[s], NT_)
        for s in each:
            qr[s] = dot_parts(v[s], gp[s], TN)

    return pl.pallas_call(
        kernel,
        grid_spec=pltpu.PrefetchScalarGridSpec(
            num_scalar_prefetch=1,
            grid=(n // many,),
            in_specs=[ranked(s) for s in range(many)] + [here, here],
            out_specs=[here] * 5,
        ),
        out_shape=[jax.ShapeDtypeStruct(g.shape, F32)] * 5,
        cost_estimate=about(8),
    )(ranks, *([g] * many), bl, br)


NB=32
def tall(parts, order):
    return jnp.concatenate([parts[which] for which in order], axis=0)


def wide(parts, order):
    return jnp.concatenate([parts[which] for which in order], axis=1)


def finish_kernel(factor, *refs):
    inputs, refs = refs[:14], refs[14:]
    results, refs = refs[:7], refs[7:]
    held, made = refs[:14], refs[14:21]
    work, elim, load_sems, store_sems = refs[21:]
    p_l, p_r, ql, qr, rot, gl, gr, sl, sr, bl, br, master, m1, m2 = held
    o_master, o_m1, o_m2, o_left, o_right, o_bl, o_br = made
    for index in range(14):
        pltpu.make_async_copy(inputs[index], held[index], load_sems.at[index]).start()

    def ready(*indices):
        for index in indices:
            pltpu.make_async_copy(inputs[index], held[index], load_sems.at[index]).wait()

    def store(*indices):
        for index in indices:
            pltpu.make_async_copy(made[index], results[index], store_sems.at[index]).start()

    n = rot.shape[0]
    count = 2 * n
    f = factor[0]
    f2 = (1.0 - STAT_DECAY) * f * f
    ready(0, 1, 2, 3)
    group = 7 if n % 7 == 0 else n
    for start in range(0, n, group):
        members = range(start, start + group)
        sums = [p_[s] + f2 * q_[s] for s in members for p_, q_ in ((p_l, ql), (p_r, qr))]
        parts = [halves(at) for at in sums]
        grams = [dot_parts(atp, atp, NT_) for atp in parts]
        for i in range(2 * group):
            work[2 * start + i, :, BLOCK_SIDE:] = sums[i]
            work[2 * start + i, :, :BLOCK_SIDE] = grams[i]

    rows = lax.broadcasted_iota(jnp.int32, (1, 8, 2 * NB), 1)
    lanes = lax.broadcasted_iota(jnp.int32, (1, 8, 2 * NB), 2)
    panels = BLOCK_SIDE // NB
    tile_count = NB // 8

    def panel(p, carry):
        for q in range(panels):
            @pl.when(p == q)
            def _(q=q):
                for t in range(tile_count):
                    block = work[:, NB * q + 8 * t : NB * q + 8 * t + 8, NB * q : NB * q + NB]
                    eye = jnp.where(lanes - NB == rows + 8 * t, 1.0, 0.0).astype(F32)
                    eye = jnp.broadcast_to(eye, (count, 8, 2 * NB))
                    elim[:, 8 * t : 8 * t + 8, :] = jnp.concatenate([block, eye[:, :, NB:]], axis=2)
        tiles = [elim[:, 8 * t : 8 * t + 8, :] for t in range(tile_count)]
        for k in range(NB):
            t0, j = divmod(k, 8)
            columns = [jnp.broadcast_to(tiles[t][:, :, k : k + 1], tiles[t].shape) for t in range(t0, tile_count)]
            row = tiles[t0][:, j : j + 1, :] * (1.0 / columns[0][:, j : j + 1, :])
            for t in range(t0, tile_count):
                new = tiles[t] - columns[t - t0] * row
                if t == t0:
                    new = jnp.where(rows > j, new, tiles[t])
                tiles[t] = new
        for t in range(tile_count):
            pivots = jnp.sum(jnp.where(lanes == rows + 8 * t, tiles[t], 0.0), axis=2, keepdims=True)
            elim[:, 8 * t : 8 * t + 8, :] = tiles[t] * lax.rsqrt(pivots)
        for q in range(panels):
            @pl.when(p == q)
            def _(q=q):
                lo, hi = NB * q, NB * q + NB
                for start in range(0, count, group):
                    members = range(start, start + group)
                    inverses = [wide(halves(elim[m, :, NB:]), (0, 0, 1)) for m in members]
                    sources = [tall(halves(work[m, lo:hi, :]), (0, 1, 0)) for m in members]
                    solved = [dot_low(inverses[i], sources[i], NN) for i in range(group)]
                    for i, m in enumerate(members):
                        (o_bl if m % 2 == 0 else o_br)[m // 2, lo:hi, :] = solved[i][:, BLOCK_SIDE:]
                    if hi < BLOCK_SIDE:
                        parts = [halves(y) for y in solved]
                        updates = [
                            dot_low(tall(yp, (0, 0, 1))[:, :BLOCK_SIDE], tall(yp, (0, 1, 0)), TN) for yp in parts
                        ]
                        for i, m in enumerate(members):
                            work[m, hi:, :] = work[m, hi:, :] - updates[i][hi:]
        return carry

    lax.fori_loop(0, panels, panel, 0)

    ready(4, 5, 6, 7, 8, 9, 10, 11, 12, 13)
    for start in range(0, n, group):
        members = range(start, start + group)
        firsts, directions = [], []
        for s in members:
            r = f * rot[s]
            m = BETA_ONE * m1[s] + (1.0 - BETA_ONE) * r
            v = BETA_TWO * m2[s] + (1.0 - BETA_TWO) * r * r
            o_m2[s] = v
            o_left[s] = STAT_DECAY * sl[s] + f2 * gl[s]
            o_right[s] = STAT_DECAY * sr[s] + f2 * gr[s]
            firsts.append(halves(m))
            directions.append(
                halves(m / (1.0 - BETA_ONE**STEP) / (jnp.sqrt(v / (1.0 - BETA_TWO**STEP)) + ADAM_EPSILON))
            )
        old_left = [halves(bl[s]) for s in members]
        old_right = [halves(br[s]) for s in members]
        new_left = [o_bl[s] for s in members]
        new_right = [o_br[s] for s in members]
        each = range(group)
        backs = [halves(dot_parts(old_left[i], directions[i], NN)) for i in each]
        turns_left = [halves(dot_parts(halves(new_left[i]), old_left[i], NN)) for i in each]
        turns_right = [halves(dot_parts(halves(new_right[i]), old_right[i], NN)) for i in each]
        returned = [dot_parts(backs[i], old_right[i], NT_) for i in each]
        parts = [halves(dot_parts(turns_left[i], firsts[i], NN)) for i in each]
        moved_firsts = [dot_parts(parts[i], turns_right[i], NT_) for i in each]
        for i, s in enumerate(members):
            o_master[s] = master[s] - LEARN_RATE * (returned[i] + WEIGHT_DECAY * master[s])
            o_m1[s] = moved_firsts[i]
            o_bl[s] = new_left[i].T
            o_br[s] = new_right[i].T
    store(0, 1, 2, 3, 4, 5, 6)
    for index in range(7):
        pltpu.make_async_copy(made[index], results[index], store_sems.at[index]).wait()


def finish(factor, rot, gl, gr, ql, qr, p_l, p_r, sl, sr, bl, br, master, m1, m2):
    n = rot.shape[0]
    shape = jax.ShapeDtypeStruct(rot.shape, F32)
    hbm = pl.BlockSpec(memory_space=pl.ANY)
    block = pltpu.VMEM((n, BLOCK_SIDE, BLOCK_SIDE), F32)
    return pl.pallas_call(
        finish_kernel,
        in_specs=[pl.BlockSpec(memory_space=pltpu.SMEM)] + [hbm] * 14,
        out_specs=[hbm] * 7,
        out_shape=[shape] * 7,
        scratch_shapes=[block] * 21
        + [
            pltpu.VMEM((2 * n, BLOCK_SIDE, 2 * BLOCK_SIDE), F32),
            pltpu.VMEM((2 * n, NB, 2 * NB), F32),
            pltpu.SemaphoreType.DMA((14,)),
            pltpu.SemaphoreType.DMA((7,)),
        ],
        compiler_params=pltpu.CompilerParams(vmem_limit_bytes=56 * 1024 * 1024),
        cost_estimate=about(30),
    )(factor, p_l, p_r, ql, qr, rot, gl, gr, sl, sr, bl, br, master, m1, m2)


def adam_update(clipped, params_old, first_old, second_old):
    first_new = BETA_ONE * first_old + (1.0 - BETA_ONE) * clipped
    second_new = BETA_TWO * second_old + (1.0 - BETA_TWO) * clipped * clipped
    stepped = (
        first_new
        / (1.0 - BETA_ONE**STEP)
        / (jnp.sqrt(second_new / (1.0 - BETA_TWO**STEP)) + ADAM_EPSILON)
    )
    return (first_new, second_new, params_old - LEARN_RATE * stepped)


FRAME_ROWS = GRID * GRID
PAD_ROWS = 208
OWN_ROWS = 2 * PAD_ROWS
LANES = 512
PAIRS = HEADS // 2
PAIR = 2 * HD
QKV_BLOCKS = 108
CODE_BASE = 1 << 16
UP_ROWS = (D + FF) // BLOCK_SIDE
BLANK_ROW = (D + 2 * FF) // BLOCK_SIDE
ALL_ROWS = BLANK_ROW * BLOCK_SIDE
VMEM_MOST = 58 * 1024 * 1024
ALL_AXES = ("fz", "fx", "by", "core")
FRAME_AXES = ("fz", "fx")
TAP_OFFSETS = [(tap // 3 - 1) * GRID + tap % 3 - 1 for tap in range(9)]


def about(microseconds):
    return pl.CostEstimate(flops=0, bytes_accessed=int(microseconds * 3e6), transcendentals=0)


def in_vmem():
    return pl.BlockSpec(memory_space=pltpu.VMEM)


def anywhere():
    return pl.BlockSpec(memory_space=pl.ANY)


def matrix_places():
    places = []
    first = 0
    for row_count, col_count in matrix_shapes():
        cols = col_count // BLOCK_SIDE
        count = row_count // BLOCK_SIDE * cols
        places.append((first, count, cols))
        first = first + count
    return places


def tile_at(ref, row, col):
    row = pl.multiple_of(row * BLOCK_SIDE, BLOCK_SIDE)
    col = pl.multiple_of(col * BLOCK_SIDE, BLOCK_SIDE)
    return ref.at[pl.ds(row, BLOCK_SIDE), pl.ds(col, BLOCK_SIDE)]


def tile_of(matrix, code):
    return tile_at(matrix, lax.bitwise_and(lax.shift_right_logical(code, 5), 63), lax.bitwise_and(code, 31))


def load_blocks(tiles, buffers, matrix, sems, matrices, base=0, count=None):
    for buffer in buffers:
        def one_load(place, carry, buffer=buffer, base=base):
            code = tiles[base + place]
            which = lax.shift_right_logical(code, 11)

            @pl.when(which < matrices)
            def _():
                pltpu.make_async_copy(buffer.at[place], tile_of(matrix, code), sems.at[which]).start()

            return carry

        if count is None:
            lax.fori_loop(0, buffer.shape[0], one_load, 0, unroll=4)
        else:
            lax.fori_loop(0, count, one_load, 0)
        base = base + buffer.shape[0]


def wait_whole(ref, sem):
    pltpu.make_async_copy(ref, ref, sem).wait()


def send_tile(code, buffers, tile, sem, first=0):
    for index, buffer in enumerate(buffers):
        @pl.when(lax.div(code, CODE_BASE) == first + index)
        def _():
            pltpu.make_async_copy(tile, buffer.at[lax.rem(code, CODE_BASE)], sem).start()


def normalized(values):
    centered = values - jnp.mean(values, -1, keepdims=True)
    spread = lax.rsqrt(jnp.mean(centered * centered, -1, keepdims=True) + NORM_EPSILON)
    return centered * spread, spread


def norm_back(grad, hat, spread, gain):
    scaled = grad * gain
    return spread * (
        scaled
        - jnp.mean(scaled, -1, keepdims=True)
        - hat * jnp.mean(scaled * hat, -1, keepdims=True)
    )


def project(tiles, early, buffers, early_buffers, seen, rows14):
    rows = seen.shape[0]
    steps = rows // OWN_ROWS
    count = len(buffers)

    def kernel(tiles, early, *refs):
        sources = refs[:count]
        seen, rows14, q, kv, low, own_low, w_qkv, sems = refs[count:]
        step = pl.program_id(0)

        @pl.when(step == 0)
        def _():
            base = 0
            if early_buffers:
                load_blocks(tiles, sources[:1], w_qkv, sems, 1, 0, early[0])
                base = sources[0].shape[0]
            load_blocks(tiles, sources[early_buffers:], w_qkv, sems, 1, base)

        hat, _ = normalized(seen[...].astype(F32))
        normed = (hat * rows14[0:1] + rows14[1:2]).astype(BF)
        low[...] = normed

        @pl.when(step == 0)
        def _():
            wait_whole(w_qkv, sems.at[0])

        kv[:, :D] = dot_low(normed, w_qkv[:, D : 2 * D], NN).astype(BF)
        kv[:, D:] = (dot_low(normed, w_qkv[:, 2 * D :], NN) + rows14[7:8]).astype(BF)

        def own(place):
            part = normed[:PAD_ROWS]
            query = (dot_low(part, w_qkv[:, :D], NN) + rows14[6:7]).astype(BF)
            q[place : place + PAD_ROWS] = query * jnp.asarray(1.0 / math.sqrt(HD), BF)
            own_low[place : place + PAD_ROWS] = part

        @pl.when(step == 0)
        def _():
            own(0)

        @pl.when(step == steps - 1)
        def _():
            own(PAD_ROWS)

    def whole(shape):
        return pl.BlockSpec(shape, lambda i, tiles, early: (0, 0))

    def moving(width):
        return pl.BlockSpec((OWN_ROWS, width), lambda i, tiles, early: (i, 0))

    return pl.pallas_call(
        kernel,
        grid_spec=pltpu.PrefetchScalarGridSpec(
            num_scalar_prefetch=2,
            grid=(steps,),
            in_specs=[anywhere()] * count + [moving(D), whole((14, D))],
            out_specs=[whole((OWN_ROWS, D)), moving(2 * D), moving(D), whole((OWN_ROWS, D)), whole((D, 3 * D))],
            scratch_shapes=[pltpu.SemaphoreType.DMA((1,))],
        ),
        out_shape=[
            jax.ShapeDtypeStruct((OWN_ROWS, D), BF),
            jax.ShapeDtypeStruct((rows, 2 * D), BF),
            jax.ShapeDtypeStruct((rows, D), BF),
            jax.ShapeDtypeStruct((OWN_ROWS, D), BF),
            jax.ShapeDtypeStruct((D, 3 * D), BF),
        ],
        compiler_params=pltpu.CompilerParams(vmem_limit_bytes=VMEM_MOST),
        cost_estimate=about(15),
    )(tiles, early, *buffers, seen, rows14)


ROW_STEP = 16


def stacked(values):
    first = lax.broadcasted_iota(jnp.int32, (1, PAIR), 1) < HD
    nothing = jnp.zeros_like(values)
    return jnp.concatenate([jnp.where(first, values, nothing), jnp.where(first, nothing, values)], axis=0)


def unstacked(values):
    first = lax.broadcasted_iota(jnp.int32, (1, PAIR), 1) < HD
    return jnp.where(first, values[:PAD_ROWS], values[PAD_ROWS:])


def attend_kernel(long_rows, q, k, v, bias, out, logs, scores, soft):
    total = k.shape[0]
    for frame, (lo, hi) in enumerate(((0, long_rows), (long_rows, total))):
        rows = slice(frame * PAD_ROWS, (frame + 1) * PAD_ROWS)
        width = hi - lo
        scores[:, :width] = dot_low(stacked(q[rows, :]), k[lo:hi, :], NT_)
        norms, peaks = [], []
        for row in range(0, OWN_ROWS, ROW_STEP):
            block = scores[row : row + ROW_STEP, :width] + bias[:, lo:hi]
            peak = jnp.max(block, axis=1, keepdims=True)
            weights = jnp.exp(block - peak)
            norms.append(jnp.sum(weights, axis=1, keepdims=True))
            peaks.append(peak)
            soft[row : row + ROW_STEP, :width] = weights.astype(BF)
        norm = jnp.concatenate(norms, axis=0)
        out[rows, :] = unstacked(dot_low(soft[:, :width], v[lo:hi, :], NN) / norm).astype(BF)
        logs[rows, :] = unstacked(jnp.broadcast_to(jnp.concatenate(peaks, axis=0) + jnp.log(norm), (OWN_ROWS, PAIR)))


def attend_back_kernel(long_rows, q, k, v, bias, out, logs, grad, dq, dk, dv, scores, soft_grads, soft, changes):
    total = k.shape[0]
    for frame, (lo, hi) in enumerate(((0, long_rows), (long_rows, total))):
        rows = slice(frame * PAD_ROWS, (frame + 1) * PAD_ROWS)
        width = hi - lo
        query, arriving = stacked(q[rows, :]), stacked(grad[rows, :])
        products = stacked(grad[rows, :].astype(F32) * out[rows, :].astype(F32))
        delta = jnp.sum(products, axis=1, keepdims=True)
        log = jnp.concatenate([logs[rows, 0:1], logs[rows, HD : HD + 1]], axis=0)
        scores[:, :width] = dot_low(query, k[lo:hi, :], NT_)
        soft_grads[:, :width] = dot_low(arriving, v[lo:hi, :], NT_)
        for row in range(0, OWN_ROWS, ROW_STEP):
            here = slice(row, row + ROW_STEP)
            weights = jnp.exp(scores[here, :width] + bias[:, lo:hi] - log[here])
            soft[here, :width] = weights.astype(BF)
            changes[here, :width] = (weights * (soft_grads[here, :width] - delta[here])).astype(BF)
        part = unstacked(dot_low(changes[:, :width], k[lo:hi, :], NN))
        dq[rows, :] = (part * (1.0 / math.sqrt(HD))).astype(BF)
        dk[lo:hi, :] = dot_low(query, changes[:, :width], TN).T.astype(BF)
        dv[lo:hi, :] = dot_low(arriving, soft[:, :width], TN).T.astype(BF)


def pair_spec(rows, offset=0):
    return pl.BlockSpec((rows, PAIR), lambda i: (0, i + offset))


def attend(q, kv, bias):
    keys_total = kv.shape[0]
    long_rows = keys_total - OWN_ROWS

    def kernel(*refs):
        attend_kernel(long_rows, *refs)

    return pl.pallas_call(
        kernel,
        grid=(PAIRS,),
        in_specs=[
            pair_spec(OWN_ROWS),
            pair_spec(keys_total),
            pair_spec(keys_total, PAIRS),
            pl.BlockSpec((1, keys_total), lambda i: (0, 0)),
        ],
        out_specs=[pair_spec(OWN_ROWS)] * 2,
        out_shape=[jax.ShapeDtypeStruct((OWN_ROWS, D), BF), jax.ShapeDtypeStruct((OWN_ROWS, D), F32)],
        scratch_shapes=[pltpu.VMEM((OWN_ROWS, long_rows), F32), pltpu.VMEM((OWN_ROWS, long_rows), BF)],
        compiler_params=pltpu.CompilerParams(vmem_limit_bytes=VMEM_MOST),
        cost_estimate=about(12),
    )(q, kv, kv, bias.reshape(1, -1))


def attend_back(pairs, before, q, kv, bias, out, logs, grad):
    keys_total = kv.shape[0]
    long_rows = keys_total - OWN_ROWS
    start, count = pairs

    def kernel(*refs):
        attend_back_kernel(long_rows, *refs[:7], *refs[7 + len(before) :])

    def spec(rows, offset=0):
        return pair_spec(rows, offset + start)

    return pl.pallas_call(
        kernel,
        grid=(count,),
        in_specs=[
            spec(OWN_ROWS),
            spec(keys_total),
            spec(keys_total, PAIRS),
            pl.BlockSpec((1, keys_total), lambda i: (0, 0)),
            spec(OWN_ROWS),
            spec(OWN_ROWS),
            spec(OWN_ROWS),
        ]
        + [anywhere()] * len(before),
        out_specs=[spec(OWN_ROWS), spec(keys_total), spec(keys_total)],
        out_shape=[
            jax.ShapeDtypeStruct((OWN_ROWS, D), BF),
            jax.ShapeDtypeStruct((keys_total, D), BF),
            jax.ShapeDtypeStruct((keys_total, D), BF),
        ],
        scratch_shapes=[pltpu.VMEM((OWN_ROWS, long_rows), F32)] * 2 + [pltpu.VMEM((OWN_ROWS, long_rows), BF)] * 2,
        input_output_aliases={7 + i: i for i in range(len(before))},
        compiler_params=pltpu.CompilerParams(vmem_limit_bytes=VMEM_MOST),
        cost_estimate=about(4 * count),
    )(q, kv, kv, bias.reshape(1, -1), out, logs, grad, *before)


def lane_masks():
    lane = np.arange(LANES)
    inner = lane % PAD_ROWS
    token = (lane < OWN_ROWS) & (inner < FRAME_ROWS)
    row, col = inner // GRID, inner % GRID
    masks = []
    for tap in range(9):
        far_row, far_col = row + tap // 3 - 1, col + tap % 3 - 1
        masks.append(token & (far_row >= 0) & (far_row < GRID) & (far_col >= 0) & (far_col < GRID))
    masks.append(token & (lane < PAD_ROWS))
    masks.append(token & (lane >= PAD_ROWS))
    masks = masks + [np.zeros(LANES, bool)] * (16 - len(masks))
    return np.stack(masks).astype(np.float32)


def ahead(values, offset):
    return values if offset == 0 else pltpu.roll(values, (-offset) % LANES, axis=1)


def cumulative(values):
    return 0.5 + 0.5 * lax.erf(values * math.sqrt(0.5))


def gelu_slope(values, portion):
    return portion + values * jnp.exp(-0.5 * values * values) * (1.0 / math.sqrt(2.0 * math.pi))


def column_sum(values):
    return jnp.sum(values, axis=0, keepdims=True)


def widened(values):
    return jnp.concatenate([values, jnp.zeros((values.shape[0], LANES - OWN_ROWS), values.dtype)], axis=1)


def wait_tiles(matrix, count, sem):
    side = D // BLOCK_SIDE
    rest = count
    while rest >= side:
        rows = min(rest // side, BLANK_ROW)
        wait_whole(matrix.at[: rows * BLOCK_SIDE], sem)
        rest = rest - rows * side
    for _ in range(rest):
        wait_whole(tile_at(matrix, 0, 0), sem)


def middle_kernel(weight_count, first_buffer, held_tiles, sent_tiles, targets, *refs):
    sources = refs[:weight_count]
    (
        att, own, cot, rows14, conv_t, taps_forward, taps_backward, tail_bias, masks,
        learned, grad_mixed, grad_att, vectors, grad_up_bias, grad_conv, grad_tail, grad_tail_bias,
    ) = refs[weight_count : weight_count + 17]
    buffers = refs[weight_count + 17 : -10]
    (
        w_all, d_all, activated, slopes, normed, hat_two, mixed, gathered_sum, load_sems, send_sems,
    ) = refs[-10:]
    chunks = FF // D
    side = D // BLOCK_SIDE
    w_out = w_all.at[:D]
    w_up = [w_all.at[(1 + chunk) * D : (2 + chunk) * D] for chunk in range(chunks)]
    w_down = [w_all.at[(1 + chunks + chunk) * D : (2 + chunks + chunk) * D] for chunk in range(chunks)]
    d_out = d_all.at[:D]
    d_up = [d_all.at[(1 + chunk) * D : (2 + chunk) * D] for chunk in range(chunks)]
    d_down = [d_all.at[(1 + chunks + chunk) * D : (2 + chunks + chunk) * D] for chunk in range(chunks)]

    load_blocks(held_tiles, sources, w_all, load_sems, 3)
    d_all[ALL_ROWS:, :BLOCK_SIDE] = jnp.zeros((BLOCK_SIDE, BLOCK_SIDE), BF)
    wait_whole(w_out, load_sems.at[0])
    start = own[...].astype(F32) + dot_low(att[...], w_out[...], NN) + rows14[8:9]
    mixed[...] = start
    hat, spread_two = normalized(start)
    hat_two[...] = hat
    normed[...] = (hat * rows14[2:3] + rows14[3:4]).astype(BF)
    gathered_sum[...] = start + rows14[13:14]
    wait_whole(w_all.at[D : D + FF], load_sems.at[1])
    wait_whole(w_all.at[D + FF : D + 2 * FF], load_sems.at[2])

    for chunk in range(chunks):
        hidden = dot_low(normed[...], w_up[chunk][...], NN) + rows14[9 + chunk : 10 + chunk]
        portion = cumulative(hidden)
        active = (hidden * portion).astype(BF)
        activated[chunk] = active
        slopes[chunk] = gelu_slope(hidden, portion)
        gathered_sum[...] += dot_low(active, w_down[chunk][...], NN)

    out_two = gathered_sum[...]
    hat, spread_three = normalized(out_two)
    low_three = (hat * rows14[4:5] + rows14[5:6]).astype(BF)

    taps = widened(dot_low(conv_t[...], low_three, NT_))
    first = tail_bias[:, 0:1]
    for tap in range(9):
        first = first + ahead(taps[NT * tap : NT * (tap + 1)], TAP_OFFSETS[tap]) * masks[tap : tap + 1]

    def around(values, sign):
        order = range(9) if sign > 0 else range(8, -1, -1)
        return jnp.concatenate(
            [
                ahead(values, sign * TAP_OFFSETS[tap]) * masks[seen : seen + 1]
                for tap, seen in zip(range(9), order)
            ],
            axis=0,
        )

    before, stacks, portions = [first], [], []
    for layer in range(3):
        portions.append(cumulative(before[-1]))
        stacks.append(around(before[-1] * portions[-1], 1))
        before.append(dot_wide(taps_forward[layer], stacks[-1], NN) + tail_bias[:, layer + 1 : layer + 2])
    maps = 1.0 / (1.0 + jnp.exp(-before[3]))
    both = jnp.concatenate([maps * masks[9:10], maps * masks[10:11]], axis=0)[:, :OWN_ROWS]
    both = halves(both)
    out_parts = halves(out_two)
    arriving = cot[...]
    learned[...] = dot_parts(both, out_parts, NN)
    seen_maps = widened(dot_low(arriving, out_parts[0], NT_) + dot_low(arriving, out_parts[1], NT_))
    grad = (seen_maps[:NT] * masks[9:10] + seen_maps[NT:] * masks[10:11]) * maps * (1.0 - maps)
    sums = [None] * 4
    for layer in (2, 1, 0):
        sums[layer + 1] = jnp.sum(grad, axis=1, keepdims=True)
        grad_tail[layer] = dot_wide(stacks[layer], grad, NT_)
        grad = dot_wide(taps_backward[layer], around(grad, -1), NN)
        grad = grad * gelu_slope(before[layer], portions[layer])
    grad = grad.astype(BF).astype(F32)
    sums[0] = jnp.sum(grad, axis=1, keepdims=True)
    grad_tail_bias[...] = jnp.concatenate(sums, axis=1)
    grad_taps = around(grad, -1)[:, :OWN_ROWS].astype(BF)
    grad_conv[...] = dot_low(grad_taps, low_three, NN)
    grad_norm_three = dot_low(grad_taps, conv_t[...], TN)
    vectors[2:3] = column_sum(grad_norm_three * hat)
    vectors[3:4] = column_sum(grad_norm_three)
    grad_out = (
        norm_back(grad_norm_three, hat, spread_three, rows14[4:5])
        + dot_low(both[0], arriving, TN)
        + dot_low(both[1], arriving, TN)
    )
    grad_down = grad_out.astype(BF)
    vectors[5:6] = column_sum(grad_down.astype(F32))

    for chunk in range(chunks):
        grad_active = dot_low(grad_down, w_down[chunk][...], NT_)
        grad_hidden = (grad_active * slopes[chunk]).astype(BF)
        grad_up_bias[chunk : chunk + 1] = column_sum(grad_hidden.astype(F32))
        part = dot_low(grad_hidden, w_up[chunk][...], NT_)
        if chunk == 0:
            gathered_sum[...] = part
        else:
            gathered_sum[...] += part
        d_down[chunk][...] = dot_low(activated[chunk], grad_down, TN).astype(BF)
        d_up[chunk][...] = dot_low(normed[...], grad_hidden, TN).astype(BF)

    base = 0
    for buffer in buffers:
        def one_tile(place, carry, buffer=buffer, base=base):
            code = sent_tiles[base + place]

            @pl.when(code >= 2048)
            def _():
                pltpu.make_async_copy(tile_of(d_all, code), buffer.at[place], send_sems.at[1]).start()

            return carry

        lax.fori_loop(0, buffer.shape[0], one_tile, 0, unroll=4)
        base = base + buffer.shape[0]

    grad_norm_two = gathered_sum[...]
    vectors[0:1] = column_sum(grad_norm_two * hat_two[...])
    vectors[1:2] = column_sum(grad_norm_two)
    total = grad_out + norm_back(grad_norm_two, hat_two[...], spread_two, rows14[2:3])
    grad_mixed[...] = total
    branch = total.astype(BF)
    vectors[4:5] = column_sum(branch.astype(F32))
    d_out[...] = dot_low(att[...], branch, TN).astype(BF)

    def one_out(tile, carry):
        code = targets[matrix_places()[1][0] + tile]
        send_tile(code, buffers, tile_at(d_out, lax.div(tile, side), lax.rem(tile, side)), send_sems.at[0], first_buffer)
        return carry

    lax.fori_loop(0, matrix_places()[1][1], one_out, 0)
    grad_att[...] = dot_low(branch, w_out[...], NT_).astype(BF)
    wait_tiles(d_all, matrix_places()[1][1], send_sems.at[0])
    wait_tiles(d_all, targets.shape[0] - matrix_places()[1][1], send_sems.at[1])


def middle(held_tiles, sent_tiles, targets, weights, first_buffer, buffer_shapes, att, own, cot, rows14, conv_t, taps_forward, taps_backward, tail_bias):
    count = len(weights)

    def kernel(*refs):
        middle_kernel(count, first_buffer, *refs)

    def f32(*shape):
        return jax.ShapeDtypeStruct(shape, F32)

    outs = [
        f32(2 * NT, D), f32(OWN_ROWS, D), jax.ShapeDtypeStruct((OWN_ROWS, D), BF), f32(8, D),
        f32(FF // D, D), f32(9 * NT, D), f32(3, 9 * NT, NT), f32(NT, 4),
    ]
    results = pl.pallas_call(
        kernel,
        grid_spec=pltpu.PrefetchScalarGridSpec(
            num_scalar_prefetch=3,
            grid=(1,),
            in_specs=[anywhere()] * count + [in_vmem()] * 9,
            out_specs=[in_vmem()] * len(outs) + [anywhere()] * len(buffer_shapes),
            scratch_shapes=[
                pltpu.VMEM((ALL_ROWS + BLOCK_SIDE, D), BF),
                pltpu.VMEM((ALL_ROWS + BLOCK_SIDE, D), BF),
                pltpu.VMEM((FF // D, OWN_ROWS, D), BF),
                pltpu.VMEM((FF // D, OWN_ROWS, D), F32),
                pltpu.VMEM((OWN_ROWS, D), BF),
                pltpu.VMEM((OWN_ROWS, D), F32),
                pltpu.VMEM((OWN_ROWS, D), F32),
                pltpu.VMEM((OWN_ROWS, D), F32),
                pltpu.SemaphoreType.DMA((3,)),
                pltpu.SemaphoreType.DMA((2,)),
            ],
        ),
        out_shape=outs + buffer_shapes,
        compiler_params=pltpu.CompilerParams(vmem_limit_bytes=VMEM_MOST),
        cost_estimate=about(40),
    )(
        held_tiles, sent_tiles, targets, *weights, att, own, cot, rows14, conv_t, taps_forward, taps_backward, tail_bias,
        jnp.asarray(lane_masks()),
    )
    return results[: len(outs)], results[len(outs) :]


def qkv_grads(targets, low, own_low, dq, dk, dv, buffers, late):
    steps = low.shape[0] // OWN_ROWS
    count = len(buffers)

    def kernel(targets, low, own_low, dq, dk, dv, *refs):
        filled = refs[count : 2 * count]
        matrix = refs[2 * count]
        totals, sem = refs[2 * count + 1 :]
        step = pl.program_id(0)

        @pl.when(step == 0)
        def _():
            totals[...] = jnp.zeros_like(totals)
            matrix[:, :D] = dot_low(own_low[...], dq[...], TN).astype(BF)

        totals[:, :D] += dot_low(low[...], dk[...], TN)
        totals[:, D:] += dot_low(low[...], dv[...], TN)

        @pl.when(step == steps - 1)
        def _():
            matrix[:, D:] = totals[...].astype(BF)
            cols = 3 * D // BLOCK_SIDE

            def one_tile(tile, sent):
                code = targets[tile]
                send_tile(code, filled, tile_at(matrix, lax.div(tile, cols), lax.rem(tile, cols)), sem, late)
                return sent + (lax.div(code, CODE_BASE) >= late).astype(jnp.int32)

            sent = lax.fori_loop(0, QKV_BLOCKS, one_tile, jnp.int32(0))

            def one_wait(index, carry):
                wait_whole(tile_at(matrix, 0, 0), sem)
                return carry

            lax.fori_loop(0, sent, one_wait, 0)

    def whole(shape):
        return pl.BlockSpec(shape, lambda i, targets: (0, 0))

    def moving(width):
        return pl.BlockSpec((OWN_ROWS, width), lambda i, targets: (i, 0))

    results = pl.pallas_call(
        kernel,
        grid_spec=pltpu.PrefetchScalarGridSpec(
            num_scalar_prefetch=1,
            grid=(steps,),
            in_specs=[moving(D), whole((OWN_ROWS, D)), whole((OWN_ROWS, D)), moving(D), moving(D)]
            + [anywhere()] * count,
            out_specs=[anywhere()] * count + [whole((D, 3 * D))],
            scratch_shapes=[pltpu.VMEM((D, 2 * D), F32), pltpu.SemaphoreType.DMA],
        ),
        out_shape=[jax.ShapeDtypeStruct(b.shape, b.dtype) for b in buffers]
        + [jax.ShapeDtypeStruct((D, 3 * D), BF)],
        input_output_aliases={6 + i: i for i in range(count)},
        compiler_params=pltpu.CompilerParams(vmem_limit_bytes=VMEM_MOST),
        cost_estimate=about(14),
    )(targets, low, own_low, dq, dk, dv, *buffers)
    return results[:count], results[count]


def input_grads(seen, own, dq, dk, dv, w_qkv):
    rows = seen.shape[0]
    steps = rows // OWN_ROWS

    def kernel(seen, own, dq, dk, dv, w_qkv, grad_seen, grad_own, sums):
        step = pl.program_id(0)

        @pl.when(step == 0)
        def _():
            grad = dot_low(dq[...], w_qkv[:, :D], NT_)
            grad_own[...] = grad
            hat, _ = normalized(own[...].astype(F32))
            sums[...] = jnp.zeros_like(sums)
            sums[0:1] = column_sum(grad * hat)
            sums[1:2] = column_sum(grad)
            sums[2:3] = column_sum(dq[...].astype(F32))

        grad = dot_low(dk[...], w_qkv[:, D : 2 * D], NT_) + dot_low(dv[...], w_qkv[:, 2 * D :], NT_)
        grad_seen[...] = grad.astype(BF)
        hat, _ = normalized(seen[...].astype(F32))
        sums[0:1] += column_sum(grad * hat)
        sums[1:2] += column_sum(grad)
        sums[3:4] += column_sum(dv[...].astype(F32))

    def whole(shape):
        return pl.BlockSpec(shape, lambda i: (0, 0))

    moving = pl.BlockSpec((OWN_ROWS, D), lambda i: (i, 0))
    return pl.pallas_call(
        kernel,
        grid=(steps,),
        in_specs=[moving, whole((OWN_ROWS, D)), whole((OWN_ROWS, D)), moving, moving, whole((D, 3 * D))],
        out_specs=[moving, whole((OWN_ROWS, D)), whole((8, D))],
        out_shape=[
            jax.ShapeDtypeStruct((rows, D), BF),
            jax.ShapeDtypeStruct((OWN_ROWS, D), F32),
            jax.ShapeDtypeStruct((8, D), F32),
        ],
        compiler_params=pltpu.CompilerParams(vmem_limit_bytes=VMEM_MOST),
        cost_estimate=about(12),
    )(seen, own, dq, dk, dv, w_qkv)


def moved(value, axis, size, step):
    return lax.ppermute(value, axis, [(i, (i + step) % size) for i in range(size)])


def reduce_axis(terms, axis, size, dim=0):
    total = lax.index_in_dim(terms, 0, dim, keepdims=False).astype(F32)
    for step in range(1, size):
        term = lax.index_in_dim(terms, step, dim, keepdims=False)
        total = total + moved(term, axis, size, step).astype(F32)
    return total


def after(value, *others):
    return lax.optimization_barrier((value, others))[0]


def gather_axis(value, axis, size):
    return jnp.stack([value] + [moved(value, axis, size, -step) for step in range(1, size)])


def line_step(state, axis, size):
    onward, backward = state
    up = [(i, i + 1) for i in range(size - 1)]
    down = [(i + 1, i) for i in range(size - 1)]
    return lax.ppermute(onward, axis, down), lax.ppermute(backward, axis, up)


def line_pieces(value, steps, axis, size):
    coord = lax.axis_index(axis)
    pieces = [value]
    for step in range(1, size):
        pieces.append(jnp.where(coord + step < size, steps[step - 1][0], steps[size - step - 1][1]))
    return pieces


def rolled(value, axis, size, step):
    return lax.dynamic_slice_in_dim(jnp.concatenate([value, value], axis), step, size, axis)


def small_shares(vector, sizes, coords):
    device_count = math.prod(sizes)
    share = -(-vector.shape[0] // (device_count * 128)) * 128
    shares = jnp.pad(vector, (0, device_count * share - vector.shape[0])).reshape(sizes + (share,))
    for axis, size in enumerate(sizes):
        shares = rolled(shares, axis, size, coords[axis])
    return shares.transpose(3, 1, 2, 0, 4)


def small_step(shares, axis, sizes):
    return reduce_axis(shares, ALL_AXES[axis], sizes[axis])


def early_slots(slots_dev):
    return slots_dev * 6 // 14


def slot_chunks(slots_dev):
    early = early_slots(slots_dev)
    late = slots_dev - early
    chunks = []
    first = 0
    for index, count in enumerate((early - early // 2, early // 2, late - late // 2, late // 2)):
        chunks.append((first, count, ("fx", "by", "fz") if index % 2 == 0 else ("by", "fx", "fz")))
        first = first + count
    return chunks


def send_table(block_owner, sizes, coords, slots_dev):
    nz, nx, ny, nc = sizes
    slots = jnp.arange(block_owner.shape[0], dtype=jnp.int32)
    device = slots // slots_dev
    place = {}
    for axis in range(3, -1, -1):
        place[ALL_AXES[axis]] = (device % sizes[axis] - coords[axis] + sizes[axis]) % sizes[axis]
        device = device // sizes[axis]
    is_late = (block_owner < QKV_BLOCKS).astype(jnp.int32).reshape(-1, slots_dev)
    late_before = jnp.cumsum(is_late, 1) - is_late
    early_before = jnp.arange(slots_dev, dtype=jnp.int32)[None] - late_before
    late_count = jnp.sum(is_late, 1, keepdims=True)
    ranks = jnp.where(is_late == 1, slots_dev - late_count + late_before, early_before)
    rank = ranks.reshape(-1)
    size_of = dict(zip(ALL_AXES, sizes))
    code = jnp.zeros_like(slots)
    chunks = slot_chunks(slots_dev)
    device_count = nz * nx * ny * nc
    for index, (first, count, axes) in enumerate(chunks):
        at = jnp.zeros_like(slots)
        for name in axes:
            at = at * size_of[name] + place[name]
        at = at * count + rank - first
        if index % 2:
            at = at + device_count // nc * chunks[index - 1][1]
        inside = (rank >= first) & (rank < first + count)
        code = jnp.where(inside, (index // 2 * 2 + place["core"]) * CODE_BASE + at, code)
    owned = block_owner[:, None] == slots[None, :]
    table = jnp.sum(jnp.where(owned, code[:, None], 0), 0)
    early = early_slots(slots_dev)
    late_size = device_count // nc * (slots_dev - early)
    early_size = device_count // nc * early
    buffer, at = code // CODE_BASE, code % CODE_BASE
    sent_at = jnp.where(buffer < 2, buffer * early_size, 2 * early_size + (buffer - 2) * late_size) + at
    held_at = jnp.where(buffer < 2, slots // slots_dev * early + rank, 2 * early_size + (buffer - 2) * late_size + at)
    tile = tile_code(block_owner)
    held_tiles = jnp.sum(jnp.where(held_at[:, None] == slots[None, :], tile[:, None], 0), 0)
    sent_tiles = jnp.sum(jnp.where(sent_at[:, None] == slots[None, :], tile[:, None], 0), 0)
    qkv_cols = 3 * D // BLOCK_SIDE
    qkv_tile = jnp.where(block_owner < QKV_BLOCKS, block_owner // qkv_cols * 32 + block_owner % qkv_cols, 2048)
    qkv_tiles = jnp.sum(jnp.where(held_at[:, None] == slots[None, :], qkv_tile[:, None], 0), 0)
    return table, qkv_tiles, held_tiles, sent_tiles, ranks, jnp.max(late_count)


def tile_code(block):
    side = D // BLOCK_SIDE
    out_tile = block - matrix_places()[1][0]
    up_tile = block - matrix_places()[2][0]
    down_tile = block - matrix_places()[3][0]
    up_row, up_col = up_tile // (FF // BLOCK_SIDE), up_tile % (FF // BLOCK_SIDE)
    row = jnp.where(
        up_tile < 0,
        out_tile // side,
        jnp.where(down_tile < 0, side + up_col // side * side + up_row, UP_ROWS + down_tile // side),
    )
    col = jnp.where(up_tile < 0, out_tile % side, jnp.where(down_tile < 0, up_col % side, down_tile % side))
    matrix = jnp.where(up_tile < 0, 0, jnp.where(down_tile < 0, 1, 2))
    used = (out_tile >= 0) & (block < MATRIX_BLOCKS)
    return jnp.where(used, matrix * 2048 + row * 32 + col, 3 * 2048 + BLANK_ROW * 32)


def reduce_core(kept, sent, chunks, sizes):
    size_of = dict(zip(ALL_AXES, sizes))
    received = moved(sent, "core", 2, 1)
    parts = []
    start = 0
    for first, count, axes in chunks:
        shape = [size_of[name] for name in axes[1:]] + [count, BLOCK_SIDE, BLOCK_SIDE]
        length = math.prod(shape[:-2])
        terms = []
        for _ in range(size_of[axes[0]]):
            stop = start + length
            total = kept[start:stop].astype(F32) + received[start:stop].astype(F32)
            terms.append(total.astype(BF).reshape(shape))
            start = stop
        parts.append(terms)
    return parts


def reduce_stage(parts, chunks, stage, sizes):
    results = []
    for terms, (first, count, axes) in zip(parts, chunks):
        received = [moved(terms[step], axes[stage], len(terms), step) for step in range(1, len(terms))]
        following = []
        for index in range(terms[0].shape[0]):
            total = terms[0][index].astype(F32)
            for term in received:
                total = total + term[index].astype(F32)
            following.append(total.astype(BF))
        results.append(following)
    return results


def reduce_last(parts, sizes):
    terms = [jnp.concatenate(pieces) for pieces in zip(*parts)]
    total = terms[0].astype(F32)
    for step in range(1, len(terms)):
        total = total + moved(terms[step], "fz", sizes[0], step).astype(F32)
    return total


def gather_stage(shard, axes, stage, sizes):
    name = axes[len(axes) - 1 - stage]
    return gather_axis(shard, name, sizes[ALL_AXES.index(name)])


def gather_last(shards, orders, sizes):
    pieces = []
    for shard, axes in zip(shards, orders):
        size = sizes[ALL_AXES.index(axes[0])]
        pieces = pieces + [shard] + [moved(shard, axes[0], size, -step) for step in range(1, size)]
    return [piece.reshape(-1, BLOCK_SIDE, BLOCK_SIDE) for piece in pieces]


def sorted_shards(device_index, block_owner, master):
    slots_dev = master.shape[0]
    early = early_slots(slots_dev)
    chunks = [(0, early, ()), (early, slots_dev - early, ())]

    def kernel(where, owner, blocks, *outs):
        base = where[0] * slots_dev
        late_count = jnp.int32(0)
        for slot in range(slots_dev):
            late_count = late_count + (owner[base + slot] < QKV_BLOCKS).astype(jnp.int32)
        early_at, late_at = jnp.int32(0), slots_dev - late_count
        for slot in range(slots_dev):
            late = owner[base + slot] < QKV_BLOCKS
            rank = jnp.where(late, late_at, early_at)
            late_at = late_at + late.astype(jnp.int32)
            early_at = early_at + 1 - late.astype(jnp.int32)
            for index, (first, count, axes) in enumerate(chunks):
                if count == 0:
                    continue

                @pl.when((rank >= first) & (rank < first + count))
                def _(index=index, first=first):
                    outs[index][rank - first] = blocks[slot].astype(BF)

    return pl.pallas_call(
        kernel,
        grid_spec=pltpu.PrefetchScalarGridSpec(
            num_scalar_prefetch=2,
            grid=(1,),
            in_specs=[in_vmem()],
            out_specs=[in_vmem()] * len(chunks),
        ),
        out_shape=[
            jax.ShapeDtypeStruct((max(count, 1), BLOCK_SIDE, BLOCK_SIDE), BF) for first, count, axes in chunks
        ],
        cost_estimate=about(3),
    )(device_index.reshape(1), block_owner, master)


def spread_early(targets, matrix, buffer_shapes):
    count = len(buffer_shapes)

    def kernel(targets, matrix, blank, *refs):
        buffers, sem = refs[:count], refs[count]

        def one_block(block, sent):
            code = targets[block]
            cols = 3 * D // BLOCK_SIDE
            early = lax.div(code, CODE_BASE) < 2

            @pl.when(early & (block < QKV_BLOCKS))
            def _():
                tile = tile_at(matrix, lax.div(block, cols), lax.rem(block, cols))
                send_tile(code, buffers, tile, sem)

            @pl.when(early & (block >= QKV_BLOCKS))
            def _():
                send_tile(code, buffers, blank, sem)

            return sent + early.astype(jnp.int32)

        sent = lax.fori_loop(0, targets.shape[0], one_block, jnp.int32(0))

        def one_wait(index, carry):
            wait_whole(blank, sem)
            return carry

        lax.fori_loop(0, sent, one_wait, 0)

    return pl.pallas_call(
        kernel,
        grid_spec=pltpu.PrefetchScalarGridSpec(
            num_scalar_prefetch=1,
            grid=(1,),
            in_specs=[in_vmem()] * 2,
            out_specs=[anywhere()] * count,
            scratch_shapes=[pltpu.SemaphoreType.DMA],
        ),
        out_shape=buffer_shapes,
        compiler_params=pltpu.CompilerParams(vmem_limit_bytes=VMEM_MOST),
    )(targets, matrix, jnp.zeros((BLOCK_SIDE, BLOCK_SIDE), BF))


def pad_frames(values):
    frames = values.reshape(2, FRAME_ROWS, values.shape[-1])
    return jnp.pad(frames, ((0, 0), (0, PAD_ROWS - FRAME_ROWS), (0, 0)))


def on_device(
    tokens,
    cotangent,
    clip_lengths,
    clip_order,
    block_owner,
    master,
    moment1,
    moment2,
    stat_left,
    stat_right,
    basis_left,
    basis_right,
    small_params,
    small_moment1,
    small_moment2,
):
    sizes = tuple(lax.axis_size(name) for name in ALL_AXES)
    coords = [lax.axis_index(name) for name in ALL_AXES]
    nz, nx, ny, nc = sizes
    device_count = nz * nx * ny * nc
    frame_count = nz * nx
    frame_index = coords[0] * nx + coords[1]
    slots_dev = master.shape[0]

    segment_slots = clip_segments(
        clip_lengths[0], clip_order[0], 2 * frame_count, 2, frame_count
    ).reshape(frame_count, 2)
    ordered_len = clip_lengths[0][clip_order[0]]
    longest = jnp.argmax(ordered_len).astype(jnp.int32)
    second_long = segment_slots[:, 1] == longest
    short_segment = jnp.where(second_long, segment_slots[:, 0], segment_slots[:, 1])
    swap = second_long[frame_index]
    padded_segment = jnp.pad(short_segment, (1, 1), constant_values=-1)
    near = lax.dynamic_slice_in_dim(padded_segment, frame_index, 3)
    with_previous = near[0] == near[1]
    with_next = near[2] == near[1]

    device_index = ((coords[0] * nx + coords[1]) * ny + coords[2]) * nc + coords[3]
    early = early_slots(slots_dev)
    chunks = slot_chunks(slots_dev)
    shards = sorted_shards(device_index, block_owner, master)
    orders = [axes for first, count, axes in chunks]
    late_shards = gather_axis(shards[1], "fz", nz)

    own_frames = pad_frames(tokens[0])
    own_frames = jnp.where(swap, own_frames[::-1], own_frames)
    long_frame, short_frame = own_frames[0], own_frames[1]
    frame_perm = [(i, (i + 1) % frame_count) for i in range(frame_count)]
    back_perm = [(j, i) for i, j in frame_perm]
    frames_seen = frame_count + 2
    own = own_frames.reshape(OWN_ROWS, D)
    row_ids = jnp.arange(frames_seen * PAD_ROWS, dtype=jnp.int32)
    hidden_key = (row_ids % PAD_ROWS >= FRAME_ROWS) | (
        (row_ids >= (frames_seen - 1) * PAD_ROWS) & ~(with_previous | with_next)
    )
    key_bias = jnp.where(hidden_key, MASK_FLOOR, 0.0).astype(F32)

    targets, qkv_tiles, held_tiles, sent_tiles, ranks, late_most = send_table(block_owner, sizes, coords, slots_dev)
    own_ranks = lax.dynamic_index_in_dim(ranks, device_index, 0, keepdims=False)
    late_fits = late_most <= slots_dev - early

    split = unpack(small_params)
    rows14 = small_params[: 14 * D].reshape(14, D)
    conv_t = split["conv_first"].astype(BF).reshape(D, 9 * NT).T
    tail = jnp.stack([split["conv_second"], split["conv_third"], split["conv_fourth"]])
    taps_forward = tail.transpose(0, 3, 1, 2).reshape(3, NT, 9 * NT)
    taps_backward = tail.transpose(0, 2, 1, 3).reshape(3, NT, 9 * NT)
    tail_bias = split["conv_bias"].T
    arriving = cotangent[0].reshape(2, NT, D)
    arriving = jnp.where(swap, arriving[::-1], arriving).reshape(2 * NT, D)

    early_looked = jnp.where(late_fits, 0, device_count * early).astype(jnp.int32).reshape(1)
    stat_parts = stat_products(stat_left, stat_right, basis_left, basis_right)

    def gather_early(shard):
        return lax.all_gather(shard, ALL_AXES, axis=0, tiled=True)

    weights = [gather_early(shards[0])] if early else []
    long_pair = gather_axis(long_frame, "fx", nx)
    from_previous = lax.ppermute(short_frame, FRAME_AXES, frame_perm)
    from_next = lax.ppermute(short_frame, FRAME_AXES, back_perm)
    (
        long_pair, late_shards, from_previous, from_next, targets, qkv_tiles, held_tiles, sent_tiles, own_ranks, early_looked,
    ) = lax.optimization_barrier(
        (
            long_pair, late_shards, from_previous, from_next, targets, qkv_tiles, held_tiles, sent_tiles, own_ranks,
            early_looked,
        )
    )
    late_shards = [late_shards[:, : chunks[2][1]], late_shards[:, chunks[2][1] :]]
    late_shards = [gather_stage(part, orders[2 + i], 1, sizes) for i, part in enumerate(late_shards)]
    line = [line_step((long_pair, long_pair), "fz", nz)]
    partner = jnp.where(with_next, from_next, from_previous)
    (
        late_shards, line[0], partner, stat_parts, key_bias, rows14, conv_t, taps_forward, taps_backward, tail_bias, arriving,
    ) = lax.optimization_barrier(
        (
            late_shards, line[0], partner, stat_parts, key_bias, rows14, conv_t, taps_forward, taps_backward, tail_bias,
            arriving,
        )
    )
    late_pieces = gather_last(late_shards, orders[2:], sizes)
    line.append(line_step(line[-1], "fz", nz))


    weights = weights + late_pieces + [moved(piece, "core", nc, 1) for piece in late_pieces]
    for _ in range(nz - 3):
        line.append(line_step(line[-1], "fz", nz))
    long_frames = line_pieces(long_pair, line, "fz", nz)
    seen = jnp.concatenate(
        [frames.reshape(-1, D) for frames in long_frames] + [short_frame, partner]
    )
    query, key_value, low, own_low, w_qkv = project(
        qkv_tiles, early_looked, weights, 1 if early else 0, seen, rows14
    )
    attended, logs = attend(query, key_value, key_bias)
    buffer_shapes = []
    for slots in (early, slots_dev - early):
        if slots:
            shape = jax.ShapeDtypeStruct((device_count // nc * slots, BLOCK_SIDE, BLOCK_SIDE), BF)
            buffer_shapes = buffer_shapes + [shape, shape]
    (learned, grad_mixed, grad_att, vectors, grad_up_bias, grad_conv, grad_tail, grad_tail_bias), buffers = middle(
        held_tiles, sent_tiles, targets, weights, 0 if early else 2, buffer_shapes, attended, own, arriving, rows14, conv_t,
        taps_forward, taps_backward, tail_bias,
    )
    learned = learned.reshape(2, NT, D)
    learned = jnp.where(swap, learned[::-1], learned).reshape(2 * NT, D)

    halfway = reduce_core(*buffers[:2], chunks[:2], sizes) if early else []
    back = attend_back((0, PAIRS // 2), [], query, key_value, key_bias, attended, logs, grad_att)
    back, halfway = lax.optimization_barrier((back, halfway))
    halfway = reduce_stage(halfway, chunks, 0, sizes)
    grad_query, grad_key, grad_value = attend_back(
        (PAIRS // 2, PAIRS - PAIRS // 2), back, query, key_value, key_bias, attended, logs, grad_att
    )
    grad_query, halfway = lax.optimization_barrier((grad_query, halfway))
    halfway = reduce_stage(halfway, chunks, 1, sizes)
    late_buffers, grad_w_qkv = qkv_grads(
        targets, low, own_low, grad_query, grad_key, grad_value, list(buffers[-2:]), 2
    )
    grad_query, late_buffers, halfway = lax.optimization_barrier((grad_query, late_buffers, halfway))
    reduced = [reduce_last(halfway, sizes)] if early else []
    late_parts = reduce_core(*late_buffers, chunks[2:], sizes)
    grad_seen, grad_own, sums = input_grads(seen, own, grad_query, grad_key, grad_value, w_qkv)
    late_parts, reduced, grad_seen, sums = lax.optimization_barrier((late_parts, reduced, grad_seen, sums))

    late_parts = reduce_stage(late_parts, chunks[2:], 0, sizes)
    small_local = jnp.concatenate(
        [
            sums[:2].reshape(-1),
            vectors[:4].reshape(-1),
            sums[2:4].reshape(-1),
            vectors[4],
            grad_up_bias.reshape(-1),
            vectors[5],
            grad_conv.T.reshape(-1),
            grad_tail.reshape(-1),
            grad_tail_bias.T.reshape(-1),
        ]
    )
    small_total = small_local.shape[0]
    small = small_step(small_shares(small_local, sizes, coords), 3, sizes)
    late_parts, small, grad_seen = lax.optimization_barrier((late_parts, small, grad_seen))
    seen_frames = grad_seen.reshape(frames_seen, PAD_ROWS, D)
    long_terms = seen_frames[:frame_count].reshape(nz, nx, PAD_ROWS, D)
    partner_term = seen_frames[frame_count + 1]
    nothing = jnp.zeros_like(partner_term)
    to_previous = jnp.where(with_previous, partner_term, nothing)
    to_next = jnp.where(with_next, partner_term, nothing)
    late_parts = reduce_stage(late_parts, chunks[2:], 1, sizes)
    small = small_step(small, 1, sizes)
    late_parts, small, long_terms, to_previous, to_next = lax.optimization_barrier(
        (late_parts, small, long_terms, to_previous, to_next)
    )
    late_total = reduce_last(late_parts, sizes)
    small = small_step(small_step(small, 2, sizes), 0, sizes)
    long_terms = reduce_axis(long_terms, "fx", nx, 1).astype(BF)
    late_total, small, long_terms = lax.optimization_barrier((late_total, small, long_terms))
    if early:
        def whole_early(share):
            extra = reduce_core(*spread_early(targets, grad_w_qkv, buffer_shapes[:2]), chunks[:2], sizes)
            for stage in range(2):
                extra = reduce_stage(extra, chunks, stage, sizes)
            return share + reduce_last(extra, sizes)

        reduced = [lax.cond(late_fits, lambda share: share, whole_early, reduced[0])]
    owned_grads = jnp.concatenate(reduced + [late_total])

    squares = jnp.sum(owned_grads * owned_grads) + jnp.sum(small * small)
    carried = jnp.concatenate([small, jnp.full((128,), squares, F32)])
    carried = gather_axis(carried, "fz", nz)
    carried = gather_axis(carried, "fx", nx)
    raw = raw_products(own_ranks, owned_grads, basis_left, basis_right)
    carried = gather_axis(carried, "by", ny)
    carried, raw = lax.optimization_barrier((carried, raw))
    carried = gather_axis(carried, "core", nc)
    share = small.shape[0]
    grad_norm = jnp.sqrt(jnp.sum(carried[..., share]))
    factor = 1.0 / jnp.maximum(grad_norm, CLIP_NORM)
    long_terms, to_previous, to_next, factor = lax.optimization_barrier((long_terms, to_previous, to_next, factor))
    long_total = reduce_axis(long_terms, "fz", nz)
    from_next = lax.ppermute(to_previous, FRAME_AXES, back_perm)
    from_previous = lax.ppermute(to_next, FRAME_AXES, frame_perm)
    carried = carried[..., :share]
    for axis, size in enumerate(sizes):
        carried = rolled(carried, 3 - axis, size, size - coords[axis])
    small_grad = carried.transpose(3, 2, 1, 0, 4).reshape(-1)[:small_total]

    small_first, small_second, small_new = adam_update(
        small_grad * factor, small_params, small_moment1, small_moment2
    )

    soap_out = finish(
        factor.reshape(1), *raw, *stat_parts, stat_left, stat_right, basis_left, basis_right, master, moment1, moment2
    )
    short_total = seen_frames[frame_count].astype(F32) + from_next.astype(F32) + from_previous.astype(F32)
    grad_normed_one = jnp.concatenate([long_total, short_total]) + grad_own
    hat, spread = normalized(own.astype(F32))
    grad_inputs = grad_mixed + norm_back(grad_normed_one, hat, spread, rows14[0:1])
    grad_inputs = grad_inputs.reshape(2, PAD_ROWS, D)[:, :FRAME_ROWS]
    grad_inputs = jnp.where(swap, grad_inputs[::-1], grad_inputs).reshape(2 * FRAME_ROWS, D)
    return (
        learned[None],
        grad_inputs[None],
        soap_out[0],
        soap_out[1],
        soap_out[2],
        soap_out[3],
        soap_out[4],
        soap_out[5],
        soap_out[6],
        small_first,
        small_second,
        small_new,
        grad_norm,
    )


def solution(mesh):
    frames, batches = mesh.shape["frame"], mesh.shape["batch"]
    split = Mesh(mesh.devices.reshape(frames // 2, 2, batches // 2, 2), ALL_AXES)
    batch = ("by", "core")
    slots = P(ALL_AXES, None, None)
    rows = P(batch, FRAME_AXES, None)
    return jax.shard_map(
        on_device,
        mesh=split,
        in_specs=(rows, rows, P(batch, None), P(batch, None), P()) + (slots,) * 7 + (P(),) * 3,
        out_specs=(rows, rows) + (slots,) * 7 + (P(),) * 4,
        check_vma=False,
    )
```

```python
import math

import jax
import jax.numpy as jnp
import numpy as np
from jax import lax
from jax.experimental import pallas as pl
from jax.experimental.pallas import tpu as pltpu
from jax.sharding import Mesh
from jax.sharding import PartitionSpec as P

D = 768
HEADS = 12
HD = 64
FF = 3072
GRID = 14
NT = 8
BLOCK_SIDE = 128
STEP = 10
MATRIX_BLOCKS = 432


FULL_PRECISION = lax.Precision.HIGHEST
NORM_EPSILON = 1e-06
BETA_ONE = 0.9
BETA_TWO = 0.95
STAT_DECAY = 0.95
LEARN_RATE = 0.1
WEIGHT_DECAY = 0.01
ADAM_EPSILON = 1e-08
CLIP_NORM = 1.0
MASK_FLOOR = -1e30


def layout():
    return [
        ("gain_one", (D,)),
        ("shift_one", (D,)),
        ("gain_two", (D,)),
        ("shift_two", (D,)),
        ("gain_three", (D,)),
        ("shift_three", (D,)),
        ("bias_query", (D,)),
        ("bias_value", (D,)),
        ("bias_out", (D,)),
        ("bias_up", (FF,)),
        ("bias_down", (D,)),
        ("conv_first", (D, 9, NT)),
        ("conv_second", (9, NT, NT)),
        ("conv_third", (9, NT, NT)),
        ("conv_fourth", (9, NT, NT)),
        ("conv_bias", (4, NT)),
    ]


def unpack(vector):
    params_split = {}
    offset = 0
    for part_name, part_shape in layout():
        entries = math.prod(part_shape)
        params_split[part_name] = vector[offset : offset + entries].reshape(part_shape)
        offset = offset + entries
    return params_split


def matrix_shapes():
    return [(D, 3 * D), (D, D), (D, FF), (FF, D)]


def to_blocks(matrix):
    row_count, col_count = matrix.shape
    tiled = matrix.reshape(row_count // BLOCK_SIDE, BLOCK_SIDE, col_count // BLOCK_SIDE, BLOCK_SIDE)
    return tiled.transpose(0, 2, 1, 3).reshape(-1, BLOCK_SIDE, BLOCK_SIDE)


def from_blocks(blocks):
    matrices = []
    offset = 0
    for row_count, col_count in matrix_shapes():
        tiles = row_count // BLOCK_SIDE * (col_count // BLOCK_SIDE)
        piece_tiles = blocks[offset : offset + tiles].reshape(
            row_count // BLOCK_SIDE, col_count // BLOCK_SIDE, BLOCK_SIDE, BLOCK_SIDE
        )
        matrices.append(piece_tiles.transpose(0, 2, 1, 3).reshape(row_count, col_count))
        offset = offset + tiles
    return matrices


def layer_norm(values, gain_vec, shift_vec):
    centre = jnp.mean(values, -1, keepdims=True)
    centered = values - centre
    spread = jnp.mean(centered * centered, -1, keepdims=True)
    return centered * lax.rsqrt(spread + NORM_EPSILON) * gain_vec + shift_vec


def gelu_exact(values):
    return jax.nn.gelu(values, approximate=False)


def taps_sum(taps):
    padded = jnp.pad(taps, ((0, 0), (1, 1), (1, 1), (0, 0), (0, 0)))
    summed = jnp.zeros(taps.shape[:3] + taps.shape[4:], taps.dtype)
    for tap_index in range(9):
        row_off = tap_index // 3 - 1
        col_off = tap_index % 3 - 1
        summed = (
            summed
            + padded[
                :, 1 + row_off : 1 + row_off + GRID, 1 + col_off : 1 + col_off + GRID, tap_index
            ]
        )
    return summed


def taps_back(grads):
    padded = jnp.pad(grads, ((0, 0), (1, 1), (1, 1), (0, 0)))
    shifted = []
    for tap_index in range(9):
        row_off = tap_index // 3 - 1
        col_off = tap_index % 3 - 1
        shifted.append(
            padded[:, 1 - row_off : 1 - row_off + GRID, 1 - col_off : 1 - col_off + GRID]
        )
    return jnp.stack(shifted, axis=3)


def conv_small(values, weight):
    taps = jnp.einsum("fyxc,tco->fyxto", values, weight, precision=FULL_PRECISION)
    return taps_sum(taps)


def learner_tail(first_pre, values, second_w, third_w, fourth_w, tail_bias):
    frames = first_pre.shape[0]
    act_one = gelu_exact(first_pre)
    act_two = gelu_exact(conv_small(act_one, second_w) + tail_bias[0])
    act_three = gelu_exact(conv_small(act_two, third_w) + tail_bias[1])
    maps = jax.nn.sigmoid(conv_small(act_three, fourth_w) + tail_bias[2])
    grid_values = values.reshape(frames, GRID, GRID, values.shape[-1])
    pooled = jnp.einsum("fyxk,fyxd->fkd", maps, grid_values, precision=FULL_PRECISION)
    return pooled.reshape(frames * NT, values.shape[-1])


def clip_segments(lengths, order_row, group_frames, frames_dev, frame_count):
    clip_ids = jnp.arange(lengths.shape[0], dtype=jnp.int32)
    ordered_len = jnp.sum(
        jnp.where(order_row[:, None] == clip_ids[None, :], lengths[None, :], 0), 1
    )
    ends = jnp.cumsum(ordered_len)
    slots = jnp.arange(group_frames, dtype=jnp.int32)
    places = slots % frames_dev * frame_count + slots // frames_dev
    return jnp.sum((ends[None, :] <= places[:, None]).astype(jnp.int32), 1)


F32=jnp.float32; BF=jnp.bfloat16
NN=(((1,),(0,)),((),()))
NT_=(((1,),(1,)),((),()))
TN=(((0,),(0,)),((),()))

def halves(a):
    high = a.astype(BF)
    return high, (a - high.astype(F32)).astype(BF)

def dot_low(a, b, dims):
    return lax.dot_general(a, b, dims, preferred_element_type=F32)

def dot_parts(a, b, dims):
    ah, al = a
    bh, bl = b
    return dot_low(ah, bh, dims) + (dot_low(ah, bl, dims) + dot_low(al, bh, dims))

def dot_wide(a, b, dims):
    return dot_parts(halves(a), halves(b), dims)

def slots_step(n):
    return 7 if n % 7 == 0 else 2 if n % 2 == 0 else 1


def stat_products(sl, sr, bl, br):
    n = sl.shape[0]
    many = slots_step(n)
    spec = pl.BlockSpec((many, BLOCK_SIDE, BLOCK_SIDE), lambda i: (i, 0, 0))

    def kernel(sl, sr, bl, br, out_left, out_right):
        for s in range(many):
            out_left[s] = STAT_DECAY * dot_wide(bl[s], sl[s], TN)
            out_right[s] = STAT_DECAY * dot_wide(br[s], sr[s], TN)

    return pl.pallas_call(
        kernel,
        grid=(n // many,),
        in_specs=[spec] * 4,
        out_specs=[spec] * 2,
        out_shape=[jax.ShapeDtypeStruct(sl.shape, F32)] * 2,
        cost_estimate=about(7),
    )(sl, sr, bl, br)


def raw_products(ranks, g, bl, br):
    n = g.shape[0]
    many = slots_step(n)
    here = pl.BlockSpec((many, BLOCK_SIDE, BLOCK_SIDE), lambda i, ranks: (i, 0, 0))

    def ranked(s):
        return pl.BlockSpec((1, BLOCK_SIDE, BLOCK_SIDE), lambda i, ranks: (ranks[i * many + s], 0, 0))

    def kernel(ranks, *refs):
        grads, (bl, br, rot, gl, gr, ql, qr) = refs[:many], refs[many:]
        each = range(many)
        gp = [halves(grads[s][0]) for s in each]
        blp, brp = [halves(bl[s]) for s in each], [halves(br[s]) for s in each]
        u = [halves(dot_parts(blp[s], gp[s], TN)) for s in each]
        v = [halves(dot_parts(gp[s], brp[s], NN)) for s in each]
        for s in each:
            gl[s] = dot_parts(gp[s], gp[s], NT_)
        for s in each:
            gr[s] = dot_parts(gp[s], gp[s], TN)
        for s in each:
            rot[s] = dot_parts(u[s], brp[s], NN)
        for s in each:
            ql[s] = dot_parts(u[s], gp[s], NT_)
        for s in each:
            qr[s] = dot_parts(v[s], gp[s], TN)

    return pl.pallas_call(
        kernel,
        grid_spec=pltpu.PrefetchScalarGridSpec(
            num_scalar_prefetch=1,
            grid=(n // many,),
            in_specs=[ranked(s) for s in range(many)] + [here, here],
            out_specs=[here] * 5,
        ),
        out_shape=[jax.ShapeDtypeStruct(g.shape, F32)] * 5,
        cost_estimate=about(8),
    )(ranks, *([g] * many), bl, br)


NB=32
def tall(parts, order):
    return jnp.concatenate([parts[which] for which in order], axis=0)


def wide(parts, order):
    return jnp.concatenate([parts[which] for which in order], axis=1)


def finish_kernel(factor, *refs):
    inputs, refs = refs[:14], refs[14:]
    results, refs = refs[:7], refs[7:]
    held, made = refs[:14], refs[14:21]
    work, elim, load_sems, store_sems = refs[21:]
    p_l, p_r, ql, qr, rot, gl, gr, sl, sr, bl, br, master, m1, m2 = held
    o_master, o_m1, o_m2, o_left, o_right, o_bl, o_br = made
    for index in range(14):
        pltpu.make_async_copy(inputs[index], held[index], load_sems.at[index]).start()

    def ready(*indices):
        for index in indices:
            pltpu.make_async_copy(inputs[index], held[index], load_sems.at[index]).wait()

    def store(*indices):
        for index in indices:
            pltpu.make_async_copy(made[index], results[index], store_sems.at[index]).start()

    n = rot.shape[0]
    count = 2 * n
    f = factor[0]
    f2 = (1.0 - STAT_DECAY) * f * f
    ready(0, 1, 2, 3)
    group = 7 if n % 7 == 0 else n
    for start in range(0, n, group):
        members = range(start, start + group)
        sums = [p_[s] + f2 * q_[s] for s in members for p_, q_ in ((p_l, ql), (p_r, qr))]
        parts = [halves(at) for at in sums]
        grams = [dot_parts(atp, atp, NT_) for atp in parts]
        for i in range(2 * group):
            work[2 * start + i, :, BLOCK_SIDE:] = sums[i]
            work[2 * start + i, :, :BLOCK_SIDE] = grams[i]

    rows = lax.broadcasted_iota(jnp.int32, (1, 8, 2 * NB), 1)
    lanes = lax.broadcasted_iota(jnp.int32, (1, 8, 2 * NB), 2)
    panels = BLOCK_SIDE // NB
    tile_count = NB // 8

    def panel(p, carry):
        for q in range(panels):
            @pl.when(p == q)
            def _(q=q):
                for t in range(tile_count):
                    block = work[:, NB * q + 8 * t : NB * q + 8 * t + 8, NB * q : NB * q + NB]
                    eye = jnp.where(lanes - NB == rows + 8 * t, 1.0, 0.0).astype(F32)
                    eye = jnp.broadcast_to(eye, (count, 8, 2 * NB))
                    elim[:, 8 * t : 8 * t + 8, :] = jnp.concatenate([block, eye[:, :, NB:]], axis=2)
        tiles = [elim[:, 8 * t : 8 * t + 8, :] for t in range(tile_count)]
        for k in range(NB):
            t0, j = divmod(k, 8)
            columns = [jnp.broadcast_to(tiles[t][:, :, k : k + 1], tiles[t].shape) for t in range(t0, tile_count)]
            row = tiles[t0][:, j : j + 1, :] * (1.0 / columns[0][:, j : j + 1, :])
            for t in range(t0, tile_count):
                new = tiles[t] - columns[t - t0] * row
                if t == t0:
                    new = jnp.where(rows > j, new, tiles[t])
                tiles[t] = new
        for t in range(tile_count):
            pivots = jnp.sum(jnp.where(lanes == rows + 8 * t, tiles[t], 0.0), axis=2, keepdims=True)
            elim[:, 8 * t : 8 * t + 8, :] = tiles[t] * lax.rsqrt(pivots)
        for q in range(panels):
            @pl.when(p == q)
            def _(q=q):
                lo, hi = NB * q, NB * q + NB
                for start in range(0, count, group):
                    members = range(start, start + group)
                    inverses = [wide(halves(elim[m, :, NB:]), (0, 0, 1)) for m in members]
                    sources = [tall(halves(work[m, lo:hi, :]), (0, 1, 0)) for m in members]
                    solved = [dot_low(inverses[i], sources[i], NN) for i in range(group)]
                    for i, m in enumerate(members):
                        (o_bl if m % 2 == 0 else o_br)[m // 2, lo:hi, :] = solved[i][:, BLOCK_SIDE:]
                    if hi < BLOCK_SIDE:
                        parts = [halves(y) for y in solved]
                        updates = [
                            dot_low(tall(yp, (0, 0, 1))[:, :BLOCK_SIDE], tall(yp, (0, 1, 0)), TN) for yp in parts
                        ]
                        for i, m in enumerate(members):
                            work[m, hi:, :] = work[m, hi:, :] - updates[i][hi:]
        return carry

    lax.fori_loop(0, panels, panel, 0)

    ready(4, 5, 6, 7, 8, 9, 10, 11, 12, 13)
    for start in range(0, n, group):
        members = range(start, start + group)
        firsts, directions = [], []
        for s in members:
            r = f * rot[s]
            m = BETA_ONE * m1[s] + (1.0 - BETA_ONE) * r
            v = BETA_TWO * m2[s] + (1.0 - BETA_TWO) * r * r
            o_m2[s] = v
            o_left[s] = STAT_DECAY * sl[s] + f2 * gl[s]
            o_right[s] = STAT_DECAY * sr[s] + f2 * gr[s]
            firsts.append(halves(m))
            directions.append(
                halves(m / (1.0 - BETA_ONE**STEP) / (jnp.sqrt(v / (1.0 - BETA_TWO**STEP)) + ADAM_EPSILON))
            )
        old_left = [halves(bl[s]) for s in members]
        old_right = [halves(br[s]) for s in members]
        new_left = [o_bl[s] for s in members]
        new_right = [o_br[s] for s in members]
        each = range(group)
        backs = [halves(dot_parts(old_left[i], directions[i], NN)) for i in each]
        turns_left = [halves(dot_parts(halves(new_left[i]), old_left[i], NN)) for i in each]
        turns_right = [halves(dot_parts(halves(new_right[i]), old_right[i], NN)) for i in each]
        returned = [dot_parts(backs[i], old_right[i], NT_) for i in each]
        parts = [halves(dot_parts(turns_left[i], firsts[i], NN)) for i in each]
        moved_firsts = [dot_parts(parts[i], turns_right[i], NT_) for i in each]
        for i, s in enumerate(members):
            o_master[s] = master[s] - LEARN_RATE * (returned[i] + WEIGHT_DECAY * master[s])
            o_m1[s] = moved_firsts[i]
            o_bl[s] = new_left[i].T
            o_br[s] = new_right[i].T
    store(0, 1, 2, 3, 4, 5, 6)
    for index in range(7):
        pltpu.make_async_copy(made[index], results[index], store_sems.at[index]).wait()


def finish(factor, rot, gl, gr, ql, qr, p_l, p_r, sl, sr, bl, br, master, m1, m2):
    n = rot.shape[0]
    shape = jax.ShapeDtypeStruct(rot.shape, F32)
    hbm = pl.BlockSpec(memory_space=pl.ANY)
    block = pltpu.VMEM((n, BLOCK_SIDE, BLOCK_SIDE), F32)
    return pl.pallas_call(
        finish_kernel,
        in_specs=[pl.BlockSpec(memory_space=pltpu.SMEM)] + [hbm] * 14,
        out_specs=[hbm] * 7,
        out_shape=[shape] * 7,
        scratch_shapes=[block] * 21
        + [
            pltpu.VMEM((2 * n, BLOCK_SIDE, 2 * BLOCK_SIDE), F32),
            pltpu.VMEM((2 * n, NB, 2 * NB), F32),
            pltpu.SemaphoreType.DMA((14,)),
            pltpu.SemaphoreType.DMA((7,)),
        ],
        compiler_params=pltpu.CompilerParams(vmem_limit_bytes=56 * 1024 * 1024),
        cost_estimate=about(30),
    )(factor, p_l, p_r, ql, qr, rot, gl, gr, sl, sr, bl, br, master, m1, m2)


def adam_update(clipped, params_old, first_old, second_old):
    first_new = BETA_ONE * first_old + (1.0 - BETA_ONE) * clipped
    second_new = BETA_TWO * second_old + (1.0 - BETA_TWO) * clipped * clipped
    stepped = (
        first_new
        / (1.0 - BETA_ONE**STEP)
        / (jnp.sqrt(second_new / (1.0 - BETA_TWO**STEP)) + ADAM_EPSILON)
    )
    return (first_new, second_new, params_old - LEARN_RATE * stepped)


FRAME_ROWS = GRID * GRID
PAD_ROWS = 208
OWN_ROWS = 2 * PAD_ROWS
LANES = 512
PAIRS = HEADS // 2
PAIR = 2 * HD
QKV_BLOCKS = 108
CODE_BASE = 1 << 16
UP_ROWS = (D + FF) // BLOCK_SIDE
BLANK_ROW = (D + 2 * FF) // BLOCK_SIDE
ALL_ROWS = BLANK_ROW * BLOCK_SIDE
VMEM_MOST = 58 * 1024 * 1024
ALL_AXES = ("fz", "fx", "by", "core")
FRAME_AXES = ("fz", "fx")
TAP_OFFSETS = [(tap // 3 - 1) * GRID + tap % 3 - 1 for tap in range(9)]


def about(microseconds):
    return pl.CostEstimate(flops=0, bytes_accessed=int(microseconds * 3e6), transcendentals=0)


def in_vmem():
    return pl.BlockSpec(memory_space=pltpu.VMEM)


def anywhere():
    return pl.BlockSpec(memory_space=pl.ANY)


def matrix_places():
    places = []
    first = 0
    for row_count, col_count in matrix_shapes():
        cols = col_count // BLOCK_SIDE
        count = row_count // BLOCK_SIDE * cols
        places.append((first, count, cols))
        first = first + count
    return places


def tile_at(ref, row, col):
    row = pl.multiple_of(row * BLOCK_SIDE, BLOCK_SIDE)
    col = pl.multiple_of(col * BLOCK_SIDE, BLOCK_SIDE)
    return ref.at[pl.ds(row, BLOCK_SIDE), pl.ds(col, BLOCK_SIDE)]


def tile_of(matrix, code):
    return tile_at(matrix, lax.bitwise_and(lax.shift_right_logical(code, 5), 63), lax.bitwise_and(code, 31))


def load_blocks(tiles, buffers, matrix, sems, matrices, base=0, count=None):
    for buffer in buffers:
        def one_load(place, carry, buffer=buffer, base=base):
            code = tiles[base + place]
            which = lax.shift_right_logical(code, 11)

            @pl.when(which < matrices)
            def _():
                pltpu.make_async_copy(buffer.at[place], tile_of(matrix, code), sems.at[which]).start()

            return carry

        if count is None:
            lax.fori_loop(0, buffer.shape[0], one_load, 0, unroll=4)
        else:
            lax.fori_loop(0, count, one_load, 0)
        base = base + buffer.shape[0]


def wait_whole(ref, sem):
    pltpu.make_async_copy(ref, ref, sem).wait()


def send_tile(code, buffers, tile, sem, first=0):
    for index, buffer in enumerate(buffers):
        @pl.when(lax.div(code, CODE_BASE) == first + index)
        def _():
            pltpu.make_async_copy(tile, buffer.at[lax.rem(code, CODE_BASE)], sem).start()


def normalized(values):
    centered = values - jnp.mean(values, -1, keepdims=True)
    spread = lax.rsqrt(jnp.mean(centered * centered, -1, keepdims=True) + NORM_EPSILON)
    return centered * spread, spread


def norm_back(grad, hat, spread, gain):
    scaled = grad * gain
    return spread * (
        scaled
        - jnp.mean(scaled, -1, keepdims=True)
        - hat * jnp.mean(scaled * hat, -1, keepdims=True)
    )


def project(tiles, early, buffers, early_buffers, seen, rows14):
    rows = seen.shape[0]
    steps = rows // OWN_ROWS
    count = len(buffers)

    def kernel(tiles, early, *refs):
        sources = refs[:count]
        seen, rows14, q, kv, low, own_low, w_qkv, sems = refs[count:]
        step = pl.program_id(0)

        @pl.when(step == 0)
        def _():
            base = 0
            if early_buffers:
                load_blocks(tiles, sources[:1], w_qkv, sems, 1, 0, early[0])
                base = sources[0].shape[0]
            load_blocks(tiles, sources[early_buffers:], w_qkv, sems, 1, base)

        hat, _ = normalized(seen[...].astype(F32))
        normed = (hat * rows14[0:1] + rows14[1:2]).astype(BF)
        low[...] = normed

        @pl.when(step == 0)
        def _():
            wait_whole(w_qkv, sems.at[0])

        kv[:, :D] = dot_low(normed, w_qkv[:, D : 2 * D], NN).astype(BF)
        kv[:, D:] = (dot_low(normed, w_qkv[:, 2 * D :], NN) + rows14[7:8]).astype(BF)

        def own(place):
            part = normed[:PAD_ROWS]
            query = (dot_low(part, w_qkv[:, :D], NN) + rows14[6:7]).astype(BF)
            q[place : place + PAD_ROWS] = query * jnp.asarray(1.0 / math.sqrt(HD), BF)
            own_low[place : place + PAD_ROWS] = part

        @pl.when(step == 0)
        def _():
            own(0)

        @pl.when(step == steps - 1)
        def _():
            own(PAD_ROWS)

    def whole(shape):
        return pl.BlockSpec(shape, lambda i, tiles, early: (0, 0))

    def moving(width):
        return pl.BlockSpec((OWN_ROWS, width), lambda i, tiles, early: (i, 0))

    return pl.pallas_call(
        kernel,
        grid_spec=pltpu.PrefetchScalarGridSpec(
            num_scalar_prefetch=2,
            grid=(steps,),
            in_specs=[anywhere()] * count + [moving(D), whole((14, D))],
            out_specs=[whole((OWN_ROWS, D)), moving(2 * D), moving(D), whole((OWN_ROWS, D)), whole((D, 3 * D))],
            scratch_shapes=[pltpu.SemaphoreType.DMA((1,))],
        ),
        out_shape=[
            jax.ShapeDtypeStruct((OWN_ROWS, D), BF),
            jax.ShapeDtypeStruct((rows, 2 * D), BF),
            jax.ShapeDtypeStruct((rows, D), BF),
            jax.ShapeDtypeStruct((OWN_ROWS, D), BF),
            jax.ShapeDtypeStruct((D, 3 * D), BF),
        ],
        compiler_params=pltpu.CompilerParams(vmem_limit_bytes=VMEM_MOST),
        cost_estimate=about(15),
    )(tiles, early, *buffers, seen, rows14)


ROW_STEP = 16


def stacked(values):
    first = lax.broadcasted_iota(jnp.int32, (1, PAIR), 1) < HD
    nothing = jnp.zeros_like(values)
    return jnp.concatenate([jnp.where(first, values, nothing), jnp.where(first, nothing, values)], axis=0)


def unstacked(values):
    first = lax.broadcasted_iota(jnp.int32, (1, PAIR), 1) < HD
    return jnp.where(first, values[:PAD_ROWS], values[PAD_ROWS:])


def attend_kernel(long_rows, q, k, v, bias, out, logs, scores, soft):
    total = k.shape[0]
    for frame, (lo, hi) in enumerate(((0, long_rows), (long_rows, total))):
        rows = slice(frame * PAD_ROWS, (frame + 1) * PAD_ROWS)
        width = hi - lo
        scores[:, :width] = dot_low(stacked(q[rows, :]), k[lo:hi, :], NT_)
        norms, peaks = [], []
        for row in range(0, OWN_ROWS, ROW_STEP):
            block = scores[row : row + ROW_STEP, :width] + bias[:, lo:hi]
            peak = jnp.max(block, axis=1, keepdims=True)
            weights = jnp.exp(block - peak)
            norms.append(jnp.sum(weights, axis=1, keepdims=True))
            peaks.append(peak)
            soft[row : row + ROW_STEP, :width] = weights.astype(BF)
        norm = jnp.concatenate(norms, axis=0)
        out[rows, :] = unstacked(dot_low(soft[:, :width], v[lo:hi, :], NN) / norm).astype(BF)
        logs[rows, :] = unstacked(jnp.broadcast_to(jnp.concatenate(peaks, axis=0) + jnp.log(norm), (OWN_ROWS, PAIR)))


def attend_back_kernel(long_rows, q, k, v, bias, out, logs, grad, dq, dk, dv, scores, soft_grads, soft, changes):
    total = k.shape[0]
    for frame, (lo, hi) in enumerate(((0, long_rows), (long_rows, total))):
        rows = slice(frame * PAD_ROWS, (frame + 1) * PAD_ROWS)
        width = hi - lo
        query, arriving = stacked(q[rows, :]), stacked(grad[rows, :])
        products = stacked(grad[rows, :].astype(F32) * out[rows, :].astype(F32))
        delta = jnp.sum(products, axis=1, keepdims=True)
        log = jnp.concatenate([logs[rows, 0:1], logs[rows, HD : HD + 1]], axis=0)
        scores[:, :width] = dot_low(query, k[lo:hi, :], NT_)
        soft_grads[:, :width] = dot_low(arriving, v[lo:hi, :], NT_)
        for row in range(0, OWN_ROWS, ROW_STEP):
            here = slice(row, row + ROW_STEP)
            weights = jnp.exp(scores[here, :width] + bias[:, lo:hi] - log[here])
            soft[here, :width] = weights.astype(BF)
            changes[here, :width] = (weights * (soft_grads[here, :width] - delta[here])).astype(BF)
        part = unstacked(dot_low(changes[:, :width], k[lo:hi, :], NN))
        dq[rows, :] = (part * (1.0 / math.sqrt(HD))).astype(BF)
        dk[lo:hi, :] = dot_low(query, changes[:, :width], TN).T.astype(BF)
        dv[lo:hi, :] = dot_low(arriving, soft[:, :width], TN).T.astype(BF)


def pair_spec(rows, offset=0):
    return pl.BlockSpec((rows, PAIR), lambda i: (0, i + offset))


def attend(q, kv, bias):
    keys_total = kv.shape[0]
    long_rows = keys_total - OWN_ROWS

    def kernel(*refs):
        attend_kernel(long_rows, *refs)

    return pl.pallas_call(
        kernel,
        grid=(PAIRS,),
        in_specs=[
            pair_spec(OWN_ROWS),
            pair_spec(keys_total),
            pair_spec(keys_total, PAIRS),
            pl.BlockSpec((1, keys_total), lambda i: (0, 0)),
        ],
        out_specs=[pair_spec(OWN_ROWS)] * 2,
        out_shape=[jax.ShapeDtypeStruct((OWN_ROWS, D), BF), jax.ShapeDtypeStruct((OWN_ROWS, D), F32)],
        scratch_shapes=[pltpu.VMEM((OWN_ROWS, long_rows), F32), pltpu.VMEM((OWN_ROWS, long_rows), BF)],
        compiler_params=pltpu.CompilerParams(vmem_limit_bytes=VMEM_MOST),
        cost_estimate=about(12),
    )(q, kv, kv, bias.reshape(1, -1))


def attend_back(pairs, before, q, kv, bias, out, logs, grad):
    keys_total = kv.shape[0]
    long_rows = keys_total - OWN_ROWS
    start, count = pairs

    def kernel(*refs):
        attend_back_kernel(long_rows, *refs[:7], *refs[7 + len(before) :])

    def spec(rows, offset=0):
        return pair_spec(rows, offset + start)

    return pl.pallas_call(
        kernel,
        grid=(count,),
        in_specs=[
            spec(OWN_ROWS),
            spec(keys_total),
            spec(keys_total, PAIRS),
            pl.BlockSpec((1, keys_total), lambda i: (0, 0)),
            spec(OWN_ROWS),
            spec(OWN_ROWS),
            spec(OWN_ROWS),
        ]
        + [anywhere()] * len(before),
        out_specs=[spec(OWN_ROWS), spec(keys_total), spec(keys_total)],
        out_shape=[
            jax.ShapeDtypeStruct((OWN_ROWS, D), BF),
            jax.ShapeDtypeStruct((keys_total, D), BF),
            jax.ShapeDtypeStruct((keys_total, D), BF),
        ],
        scratch_shapes=[pltpu.VMEM((OWN_ROWS, long_rows), F32)] * 2 + [pltpu.VMEM((OWN_ROWS, long_rows), BF)] * 2,
        input_output_aliases={7 + i: i for i in range(len(before))},
        compiler_params=pltpu.CompilerParams(vmem_limit_bytes=VMEM_MOST),
        cost_estimate=about(4 * count),
    )(q, kv, kv, bias.reshape(1, -1), out, logs, grad, *before)


def lane_masks():
    lane = np.arange(LANES)
    inner = lane % PAD_ROWS
    token = (lane < OWN_ROWS) & (inner < FRAME_ROWS)
    row, col = inner // GRID, inner % GRID
    masks = []
    for tap in range(9):
        far_row, far_col = row + tap // 3 - 1, col + tap % 3 - 1
        masks.append(token & (far_row >= 0) & (far_row < GRID) & (far_col >= 0) & (far_col < GRID))
    masks.append(token & (lane < PAD_ROWS))
    masks.append(token & (lane >= PAD_ROWS))
    masks = masks + [np.zeros(LANES, bool)] * (16 - len(masks))
    return np.stack(masks).astype(np.float32)


def ahead(values, offset):
    return values if offset == 0 else pltpu.roll(values, (-offset) % LANES, axis=1)


def cumulative(values):
    return 0.5 + 0.5 * lax.erf(values * math.sqrt(0.5))


def gelu_slope(values, portion):
    return portion + values * jnp.exp(-0.5 * values * values) * (1.0 / math.sqrt(2.0 * math.pi))


def column_sum(values):
    return jnp.sum(values, axis=0, keepdims=True)


def widened(values):
    return jnp.concatenate([values, jnp.zeros((values.shape[0], LANES - OWN_ROWS), values.dtype)], axis=1)


def wait_tiles(matrix, count, sem):
    side = D // BLOCK_SIDE
    rest = count
    while rest >= side:
        rows = min(rest // side, BLANK_ROW)
        wait_whole(matrix.at[: rows * BLOCK_SIDE], sem)
        rest = rest - rows * side
    for _ in range(rest):
        wait_whole(tile_at(matrix, 0, 0), sem)


def middle_kernel(weight_count, first_buffer, held_tiles, sent_tiles, targets, *refs):
    sources = refs[:weight_count]
    (
        att, own, cot, rows14, conv_t, taps_forward, taps_backward, tail_bias, masks,
        learned, grad_mixed, grad_att, vectors, grad_up_bias, grad_conv, grad_tail, grad_tail_bias,
    ) = refs[weight_count : weight_count + 17]
    buffers = refs[weight_count + 17 : -10]
    (
        w_all, d_all, activated, slopes, normed, hat_two, mixed, gathered_sum, load_sems, send_sems,
    ) = refs[-10:]
    chunks = FF // D
    side = D // BLOCK_SIDE
    w_out = w_all.at[:D]
    w_up = [w_all.at[(1 + chunk) * D : (2 + chunk) * D] for chunk in range(chunks)]
    w_down = [w_all.at[(1 + chunks + chunk) * D : (2 + chunks + chunk) * D] for chunk in range(chunks)]
    d_out = d_all.at[:D]
    d_up = [d_all.at[(1 + chunk) * D : (2 + chunk) * D] for chunk in range(chunks)]
    d_down = [d_all.at[(1 + chunks + chunk) * D : (2 + chunks + chunk) * D] for chunk in range(chunks)]

    load_blocks(held_tiles, sources, w_all, load_sems, 3)
    d_all[ALL_ROWS:, :BLOCK_SIDE] = jnp.zeros((BLOCK_SIDE, BLOCK_SIDE), BF)
    wait_whole(w_out, load_sems.at[0])
    start = own[...].astype(F32) + dot_low(att[...], w_out[...], NN) + rows14[8:9]
    mixed[...] = start
    hat, spread_two = normalized(start)
    hat_two[...] = hat
    normed[...] = (hat * rows14[2:3] + rows14[3:4]).astype(BF)
    gathered_sum[...] = start + rows14[13:14]
    wait_whole(w_all.at[D : D + FF], load_sems.at[1])
    wait_whole(w_all.at[D + FF : D + 2 * FF], load_sems.at[2])

    for chunk in range(chunks):
        hidden = dot_low(normed[...], w_up[chunk][...], NN) + rows14[9 + chunk : 10 + chunk]
        portion = cumulative(hidden)
        active = (hidden * portion).astype(BF)
        activated[chunk] = active
        slopes[chunk] = gelu_slope(hidden, portion)
        gathered_sum[...] += dot_low(active, w_down[chunk][...], NN)

    out_two = gathered_sum[...]
    hat, spread_three = normalized(out_two)
    low_three = (hat * rows14[4:5] + rows14[5:6]).astype(BF)

    taps = widened(dot_low(conv_t[...], low_three, NT_))
    first = tail_bias[:, 0:1]
    for tap in range(9):
        first = first + ahead(taps[NT * tap : NT * (tap + 1)], TAP_OFFSETS[tap]) * masks[tap : tap + 1]

    def around(values, sign):
        order = range(9) if sign > 0 else range(8, -1, -1)
        return jnp.concatenate(
            [
                ahead(values, sign * TAP_OFFSETS[tap]) * masks[seen : seen + 1]
                for tap, seen in zip(range(9), order)
            ],
            axis=0,
        )

    before, stacks, portions = [first], [], []
    for layer in range(3):
        portions.append(cumulative(before[-1]))
        stacks.append(around(before[-1] * portions[-1], 1))
        before.append(dot_wide(taps_forward[layer], stacks[-1], NN) + tail_bias[:, layer + 1 : layer + 2])
    maps = 1.0 / (1.0 + jnp.exp(-before[3]))
    both = jnp.concatenate([maps * masks[9:10], maps * masks[10:11]], axis=0)[:, :OWN_ROWS]
    both = halves(both)
    out_parts = halves(out_two)
    arriving = cot[...]
    learned[...] = dot_parts(both, out_parts, NN)
    seen_maps = widened(dot_low(arriving, out_parts[0], NT_) + dot_low(arriving, out_parts[1], NT_))
    grad = (seen_maps[:NT] * masks[9:10] + seen_maps[NT:] * masks[10:11]) * maps * (1.0 - maps)
    sums = [None] * 4
    for layer in (2, 1, 0):
        sums[layer + 1] = jnp.sum(grad, axis=1, keepdims=True)
        grad_tail[layer] = dot_wide(stacks[layer], grad, NT_)
        grad = dot_wide(taps_backward[layer], around(grad, -1), NN)
        grad = grad * gelu_slope(before[layer], portions[layer])
    grad = grad.astype(BF).astype(F32)
    sums[0] = jnp.sum(grad, axis=1, keepdims=True)
    grad_tail_bias[...] = jnp.concatenate(sums, axis=1)
    grad_taps = around(grad, -1)[:, :OWN_ROWS].astype(BF)
    grad_conv[...] = dot_low(grad_taps, low_three, NN)
    grad_norm_three = dot_low(grad_taps, conv_t[...], TN)
    vectors[2:3] = column_sum(grad_norm_three * hat)
    vectors[3:4] = column_sum(grad_norm_three)
    grad_out = (
        norm_back(grad_norm_three, hat, spread_three, rows14[4:5])
        + dot_low(both[0], arriving, TN)
        + dot_low(both[1], arriving, TN)
    )
    grad_down = grad_out.astype(BF)
    vectors[5:6] = column_sum(grad_down.astype(F32))

    for chunk in range(chunks):
        grad_active = dot_low(grad_down, w_down[chunk][...], NT_)
        grad_hidden = (grad_active * slopes[chunk]).astype(BF)
        grad_up_bias[chunk : chunk + 1] = column_sum(grad_hidden.astype(F32))
        part = dot_low(grad_hidden, w_up[chunk][...], NT_)
        if chunk == 0:
            gathered_sum[...] = part
        else:
            gathered_sum[...] += part
        d_down[chunk][...] = dot_low(activated[chunk], grad_down, TN).astype(BF)
        d_up[chunk][...] = dot_low(normed[...], grad_hidden, TN).astype(BF)

    base = 0
    for buffer in buffers:
        def one_tile(place, carry, buffer=buffer, base=base):
            code = sent_tiles[base + place]

            @pl.when(code >= 2048)
            def _():
                pltpu.make_async_copy(tile_of(d_all, code), buffer.at[place], send_sems.at[1]).start()

            return carry

        lax.fori_loop(0, buffer.shape[0], one_tile, 0, unroll=4)
        base = base + buffer.shape[0]

    grad_norm_two = gathered_sum[...]
    vectors[0:1] = column_sum(grad_norm_two * hat_two[...])
    vectors[1:2] = column_sum(grad_norm_two)
    total = grad_out + norm_back(grad_norm_two, hat_two[...], spread_two, rows14[2:3])
    grad_mixed[...] = total
    branch = total.astype(BF)
    vectors[4:5] = column_sum(branch.astype(F32))
    d_out[...] = dot_low(att[...], branch, TN).astype(BF)

    def one_out(tile, carry):
        code = targets[matrix_places()[1][0] + tile]
        send_tile(code, buffers, tile_at(d_out, lax.div(tile, side), lax.rem(tile, side)), send_sems.at[0], first_buffer)
        return carry

    lax.fori_loop(0, matrix_places()[1][1], one_out, 0)
    grad_att[...] = dot_low(branch, w_out[...], NT_).astype(BF)
    wait_tiles(d_all, matrix_places()[1][1], send_sems.at[0])
    wait_tiles(d_all, targets.shape[0] - matrix_places()[1][1], send_sems.at[1])


def middle(held_tiles, sent_tiles, targets, weights, first_buffer, buffer_shapes, att, own, cot, rows14, conv_t, taps_forward, taps_backward, tail_bias):
    count = len(weights)

    def kernel(*refs):
        middle_kernel(count, first_buffer, *refs)

    def f32(*shape):
        return jax.ShapeDtypeStruct(shape, F32)

    outs = [
        f32(2 * NT, D), f32(OWN_ROWS, D), jax.ShapeDtypeStruct((OWN_ROWS, D), BF), f32(8, D),
        f32(FF // D, D), f32(9 * NT, D), f32(3, 9 * NT, NT), f32(NT, 4),
    ]
    results = pl.pallas_call(
        kernel,
        grid_spec=pltpu.PrefetchScalarGridSpec(
            num_scalar_prefetch=3,
            grid=(1,),
            in_specs=[anywhere()] * count + [in_vmem()] * 9,
            out_specs=[in_vmem()] * len(outs) + [anywhere()] * len(buffer_shapes),
            scratch_shapes=[
                pltpu.VMEM((ALL_ROWS + BLOCK_SIDE, D), BF),
                pltpu.VMEM((ALL_ROWS + BLOCK_SIDE, D), BF),
                pltpu.VMEM((FF // D, OWN_ROWS, D), BF),
                pltpu.VMEM((FF // D, OWN_ROWS, D), F32),
                pltpu.VMEM((OWN_ROWS, D), BF),
                pltpu.VMEM((OWN_ROWS, D), F32),
                pltpu.VMEM((OWN_ROWS, D), F32),
                pltpu.VMEM((OWN_ROWS, D), F32),
                pltpu.SemaphoreType.DMA((3,)),
                pltpu.SemaphoreType.DMA((2,)),
            ],
        ),
        out_shape=outs + buffer_shapes,
        compiler_params=pltpu.CompilerParams(vmem_limit_bytes=VMEM_MOST),
        cost_estimate=about(40),
    )(
        held_tiles, sent_tiles, targets, *weights, att, own, cot, rows14, conv_t, taps_forward, taps_backward, tail_bias,
        jnp.asarray(lane_masks()),
    )
    return results[: len(outs)], results[len(outs) :]


def qkv_grads(targets, low, own_low, dq, dk, dv, buffers, late):
    steps = low.shape[0] // OWN_ROWS
    count = len(buffers)

    def kernel(targets, low, own_low, dq, dk, dv, *refs):
        filled = refs[count : 2 * count]
        matrix = refs[2 * count]
        totals, sem = refs[2 * count + 1 :]
        step = pl.program_id(0)

        @pl.when(step == 0)
        def _():
            totals[...] = jnp.zeros_like(totals)
            matrix[:, :D] = dot_low(own_low[...], dq[...], TN).astype(BF)

        totals[:, :D] += dot_low(low[...], dk[...], TN)
        totals[:, D:] += dot_low(low[...], dv[...], TN)

        @pl.when(step == steps - 1)
        def _():
            matrix[:, D:] = totals[...].astype(BF)
            cols = 3 * D // BLOCK_SIDE

            def one_tile(tile, sent):
                code = targets[tile]
                send_tile(code, filled, tile_at(matrix, lax.div(tile, cols), lax.rem(tile, cols)), sem, late)
                return sent + (lax.div(code, CODE_BASE) >= late).astype(jnp.int32)

            sent = lax.fori_loop(0, QKV_BLOCKS, one_tile, jnp.int32(0))

            def one_wait(index, carry):
                wait_whole(tile_at(matrix, 0, 0), sem)
                return carry

            lax.fori_loop(0, sent, one_wait, 0)

    def whole(shape):
        return pl.BlockSpec(shape, lambda i, targets: (0, 0))

    def moving(width):
        return pl.BlockSpec((OWN_ROWS, width), lambda i, targets: (i, 0))

    results = pl.pallas_call(
        kernel,
        grid_spec=pltpu.PrefetchScalarGridSpec(
            num_scalar_prefetch=1,
            grid=(steps,),
            in_specs=[moving(D), whole((OWN_ROWS, D)), whole((OWN_ROWS, D)), moving(D), moving(D)]
            + [anywhere()] * count,
            out_specs=[anywhere()] * count + [whole((D, 3 * D))],
            scratch_shapes=[pltpu.VMEM((D, 2 * D), F32), pltpu.SemaphoreType.DMA],
        ),
        out_shape=[jax.ShapeDtypeStruct(b.shape, b.dtype) for b in buffers]
        + [jax.ShapeDtypeStruct((D, 3 * D), BF)],
        input_output_aliases={6 + i: i for i in range(count)},
        compiler_params=pltpu.CompilerParams(vmem_limit_bytes=VMEM_MOST),
        cost_estimate=about(14),
    )(targets, low, own_low, dq, dk, dv, *buffers)
    return results[:count], results[count]


def input_grads(seen, own, dq, dk, dv, w_qkv):
    rows = seen.shape[0]
    steps = rows // OWN_ROWS

    def kernel(seen, own, dq, dk, dv, w_qkv, grad_seen, grad_own, sums):
        step = pl.program_id(0)

        @pl.when(step == 0)
        def _():
            grad = dot_low(dq[...], w_qkv[:, :D], NT_)
            grad_own[...] = grad
            hat, _ = normalized(own[...].astype(F32))
            sums[...] = jnp.zeros_like(sums)
            sums[0:1] = column_sum(grad * hat)
            sums[1:2] = column_sum(grad)
            sums[2:3] = column_sum(dq[...].astype(F32))

        grad = dot_low(dk[...], w_qkv[:, D : 2 * D], NT_) + dot_low(dv[...], w_qkv[:, 2 * D :], NT_)
        grad_seen[...] = grad.astype(BF)
        hat, _ = normalized(seen[...].astype(F32))
        sums[0:1] += column_sum(grad * hat)
        sums[1:2] += column_sum(grad)
        sums[3:4] += column_sum(dv[...].astype(F32))

    def whole(shape):
        return pl.BlockSpec(shape, lambda i: (0, 0))

    moving = pl.BlockSpec((OWN_ROWS, D), lambda i: (i, 0))
    return pl.pallas_call(
        kernel,
        grid=(steps,),
        in_specs=[moving, whole((OWN_ROWS, D)), whole((OWN_ROWS, D)), moving, moving, whole((D, 3 * D))],
        out_specs=[moving, whole((OWN_ROWS, D)), whole((8, D))],
        out_shape=[
            jax.ShapeDtypeStruct((rows, D), BF),
            jax.ShapeDtypeStruct((OWN_ROWS, D), F32),
            jax.ShapeDtypeStruct((8, D), F32),
        ],
        compiler_params=pltpu.CompilerParams(vmem_limit_bytes=VMEM_MOST),
        cost_estimate=about(12),
    )(seen, own, dq, dk, dv, w_qkv)


def moved(value, axis, size, step):
    return lax.ppermute(value, axis, [(i, (i + step) % size) for i in range(size)])


def reduce_axis(terms, axis, size, dim=0):
    total = lax.index_in_dim(terms, 0, dim, keepdims=False).astype(F32)
    for step in range(1, size):
        term = lax.index_in_dim(terms, step, dim, keepdims=False)
        total = total + moved(term, axis, size, step).astype(F32)
    return total


def after(value, *others):
    return lax.optimization_barrier((value, others))[0]


def gather_axis(value, axis, size):
    return jnp.stack([value] + [moved(value, axis, size, -step) for step in range(1, size)])


def line_step(state, axis, size):
    onward, backward = state
    up = [(i, i + 1) for i in range(size - 1)]
    down = [(i + 1, i) for i in range(size - 1)]
    return lax.ppermute(onward, axis, down), lax.ppermute(backward, axis, up)


def line_pieces(value, steps, axis, size):
    coord = lax.axis_index(axis)
    pieces = [value]
    for step in range(1, size):
        pieces.append(jnp.where(coord + step < size, steps[step - 1][0], steps[size - step - 1][1]))
    return pieces


def rolled(value, axis, size, step):
    return lax.dynamic_slice_in_dim(jnp.concatenate([value, value], axis), step, size, axis)


def small_shares(vector, sizes, coords):
    device_count = math.prod(sizes)
    share = -(-vector.shape[0] // (device_count * 128)) * 128
    shares = jnp.pad(vector, (0, device_count * share - vector.shape[0])).reshape(sizes + (share,))
    for axis, size in enumerate(sizes):
        shares = rolled(shares, axis, size, coords[axis])
    return shares.transpose(3, 0, 1, 2, 4)


def small_step(shares, axis, sizes):
    return reduce_axis(shares, ALL_AXES[axis], sizes[axis])


def early_slots(slots_dev):
    return slots_dev * 6 // 14


def slot_chunks(slots_dev):
    early = early_slots(slots_dev)
    late = slots_dev - early
    chunks = []
    first = 0
    for index, count in enumerate((early - early // 2, early // 2, late - late // 2, late // 2)):
        chunks.append((first, count, ("fx", "by", "fz") if index % 2 == 0 else ("by", "fx", "fz")))
        first = first + count
    return chunks


def send_table(block_owner, sizes, coords, slots_dev):
    nz, nx, ny, nc = sizes
    slots = jnp.arange(block_owner.shape[0], dtype=jnp.int32)
    device = slots // slots_dev
    place = {}
    for axis in range(3, -1, -1):
        place[ALL_AXES[axis]] = (device % sizes[axis] - coords[axis] + sizes[axis]) % sizes[axis]
        device = device // sizes[axis]
    is_late = (block_owner < QKV_BLOCKS).astype(jnp.int32).reshape(-1, slots_dev)
    late_before = jnp.cumsum(is_late, 1) - is_late
    early_before = jnp.arange(slots_dev, dtype=jnp.int32)[None] - late_before
    late_count = jnp.sum(is_late, 1, keepdims=True)
    ranks = jnp.where(is_late == 1, slots_dev - late_count + late_before, early_before)
    rank = ranks.reshape(-1)
    size_of = dict(zip(ALL_AXES, sizes))
    code = jnp.zeros_like(slots)
    chunks = slot_chunks(slots_dev)
    device_count = nz * nx * ny * nc
    for index, (first, count, axes) in enumerate(chunks):
        at = jnp.zeros_like(slots)
        for name in axes:
            at = at * size_of[name] + place[name]
        at = at * count + rank - first
        if index % 2:
            at = at + device_count // nc * chunks[index - 1][1]
        inside = (rank >= first) & (rank < first + count)
        code = jnp.where(inside, (index // 2 * 2 + place["core"]) * CODE_BASE + at, code)
    owned = block_owner[:, None] == slots[None, :]
    table = jnp.sum(jnp.where(owned, code[:, None], 0), 0)
    early = early_slots(slots_dev)
    late_size = device_count // nc * (slots_dev - early)
    early_size = device_count // nc * early
    buffer, at = code // CODE_BASE, code % CODE_BASE
    sent_at = jnp.where(buffer < 2, buffer * early_size, 2 * early_size + (buffer - 2) * late_size) + at
    held_at = jnp.where(buffer < 2, slots // slots_dev * early + rank, 2 * early_size + (buffer - 2) * late_size + at)
    tile = tile_code(block_owner)
    held_tiles = jnp.sum(jnp.where(held_at[:, None] == slots[None, :], tile[:, None], 0), 0)
    sent_tiles = jnp.sum(jnp.where(sent_at[:, None] == slots[None, :], tile[:, None], 0), 0)
    qkv_cols = 3 * D // BLOCK_SIDE
    qkv_tile = jnp.where(block_owner < QKV_BLOCKS, block_owner // qkv_cols * 32 + block_owner % qkv_cols, 2048)
    qkv_tiles = jnp.sum(jnp.where(held_at[:, None] == slots[None, :], qkv_tile[:, None], 0), 0)
    return table, qkv_tiles, held_tiles, sent_tiles, ranks, jnp.max(late_count)


def tile_code(block):
    side = D // BLOCK_SIDE
    out_tile = block - matrix_places()[1][0]
    up_tile = block - matrix_places()[2][0]
    down_tile = block - matrix_places()[3][0]
    up_row, up_col = up_tile // (FF // BLOCK_SIDE), up_tile % (FF // BLOCK_SIDE)
    row = jnp.where(
        up_tile < 0,
        out_tile // side,
        jnp.where(down_tile < 0, side + up_col // side * side + up_row, UP_ROWS + down_tile // side),
    )
    col = jnp.where(up_tile < 0, out_tile % side, jnp.where(down_tile < 0, up_col % side, down_tile % side))
    matrix = jnp.where(up_tile < 0, 0, jnp.where(down_tile < 0, 1, 2))
    used = (out_tile >= 0) & (block < MATRIX_BLOCKS)
    return jnp.where(used, matrix * 2048 + row * 32 + col, 3 * 2048 + BLANK_ROW * 32)


def reduce_core(kept, sent, chunks, sizes):
    size_of = dict(zip(ALL_AXES, sizes))
    received = moved(sent, "core", 2, 1)
    parts = []
    start = 0
    for first, count, axes in chunks:
        shape = [size_of[name] for name in axes[1:]] + [count, BLOCK_SIDE, BLOCK_SIDE]
        length = math.prod(shape[:-2])
        terms = []
        for _ in range(size_of[axes[0]]):
            stop = start + length
            total = kept[start:stop].astype(F32) + received[start:stop].astype(F32)
            terms.append(total.astype(BF).reshape(shape))
            start = stop
        parts.append(terms)
    return parts


def reduce_stage(parts, chunks, stage, sizes):
    results = []
    for terms, (first, count, axes) in zip(parts, chunks):
        received = [moved(terms[step], axes[stage], len(terms), step) for step in range(1, len(terms))]
        following = []
        for index in range(terms[0].shape[0]):
            total = terms[0][index].astype(F32)
            for term in received:
                total = total + term[index].astype(F32)
            following.append(total.astype(BF))
        results.append(following)
    return results


def reduce_last(parts, sizes):
    terms = [jnp.concatenate(pieces) for pieces in zip(*parts)]
    total = terms[0].astype(F32)
    for step in range(1, len(terms)):
        total = total + moved(terms[step], "fz", sizes[0], step).astype(F32)
    return total


def gather_stage(shard, axes, stage, sizes):
    name = axes[len(axes) - 1 - stage]
    return gather_axis(shard, name, sizes[ALL_AXES.index(name)])


def gather_last(shards, orders, sizes):
    pieces = []
    for shard, axes in zip(shards, orders):
        size = sizes[ALL_AXES.index(axes[0])]
        pieces = pieces + [shard] + [moved(shard, axes[0], size, -step) for step in range(1, size)]
    return [piece.reshape(-1, BLOCK_SIDE, BLOCK_SIDE) for piece in pieces]


def sorted_shards(device_index, block_owner, master):
    slots_dev = master.shape[0]
    early = early_slots(slots_dev)
    chunks = [(0, early, ()), (early, slots_dev - early, ())]

    def kernel(where, owner, blocks, *outs):
        base = where[0] * slots_dev
        late_count = jnp.int32(0)
        for slot in range(slots_dev):
            late_count = late_count + (owner[base + slot] < QKV_BLOCKS).astype(jnp.int32)
        early_at, late_at = jnp.int32(0), slots_dev - late_count
        for slot in range(slots_dev):
            late = owner[base + slot] < QKV_BLOCKS
            rank = jnp.where(late, late_at, early_at)
            late_at = late_at + late.astype(jnp.int32)
            early_at = early_at + 1 - late.astype(jnp.int32)
            for index, (first, count, axes) in enumerate(chunks):
                if count == 0:
                    continue

                @pl.when((rank >= first) & (rank < first + count))
                def _(index=index, first=first):
                    outs[index][rank - first] = blocks[slot].astype(BF)

    return pl.pallas_call(
        kernel,
        grid_spec=pltpu.PrefetchScalarGridSpec(
            num_scalar_prefetch=2,
            grid=(1,),
            in_specs=[in_vmem()],
            out_specs=[in_vmem()] * len(chunks),
        ),
        out_shape=[
            jax.ShapeDtypeStruct((max(count, 1), BLOCK_SIDE, BLOCK_SIDE), BF) for first, count, axes in chunks
        ],
        cost_estimate=about(3),
    )(device_index.reshape(1), block_owner, master)


def spread_early(targets, matrix, buffer_shapes):
    count = len(buffer_shapes)

    def kernel(targets, matrix, blank, *refs):
        buffers, sem = refs[:count], refs[count]

        def one_block(block, sent):
            code = targets[block]
            cols = 3 * D // BLOCK_SIDE
            early = lax.div(code, CODE_BASE) < 2

            @pl.when(early & (block < QKV_BLOCKS))
            def _():
                tile = tile_at(matrix, lax.div(block, cols), lax.rem(block, cols))
                send_tile(code, buffers, tile, sem)

            @pl.when(early & (block >= QKV_BLOCKS))
            def _():
                send_tile(code, buffers, blank, sem)

            return sent + early.astype(jnp.int32)

        sent = lax.fori_loop(0, targets.shape[0], one_block, jnp.int32(0))

        def one_wait(index, carry):
            wait_whole(blank, sem)
            return carry

        lax.fori_loop(0, sent, one_wait, 0)

    return pl.pallas_call(
        kernel,
        grid_spec=pltpu.PrefetchScalarGridSpec(
            num_scalar_prefetch=1,
            grid=(1,),
            in_specs=[in_vmem()] * 2,
            out_specs=[anywhere()] * count,
            scratch_shapes=[pltpu.SemaphoreType.DMA],
        ),
        out_shape=buffer_shapes,
        compiler_params=pltpu.CompilerParams(vmem_limit_bytes=VMEM_MOST),
    )(targets, matrix, jnp.zeros((BLOCK_SIDE, BLOCK_SIDE), BF))


def pad_frames(values):
    frames = values.reshape(2, FRAME_ROWS, values.shape[-1])
    return jnp.pad(frames, ((0, 0), (0, PAD_ROWS - FRAME_ROWS), (0, 0)))


def on_device(
    tokens,
    cotangent,
    clip_lengths,
    clip_order,
    block_owner,
    master,
    moment1,
    moment2,
    stat_left,
    stat_right,
    basis_left,
    basis_right,
    small_params,
    small_moment1,
    small_moment2,
):
    sizes = tuple(lax.axis_size(name) for name in ALL_AXES)
    coords = [lax.axis_index(name) for name in ALL_AXES]
    nz, nx, ny, nc = sizes
    device_count = nz * nx * ny * nc
    frame_count = nz * nx
    frame_index = coords[0] * nx + coords[1]
    slots_dev = master.shape[0]

    segment_slots = clip_segments(
        clip_lengths[0], clip_order[0], 2 * frame_count, 2, frame_count
    ).reshape(frame_count, 2)
    ordered_len = clip_lengths[0][clip_order[0]]
    longest = jnp.argmax(ordered_len).astype(jnp.int32)
    second_long = segment_slots[:, 1] == longest
    short_segment = jnp.where(second_long, segment_slots[:, 0], segment_slots[:, 1])
    swap = second_long[frame_index]
    padded_segment = jnp.pad(short_segment, (1, 1), constant_values=-1)
    near = lax.dynamic_slice_in_dim(padded_segment, frame_index, 3)
    with_previous = near[0] == near[1]
    with_next = near[2] == near[1]

    device_index = ((coords[0] * nx + coords[1]) * ny + coords[2]) * nc + coords[3]
    early = early_slots(slots_dev)
    chunks = slot_chunks(slots_dev)
    shards = sorted_shards(device_index, block_owner, master)
    orders = [axes for first, count, axes in chunks]
    late_shards = gather_axis(shards[1], "fz", nz)

    own_frames = pad_frames(tokens[0])
    own_frames = jnp.where(swap, own_frames[::-1], own_frames)
    long_frame, short_frame = own_frames[0], own_frames[1]
    frame_perm = [(i, (i + 1) % frame_count) for i in range(frame_count)]
    back_perm = [(j, i) for i, j in frame_perm]
    frames_seen = frame_count + 2
    own = own_frames.reshape(OWN_ROWS, D)
    row_ids = jnp.arange(frames_seen * PAD_ROWS, dtype=jnp.int32)
    hidden_key = (row_ids % PAD_ROWS >= FRAME_ROWS) | (
        (row_ids >= (frames_seen - 1) * PAD_ROWS) & ~(with_previous | with_next)
    )
    key_bias = jnp.where(hidden_key, MASK_FLOOR, 0.0).astype(F32)

    targets, qkv_tiles, held_tiles, sent_tiles, ranks, late_most = send_table(block_owner, sizes, coords, slots_dev)
    own_ranks = lax.dynamic_index_in_dim(ranks, device_index, 0, keepdims=False)
    late_fits = late_most <= slots_dev - early

    split = unpack(small_params)
    rows14 = small_params[: 14 * D].reshape(14, D)
    conv_t = split["conv_first"].astype(BF).reshape(D, 9 * NT).T
    tail = jnp.stack([split["conv_second"], split["conv_third"], split["conv_fourth"]])
    taps_forward = tail.transpose(0, 3, 1, 2).reshape(3, NT, 9 * NT)
    taps_backward = tail.transpose(0, 2, 1, 3).reshape(3, NT, 9 * NT)
    tail_bias = split["conv_bias"].T
    arriving = cotangent[0].reshape(2, NT, D)
    arriving = jnp.where(swap, arriving[::-1], arriving).reshape(2 * NT, D)

    early_looked = jnp.where(late_fits, 0, device_count * early).astype(jnp.int32).reshape(1)
    stat_parts = stat_products(stat_left, stat_right, basis_left, basis_right)

    def gather_early(shard):
        return lax.all_gather(shard, ALL_AXES, axis=0, tiled=True)

    weights = [gather_early(shards[0])] if early else []
    long_pair = gather_axis(long_frame, "fx", nx)
    from_previous = lax.ppermute(short_frame, FRAME_AXES, frame_perm)
    from_next = lax.ppermute(short_frame, FRAME_AXES, back_perm)
    (
        long_pair, late_shards, from_previous, from_next, targets, qkv_tiles, held_tiles, sent_tiles, own_ranks, early_looked,
    ) = lax.optimization_barrier(
        (
            long_pair, late_shards, from_previous, from_next, targets, qkv_tiles, held_tiles, sent_tiles, own_ranks,
            early_looked,
        )
    )
    late_shards = [late_shards[:, : chunks[2][1]], late_shards[:, chunks[2][1] :]]
    late_shards = [gather_stage(part, orders[2 + i], 1, sizes) for i, part in enumerate(late_shards)]
    line = [line_step((long_pair, long_pair), "fz", nz)]
    partner = jnp.where(with_next, from_next, from_previous)
    (
        late_shards, line[0], partner, stat_parts, key_bias, rows14, conv_t, taps_forward, taps_backward, tail_bias, arriving,
    ) = lax.optimization_barrier(
        (
            late_shards, line[0], partner, stat_parts, key_bias, rows14, conv_t, taps_forward, taps_backward, tail_bias,
            arriving,
        )
    )
    late_pieces = gather_last(late_shards, orders[2:], sizes)
    line.append(line_step(line[-1], "fz", nz))


    weights = weights + late_pieces + [moved(piece, "core", nc, 1) for piece in late_pieces]
    for _ in range(nz - 3):
        line.append(line_step(line[-1], "fz", nz))
    long_frames = line_pieces(long_pair, line, "fz", nz)
    seen = jnp.concatenate(
        [frames.reshape(-1, D) for frames in long_frames] + [short_frame, partner]
    )
    query, key_value, low, own_low, w_qkv = project(
        qkv_tiles, early_looked, weights, 1 if early else 0, seen, rows14
    )
    attended, logs = attend(query, key_value, key_bias)
    buffer_shapes = []
    for slots in (early, slots_dev - early):
        if slots:
            shape = jax.ShapeDtypeStruct((device_count // nc * slots, BLOCK_SIDE, BLOCK_SIDE), BF)
            buffer_shapes = buffer_shapes + [shape, shape]
    (learned, grad_mixed, grad_att, vectors, grad_up_bias, grad_conv, grad_tail, grad_tail_bias), buffers = middle(
        held_tiles, sent_tiles, targets, weights, 0 if early else 2, buffer_shapes, attended, own, arriving, rows14, conv_t,
        taps_forward, taps_backward, tail_bias,
    )
    learned = learned.reshape(2, NT, D)
    learned = jnp.where(swap, learned[::-1], learned).reshape(2 * NT, D)

    halfway = reduce_core(*buffers[:2], chunks[:2], sizes) if early else []
    back = attend_back((0, PAIRS // 3), [], query, key_value, key_bias, attended, logs, grad_att)
    back, halfway = lax.optimization_barrier((back, halfway))
    halfway = reduce_stage(halfway, chunks, 0, sizes)
    grad_query, grad_key, grad_value = attend_back(
        (PAIRS // 3, PAIRS - PAIRS // 3), back, query, key_value, key_bias, attended, logs, grad_att
    )
    grad_query, halfway = lax.optimization_barrier((grad_query, halfway))
    halfway = reduce_stage(halfway, chunks, 1, sizes)
    late_buffers, grad_w_qkv = qkv_grads(
        targets, low, own_low, grad_query, grad_key, grad_value, list(buffers[-2:]), 2
    )
    grad_query, late_buffers, halfway = lax.optimization_barrier((grad_query, late_buffers, halfway))
    reduced = [reduce_last(halfway, sizes)] if early else []
    late_parts = reduce_core(*late_buffers, chunks[2:], sizes)
    grad_seen, grad_own, sums = input_grads(seen, own, grad_query, grad_key, grad_value, w_qkv)
    late_parts, reduced, grad_seen, sums = lax.optimization_barrier((late_parts, reduced, grad_seen, sums))

    late_parts = reduce_stage(late_parts, chunks[2:], 0, sizes)
    small_local = jnp.concatenate(
        [
            sums[:2].reshape(-1),
            vectors[:4].reshape(-1),
            sums[2:4].reshape(-1),
            vectors[4],
            grad_up_bias.reshape(-1),
            vectors[5],
            grad_conv.T.reshape(-1),
            grad_tail.reshape(-1),
            grad_tail_bias.T.reshape(-1),
        ]
    )
    small_total = small_local.shape[0]
    small = small_step(small_step(small_shares(small_local, sizes, coords), 3, sizes), 0, sizes)
    late_parts, small, grad_seen = lax.optimization_barrier((late_parts, small, grad_seen))
    seen_frames = grad_seen.reshape(frames_seen, PAD_ROWS, D)
    long_terms = seen_frames[:frame_count].reshape(nz, nx, PAD_ROWS, D)
    partner_term = seen_frames[frame_count + 1]
    nothing = jnp.zeros_like(partner_term)
    to_previous = jnp.where(with_previous, partner_term, nothing)
    to_next = jnp.where(with_next, partner_term, nothing)
    late_parts = reduce_stage(late_parts, chunks[2:], 1, sizes)
    small = small_step(small, 1, sizes)
    late_parts, small, long_terms, to_previous, to_next = lax.optimization_barrier(
        (late_parts, small, long_terms, to_previous, to_next)
    )
    late_total = reduce_last(late_parts, sizes)
    small = small_step(small, 2, sizes)
    long_terms = reduce_axis(long_terms, "fx", nx, 1).astype(BF)
    late_total, small, long_terms = lax.optimization_barrier((late_total, small, long_terms))
    if early:
        def whole_early(share):
            extra = reduce_core(*spread_early(targets, grad_w_qkv, buffer_shapes[:2]), chunks[:2], sizes)
            for stage in range(2):
                extra = reduce_stage(extra, chunks, stage, sizes)
            return share + reduce_last(extra, sizes)

        reduced = [lax.cond(late_fits, lambda share: share, whole_early, reduced[0])]
    owned_grads = jnp.concatenate(reduced + [late_total])

    squares = jnp.sum(owned_grads * owned_grads) + jnp.sum(small * small)
    carried = jnp.concatenate([small, jnp.full((128,), squares, F32)])
    carried = gather_axis(carried, "fz", nz)
    carried = gather_axis(carried, "fx", nx)
    raw = raw_products(own_ranks, owned_grads, basis_left, basis_right)
    carried = gather_axis(carried, "by", ny)
    carried, raw = lax.optimization_barrier((carried, raw))
    carried = gather_axis(carried, "core", nc)
    share = small.shape[0]
    grad_norm = jnp.sqrt(jnp.sum(carried[..., share]))
    factor = 1.0 / jnp.maximum(grad_norm, CLIP_NORM)
    long_terms, to_previous, to_next, factor = lax.optimization_barrier((long_terms, to_previous, to_next, factor))
    long_total = reduce_axis(long_terms, "fz", nz)
    from_next = lax.ppermute(to_previous, FRAME_AXES, back_perm)
    from_previous = lax.ppermute(to_next, FRAME_AXES, frame_perm)
    carried = carried[..., :share]
    for axis, size in enumerate(sizes):
        carried = rolled(carried, 3 - axis, size, size - coords[axis])
    small_grad = carried.transpose(3, 2, 1, 0, 4).reshape(-1)[:small_total]

    small_first, small_second, small_new = adam_update(
        small_grad * factor, small_params, small_moment1, small_moment2
    )

    soap_out = finish(
        factor.reshape(1), *raw, *stat_parts, stat_left, stat_right, basis_left, basis_right, master, moment1, moment2
    )
    short_total = seen_frames[frame_count].astype(F32) + from_next.astype(F32) + from_previous.astype(F32)
    grad_normed_one = jnp.concatenate([long_total, short_total]) + grad_own
    hat, spread = normalized(own.astype(F32))
    grad_inputs = grad_mixed + norm_back(grad_normed_one, hat, spread, rows14[0:1])
    grad_inputs = grad_inputs.reshape(2, PAD_ROWS, D)[:, :FRAME_ROWS]
    grad_inputs = jnp.where(swap, grad_inputs[::-1], grad_inputs).reshape(2 * FRAME_ROWS, D)
    return (
        learned[None],
        grad_inputs[None],
        soap_out[0],
        soap_out[1],
        soap_out[2],
        soap_out[3],
        soap_out[4],
        soap_out[5],
        soap_out[6],
        small_first,
        small_second,
        small_new,
        grad_norm,
    )


def solution(mesh):
    frames, batches = mesh.shape["frame"], mesh.shape["batch"]
    split = Mesh(mesh.devices.reshape(frames // 2, 2, batches // 2, 2), ALL_AXES)
    batch = ("by", "core")
    slots = P(ALL_AXES, None, None)
    rows = P(batch, FRAME_AXES, None)
    return jax.shard_map(
        on_device,
        mesh=split,
        in_specs=(rows, rows, P(batch, None), P(batch, None), P()) + (slots,) * 7 + (P(),) * 3,
        out_specs=(rows, rows) + (slots,) * 7 + (P(),) * 4,
        check_vma=False,
    )
```
